32 devices in a mesh: acq: 8 (over y, x, core), strip: 4 (over z).
Axes of the slice: x: 2, y: 2, z: 4, core: 2. Of those that a mesh axis runs over, the one named last changes fastest.
Arguments:
- raw_echoes: float32 [8, 2, 1024, 2048], P('acq', None, 'strip'), may hold values from -6 to 6
- range_filter: float32 [2, 2048], replicated, may hold values from -5 to 5
- azimuth_filter: float32 [2, 1024, 2048], P(None, None, 'strip'), may hold values from -5 to 5
- pair_mask: int32 [8, 2], P('acq'), may hold values 0 or 1
- inversion: float32 [8, 8, 2], P(None, 'acq'), may hold values from -2 to 2
Outputs:
- epoch_gradients: float32 [8, 2, 512, 256], P('acq', None, 'strip')
The draws below stay inside these ranges and needn't reach their ends.
Inputs may be any that keep to these rules, and one draw needn't show every extreme that they name: `pair_mask`: 1 where the pair is in the network, 0 where it is not.
All inputs are finite; a program needn't handle non-finite values. No bound on the sum of `pair_mask` on one device may be relied on, other than what follows from the above.
Results may differ from the reference program's by a relative error of at most 0.00014.
Values sent between devices are 32-bit elements; how exact they have to be, the bound alone decides.
No kernel may reach another device: no remote copies, remote signals or barrier semaphores. Data moves between devices by JAX's collectives and lax.ppermute only.
A program may use at most 128 MiB of HBM per device.

```python
import jax
import jax.numpy as jnp
from jax import lax

NA = 1024
NR = 2048
LOOK = 4
EPOCHS = 8


def set_ends(drawn, rng, smallest, high):
    extent = drawn.shape
    index_at = [jax.random.randint(jax.random.fold_in(rng, axis), (), 0, extent[axis]) for axis in range(len(extent))]
    drawn = drawn.at[tuple(index_at)].set(smallest)
    longest = extent.index(max(extent))
    index_at[longest] = (index_at[longest] + 1) % extent[longest]
    return drawn.at[tuple(index_at)].set(high)


def strengthened(drawn, rng, source, target, shards_of, factor):
    def block_of(axis_at):
        return (jnp.arange(drawn.shape[axis_at]) // (drawn.shape[axis_at] // shards_of)).reshape((-1,) + (1,) * (drawn.ndim - 1 - axis_at))

    first = jax.random.permutation(rng, shards_of)[block_of(target)]
    second = (block_of(target) + shards_of // 2) % shards_of
    return jnp.where((block_of(source) == first) | (block_of(source) == second), factor * drawn, drawn)


def levels(own_key, shape, shards, low, high):
    level = 1.0
    for axis_at, blocks in shards:
        draws = jax.random.uniform(jax.random.fold_in(jax.random.fold_in(own_key, 6), axis_at), (blocks,), jnp.float32, low / len(shards), high / len(shards))
        level = level * jnp.repeat(jnp.exp(draws), shape[axis_at] // blocks).reshape((-1,) + (1,) * (len(shape) - 1 - axis_at))
    return level


def gaussian(rng, extent, spread, bound, shards=(), kind=jnp.bfloat16):
    drawn = spread * jax.random.normal(rng, extent, jnp.float32)
    if shards:
        drawn = drawn * levels(rng, extent, shards, -0.22, 0.18)
    return jnp.clip(drawn, -bound, bound).astype(kind)


def noise_with(rng, shape, width, bound, shards, heavy, held_as=jnp.bfloat16):
    drawn = width * jax.random.normal(rng, shape, jnp.float32)
    if shards:
        drawn = drawn * levels(rng, shape, shards, -0.22, 0.18)
    return jnp.clip(strengthened(drawn, jax.random.fold_in(rng, 3), *heavy), -bound, bound).astype(held_as)


def setup_inputs(seed: int = 0) -> dict:
    keys = jax.random.split(jax.random.key(seed), 6)
    return {
        "raw_echoes": gaussian(keys[0], (EPOCHS, 2, NA, NR), 1.0, 6.0, ((0, 8), (2, 4)), jnp.float32),
        "range_filter": gaussian(keys[1], (2, NR), 0.7071, 5.0, (), jnp.float32),
        "azimuth_filter": gaussian(keys[2], (2, NA, NR), 0.7071, 5.0, ((2, 4),), jnp.float32),
        "pair_mask": set_ends((jax.random.randint(keys[3], (EPOCHS, 2), 0, 4) < 3).astype(jnp.int32), jax.random.fold_in(keys[3], 1), 0, 1),
        "inversion": noise_with(keys[4], (EPOCHS, EPOCHS, 2), (2 * EPOCHS) ** -0.5, 2.0, ((1, 8),), (1, 0, 8, 2.0), jnp.float32),
    }


def multilook(field):
    rows, cols = field.shape
    summed = field.reshape(rows // LOOK, LOOK, cols // LOOK, LOOK).sum(axis=(1, 3)) / LOOK
    return summed.T


def reference(raw_echoes, range_filter, azimuth_filter, pair_mask, inversion):
    range_spec = lax.complex(range_filter[0], range_filter[1])
    azimuth_spec = lax.complex(azimuth_filter[0], azimuth_filter[1])

    def focus(single):
        echo = lax.complex(single[0], single[1])
        compressed = jnp.fft.ifft(jnp.fft.fft(echo, axis=1) * range_spec[None, :], axis=1)
        return jnp.fft.ifft(jnp.fft.fft(compressed, axis=0) * azimuth_spec, axis=0)

    scenes = lax.map(focus, raw_echoes)

    def pair_slopes(later_index):
        later = scenes[later_index]
        slopes = []
        for lag in (1, 2):
            earlier = scenes[jnp.maximum(later_index - lag, 0)]
            product = earlier * jnp.conj(later)
            looked = lax.complex(multilook(jnp.real(product)), multilook(jnp.imag(product)))
            along_azimuth = jnp.imag(looked[:, 1:] * jnp.conj(looked[:, :-1]))
            along_azimuth = jnp.pad(along_azimuth, ((0, 0), (0, 1)))
            along_range = jnp.imag(looked[1:, :] * jnp.conj(looked[:-1, :]))
            along_range = jnp.pad(along_range, ((0, 1), (0, 0)))
            slopes.append(jnp.stack([along_azimuth, along_range]))
        return jnp.stack(slopes)

    epochs = raw_echoes.shape[0]
    slope = lax.map(pair_slopes, jnp.arange(epochs, dtype=jnp.int32))
    lags = jnp.array([1, 2], dtype=jnp.int32)
    usable = pair_mask.astype(jnp.float32) * (jnp.arange(epochs, dtype=jnp.int32)[:, None] >= lags[None, :]).astype(jnp.float32)
    weights = inversion.astype(jnp.float32) * usable[None, :, :]
    return jnp.einsum('ejl,jldra->edra', weights, slope.astype(jnp.float32), precision=lax.Precision.HIGHEST)
```

```python
import functools
import math

import jax
import jax.numpy as jnp
import ml_dtypes
import numpy as np
from jax import lax
from jax.experimental import pallas as pl
from jax.experimental.pallas import tpu as pltpu
from jax.sharding import PartitionSpec as P

LOOK = 4
RADIX = 8
ROWS = 8
VMEM_BYTES = 48 * 1024 * 1024
OWNERS = ("strip", "acq")


def add(left, right):
    return (left[0] + right[0], left[1] + right[1])


def sub(left, right):
    return (left[0] - right[0], left[1] - right[1])


def turn(value, sign):
    if sign > 0:
        return (-value[1], value[0])
    return (value[1], -value[0])


def dft4(x0, x1, x2, x3, sign):
    a, b = add(x0, x2), sub(x0, x2)
    c, d = add(x1, x3), turn(sub(x1, x3), sign)
    return [add(a, c), add(b, d), sub(a, c), sub(b, d)]


def dft8(x, sign):
    even = dft4(x[0], x[2], x[4], x[6], sign)
    odd = dft4(x[1], x[3], x[5], x[7], sign)
    half = math.sqrt(0.5)
    o1, o3 = odd[1], odd[3]
    t1 = add(o1, turn(o1, sign))
    t3 = sub(turn(o3, sign), o3)
    odd = [
        odd[0],
        (t1[0] * half, t1[1] * half),
        turn(odd[2], sign),
        (t3[0] * half, t3[1] * half),
    ]
    return [add(e, o) for e, o in zip(even, odd)] + [sub(e, o) for e, o in zip(even, odd)]


def two_parts(value):
    high = value.astype(jnp.bfloat16)
    low = (value - high.astype(jnp.float32)).astype(jnp.bfloat16)
    return high, low


def three_products(left_high, left_low, right_high, right_low, contract):
    def product(left, right):
        return lax.dot_general(
            left, right, (contract, ((), ())), preferred_element_type=jnp.float32
        )

    return (
        product(left_high, right_high)
        + product(left_high, right_low)
        + product(left_low, right_high)
    )


def host_parts(table):
    table = np.asarray(table, np.float64)
    high = table.astype(np.float32).astype(ml_dtypes.bfloat16)
    low = (table - high.astype(np.float64)).astype(np.float32).astype(ml_dtypes.bfloat16)
    return high, low


def unit(exponent, size, sign):
    angle = sign * 2.0 * np.pi / size * (exponent % size)
    return np.cos(angle), np.sin(angle)


def real_form(cosine, sine):
    top = np.concatenate([cosine, sine], axis=-1)
    bottom = np.concatenate([-sine, cosine], axis=-1)
    return np.concatenate([top, bottom], axis=-2)


class Plan:
    def __init__(self, strips, epochs, pulses, samples):
        self.strips, self.epochs = strips, epochs
        self.pulses, self.samples = pulses, samples
        self.azimuth = pulses * strips
        self.base = samples // RADIX
        self.owned = samples // (strips * epochs)
        self.parts = 2 if self.owned % (2 * LOOK * ROWS) == 0 else 1
        self.rows = self.owned // self.parts
        self.looks = self.rows // LOOK
        self.planes = self.looks % ROWS == 0
        self.blocks = self.base // self.owned
        self.lanes = self.azimuth // RADIX
        self.azimuth_looks = self.azimuth // LOOK

    def tile_shift(self, part, block, tile):
        start = block * self.owned + part * self.rows
        if self.planes:
            plane, look = divmod(tile * ROWS, self.looks)
            return start + LOOK * look + plane
        return start + tile * ROWS

    def tile_stride(self):
        return LOOK if self.planes else 1


def lag_vectors(range_filter, plan):
    base, samples = plan.base, plan.samples
    field = range_filter.reshape(2, base, RADIX).transpose(2, 0, 1).reshape(RADIX, 2 * base)
    index = np.arange(base)
    table = real_form(*unit(index[:, None] * index[None, :], base, -1.0)) / samples
    sums = jnp.dot(
        field, jnp.asarray(table.astype(np.float32)), precision=lax.Precision.HIGHEST
    ).reshape(RADIX, 2, base)
    lag = np.arange(2 * base)
    lag = np.where(lag <= base, lag, lag - 2 * base)
    turn_cos, turn_sin = unit(lag[None, :] * np.arange(RADIX)[:, None], samples, -1.0)
    turn_cos = jnp.asarray(turn_cos.astype(np.float32))
    turn_sin = jnp.asarray(turn_sin.astype(np.float32))
    real = jnp.concatenate([sums[:, 0], sums[:, 0]], axis=1)
    imag = jnp.concatenate([sums[:, 1], sums[:, 1]], axis=1)
    return jnp.stack(
        [real * turn_cos - imag * turn_sin, real * turn_sin + imag * turn_cos], axis=1
    )


def compress_kernel(plan, part, lag_ref, raw_ref, out_ref, t_high, t_low, y_high, y_low, z_ref):
    base, blocks = plan.base, plan.blocks
    tiles = plan.rows // ROWS
    chunk = blocks * plan.rows

    def build(d, carry):
        spread = [
            pltpu.roll(
                jnp.broadcast_to(lag_ref[d, c : c + 1, :], (ROWS, 2 * base)),
                0,
                1,
                stride=plan.tile_stride(),
                stride_axis=0,
            )
            for c in range(2)
        ]
        for pair in range(blocks * tiles // 2):
            real, imag = [], []
            for at in (2 * pair, 2 * pair + 1):
                shift = plan.tile_shift(part, at // tiles, at % tiles)
                real.append(pltpu.roll(spread[0], shift, 1)[:, :base])
                imag.append(pltpu.roll(spread[1], shift, 1)[:, :base])
            real_high, real_low = two_parts(jnp.concatenate(real, axis=0))
            imag_high, imag_low = two_parts(jnp.concatenate(imag, axis=0))
            top = pl.ds(pair * 2 * ROWS, 2 * ROWS)
            bottom = pl.ds(chunk + pair * 2 * ROWS, 2 * ROWS)
            t_high[d, top, :base] = real_high
            t_high[d, top, base:] = -imag_high
            t_high[d, bottom, :base] = imag_high
            t_high[d, bottom, base:] = real_high
            t_low[d, top, :base] = real_low
            t_low[d, top, base:] = -imag_low
            t_low[d, bottom, :base] = imag_low
            t_low[d, bottom, base:] = real_low
        return carry

    lax.fori_loop(0, RADIX, build, 0)

    def spread_pulses(at, carry):
        rows = pl.ds(at * 2 * ROWS, 2 * ROWS)
        x = [
            tuple(raw_ref[c, rows, a * base : (a + 1) * base] for c in range(2))
            for a in range(RADIX)
        ]
        for d, value in enumerate(dft8(x, -1.0)):
            for c in range(2):
                high, low = two_parts(value[c])
                y_high[d, rows, c * base : (c + 1) * base] = high
                y_low[d, rows, c * base : (c + 1) * base] = low
        return carry

    lax.fori_loop(0, plan.pulses // (2 * ROWS), spread_pulses, 0)

    def multiply(d, carry):
        z_ref[d] = three_products(t_high[d], t_low[d], y_high[d], y_low[d], ((1,), (1,)))
        return carry

    lax.fori_loop(0, RADIX, multiply, 0)

    for block in range(blocks):
        for tile in range(tiles):
            top = (block * tiles + tile) * ROWS
            z = [
                (z_ref[d, top : top + ROWS, :], z_ref[d, chunk + top : chunk + top + ROWS, :])
                for d in range(RADIX)
            ]
            for a, value in enumerate(dft8(z, 1.0)):
                for c in range(2):
                    out_ref[a * blocks + block, c, tile * ROWS : (tile + 1) * ROWS, :] = value[c]


def compress(plan, part, lags, raw):
    chunk = plan.blocks * plan.rows
    whole = pl.BlockSpec(memory_space=pltpu.VMEM)
    bytes_moved = 4 * (raw.size + raw.size // plan.parts)
    return pl.pallas_call(
        functools.partial(compress_kernel, plan, part),
        out_shape=jax.ShapeDtypeStruct(
            (plan.strips * plan.epochs, 2, plan.rows, plan.pulses), jnp.float32
        ),
        in_specs=[whole, whole],
        out_specs=whole,
        scratch_shapes=[
            pltpu.VMEM((RADIX, 2 * chunk, 2 * plan.base), jnp.bfloat16),
            pltpu.VMEM((RADIX, 2 * chunk, 2 * plan.base), jnp.bfloat16),
            pltpu.VMEM((RADIX, plan.pulses, 2 * plan.base), jnp.bfloat16),
            pltpu.VMEM((RADIX, plan.pulses, 2 * plan.base), jnp.bfloat16),
            pltpu.VMEM((RADIX, 2 * chunk, plan.pulses), jnp.float32),
        ],
        compiler_params=pltpu.CompilerParams(vmem_limit_bytes=VMEM_BYTES),
        cost_estimate=pl.CostEstimate(
            flops=6 * RADIX * 4 * chunk * plan.base * plan.pulses,
            bytes_accessed=bytes_moved,
            transcendentals=0,
        ),
        name="range_compress",
    )(lags, raw)


def focus_kernel(
    plan, field_ref, filter_ref, fh_ref, fl_ref, bh_ref, bl_ref, sum_ref, looked_ref,
    y_high, y_low, z_ref, scene_ref, product_ref,
):
    rows, lanes, epochs, looks = plan.rows, plan.lanes, plan.epochs, plan.looks
    per_block = field_ref.shape[-1] // lanes

    def forward(j, carry):
        for top in range(0, rows, ROWS):
            x = []
            for a in range(RADIX):
                strip, start = a // per_block, a % per_block * lanes
                x.append(
                    tuple(
                        field_ref[strip, j, c, top : top + ROWS, start : start + lanes]
                        for c in range(2)
                    )
                )
            for d, value in enumerate(dft8(x, -1.0)):
                for c in range(2):
                    at = pl.ds(pl.multiple_of(j * rows + top, ROWS), ROWS)
                    z_ref[d, at, c * lanes : (c + 1) * lanes] = value[c]
        return carry

    lax.fori_loop(0, epochs, forward, 0)

    def filtered(d, carry):
        y_high[...], y_low[...] = two_parts(z_ref[d])
        spectrum = three_products(
            y_high[...], y_low[...], fh_ref[d], fl_ref[d], ((1,), (0,))
        ).reshape(epochs, rows, 2 * lanes)
        real, imag = spectrum[:, :, :lanes], spectrum[:, :, lanes:]
        by_real, by_imag = filter_ref[0, d][None], filter_ref[1, d][None]
        real, imag = real * by_real - imag * by_imag, real * by_imag + imag * by_real
        for c, value in enumerate((real, imag)):
            high, low = two_parts(value.reshape(epochs * rows, lanes))
            y_high[:, c * lanes : (c + 1) * lanes] = high
            y_low[:, c * lanes : (c + 1) * lanes] = low
        z_ref[d] = three_products(
            y_high[...], y_low[...], bh_ref[d], bl_ref[d], ((1,), (0,))
        )
        return carry

    lax.fori_loop(0, RADIX, filtered, 0)

    scene_ref[0] = jnp.zeros_like(scene_ref[0])
    scene_ref[1] = jnp.zeros_like(scene_ref[1])

    def backward(j, carry):
        for top in range(0, rows, ROWS):
            at = pl.ds(pl.multiple_of(j * rows + top, ROWS), ROWS)
            z = [
                tuple(z_ref[d, at, c * lanes : (c + 1) * lanes] for c in range(2))
                for d in range(RADIX)
            ]
            for a, value in enumerate(dft8(z, 1.0)):
                for c in range(2):
                    scene_ref[j + 2, c, top : top + ROWS, a * lanes : (a + 1) * lanes] = value[c]
        return carry

    lax.fori_loop(0, epochs, backward, 0)

    def look(value):
        if plan.planes:
            return sum(value[q * looks : (q + 1) * looks] for q in range(1, LOOK)) + value[:looks]
        return value.reshape(looks, LOOK, value.shape[-1]).sum(axis=1)

    def interfere(j, carry):
        for a in range(RADIX):
            columns = pl.ds(a * lanes, lanes)
            later = (scene_ref[j + 2, 0, :, columns], scene_ref[j + 2, 1, :, columns])
            for lag in (1, 2):
                earlier = (
                    scene_ref[j + 2 - lag, 0, :, columns],
                    scene_ref[j + 2 - lag, 1, :, columns],
                )
                real = earlier[0] * later[0] + earlier[1] * later[1]
                imag = earlier[1] * later[0] - earlier[0] * later[1]
                product_ref[j, lag - 1, 0, :, columns] = look(real)
                product_ref[j, lag - 1, 1, :, columns] = look(imag)
        return carry

    lax.fori_loop(0, epochs, interfere, 0)

    total = epochs * 4 * looks
    products = product_ref[...].reshape(total, plan.azimuth)
    high, low = two_parts(products)
    weights = sum_ref[...]
    looked = jnp.dot(high, weights, preferred_element_type=jnp.float32) + jnp.dot(
        low, weights, preferred_element_type=jnp.float32
    )
    looked_ref[...] = looked.reshape(looked_ref.shape)


def focus(plan, field, spectrum):
    lanes = plan.lanes
    b = np.arange(lanes)[None, :, None]
    k = RADIX * np.arange(lanes)[None, None, :] + np.arange(RADIX)[:, None, None]
    cosine, sine = unit(b * k, plan.azimuth, -1.0)
    ahead = host_parts(real_form(cosine, sine))
    cosine, sine = cosine.swapaxes(1, 2), -sine.swapaxes(1, 2)
    back = host_parts(real_form(cosine, sine) / plan.azimuth)
    sums = (np.arange(plan.azimuth)[:, None] // LOOK == np.arange(plan.azimuth_looks)[None, :]) / LOOK
    sums = sums.astype(ml_dtypes.bfloat16)
    total = plan.epochs * plan.rows
    whole = pl.BlockSpec(memory_space=pltpu.VMEM)
    return pl.pallas_call(
        functools.partial(focus_kernel, plan),
        out_shape=jax.ShapeDtypeStruct(
            (plan.epochs, 2, 2, plan.looks, plan.azimuth_looks), jnp.float32
        ),
        in_specs=[whole] * 7,
        out_specs=whole,
        scratch_shapes=[
            pltpu.VMEM((total, 2 * lanes), jnp.bfloat16),
            pltpu.VMEM((total, 2 * lanes), jnp.bfloat16),
            pltpu.VMEM((RADIX, total, 2 * lanes), jnp.float32),
            pltpu.VMEM((plan.epochs + 2, 2, plan.rows, plan.azimuth), jnp.float32),
            pltpu.VMEM((plan.epochs, 2, 2, plan.looks, plan.azimuth), jnp.float32),
        ],
        compiler_params=pltpu.CompilerParams(vmem_limit_bytes=VMEM_BYTES),
        cost_estimate=pl.CostEstimate(
            flops=2 * 6 * RADIX * total * 4 * lanes * lanes,
            bytes_accessed=4 * field.size + 4 * 1024 * 1024,
            transcendentals=0,
        ),
        name="azimuth_focus",
    )(field, spectrum, *ahead, *back, sums)


def slope_kernel(plan, weight_ref, looked_ref, halo_ref, out_ref, slope_ref):
    epochs = plan.epochs
    columns = plan.azimuth_looks
    inner = lax.broadcasted_iota(jnp.int32, (plan.looks * plan.parts, columns), 1) < columns - 1

    def slopes(at, carry):
        j, lag = at // 2, at % 2
        real, imag = looked_ref[j, lag, 0], looked_ref[j, lag, 1]
        next_real = pltpu.roll(real, columns - 1, 1)
        next_imag = pltpu.roll(imag, columns - 1, 1)
        slope_ref[at, 0] = jnp.where(inner, next_imag * real - next_real * imag, 0.0)
        next_real = jnp.concatenate([real[1:], halo_ref[j, lag, 0]], axis=0)
        next_imag = jnp.concatenate([imag[1:], halo_ref[j, lag, 1]], axis=0)
        slope_ref[at, 1] = next_imag * real - next_real * imag
        return carry

    lax.fori_loop(0, 2 * epochs, slopes, 0)

    def epoch(e, carry):
        total = weight_ref[e, 0] * slope_ref[0]
        for at in range(1, 2 * epochs):
            total = total + weight_ref[e, at] * slope_ref[at]
        out_ref[e] = total
        return carry

    lax.fori_loop(0, epochs, epoch, 0)


def slopes_to_epochs(plan, weights, looked, halo):
    whole = pl.BlockSpec(memory_space=pltpu.VMEM)
    looks = plan.looks * plan.parts
    return pl.pallas_call(
        functools.partial(slope_kernel, plan),
        out_shape=jax.ShapeDtypeStruct(
            (plan.epochs, 2, looks, plan.azimuth_looks), jnp.float32
        ),
        in_specs=[pl.BlockSpec(memory_space=pltpu.SMEM), whole, whole],
        out_specs=whole,
        scratch_shapes=[
            pltpu.VMEM((2 * plan.epochs, 2, looks, plan.azimuth_looks), jnp.float32)
        ],
        compiler_params=pltpu.CompilerParams(vmem_limit_bytes=VMEM_BYTES),
        cost_estimate=pl.CostEstimate(
            flops=8 * looked.size * plan.epochs, bytes_accessed=5 * looked.size, transcendentals=0
        ),
        name="slopes_to_epochs",
    )(weights, looked, halo)


def own_filter(plan, azimuth_filter):
    start = lax.axis_index("acq") * plan.owned
    own = lax.dynamic_slice_in_dim(azimuth_filter, start, plan.owned, axis=2)
    own = own.reshape(2, plan.lanes, RADIX, plan.parts, plan.looks, LOOK)
    order = (3, 0, 2, 5, 4, 1) if plan.planes else (3, 0, 2, 4, 5, 1)
    return own.transpose(order).reshape(plan.parts, 2, RADIX, plan.rows, plan.lanes)


def exchange(plan, block):
    received = lax.all_to_all(block, OWNERS, split_axis=0, concat_axis=0, tiled=True)
    join = max(1, plan.lanes // plan.pulses)
    received = received.reshape(
        plan.strips // join, join, plan.epochs, 2, plan.rows, plan.pulses
    )
    if join > 1:
        received = received.transpose(0, 2, 3, 4, 1, 5)
    return received.reshape(
        plan.strips // join, plan.epochs, 2, plan.rows, join * plan.pulses
    )


def per_device(raw_echoes, range_filter, azimuth_filter, pair_mask, inversion):
    strips, epochs = lax.axis_size("strip"), lax.axis_size("acq")
    plan = Plan(strips, epochs, raw_echoes.shape[2], raw_echoes.shape[3])

    lags = jnp.array([1, 2], dtype=jnp.int32)
    usable = pair_mask[0].astype(jnp.float32) * (lax.axis_index("acq") >= lags).astype(jnp.float32)
    weights = lax.all_gather(inversion[:, 0, :] * usable[None, :], "acq", axis=1, tiled=False)
    weights = weights.reshape(epochs, 2 * epochs)

    vectors = lag_vectors(range_filter, plan)
    spectrum = own_filter(plan, azimuth_filter)
    looked = []
    fields = [
        exchange(plan, compress(plan, part, vectors, raw_echoes[0])) for part in range(plan.parts)
    ]
    for part in range(plan.parts):
        looked.append(focus(plan, fields[part], spectrum[part]))

    owners = strips * epochs
    device = [i % epochs * strips + i // epochs for i in range(owners)]
    halo = lax.ppermute(
        looked[0][:, :, :, :1, :],
        ("acq", "strip"),
        [(device[i], device[i - 1]) for i in range(1, owners)],
    )
    looked = jnp.concatenate(looked, axis=3)
    gradients = slopes_to_epochs(plan, weights, looked, halo)
    gathered = lax.all_to_all(gradients, "acq", split_axis=0, concat_axis=0, tiled=True)
    gathered = gathered.reshape(epochs, 2, looked.shape[3], plan.azimuth_looks)
    return gathered.swapaxes(0, 1).reshape(1, 2, -1, plan.azimuth_looks)


def solution(mesh):
    return jax.shard_map(
        per_device,
        mesh=mesh,
        in_specs=(
            P("acq", None, "strip", None),
            P(),
            P(None, None, "strip"),
            P("acq", None),
            P(None, "acq", None),
        ),
        out_specs=P("acq", None, "strip", None),
        check_vma=False,
    )
```

```python
import functools
import math

import jax
import jax.numpy as jnp
import ml_dtypes
import numpy as np
from jax import lax
from jax.experimental import pallas as pl
from jax.experimental.pallas import tpu as pltpu
from jax.sharding import PartitionSpec as P

LOOK = 4
RADIX = 8
ROWS = 8
VMEM_BYTES = 48 * 1024 * 1024
OWNERS = ("strip", "acq")


def add(left, right):
    return (left[0] + right[0], left[1] + right[1])


def sub(left, right):
    return (left[0] - right[0], left[1] - right[1])


def turn(value, sign):
    if sign > 0:
        return (-value[1], value[0])
    return (value[1], -value[0])


def dft4(x0, x1, x2, x3, sign):
    a, b = add(x0, x2), sub(x0, x2)
    c, d = add(x1, x3), turn(sub(x1, x3), sign)
    return [add(a, c), add(b, d), sub(a, c), sub(b, d)]


def dft8(x, sign):
    even = dft4(x[0], x[2], x[4], x[6], sign)
    odd = dft4(x[1], x[3], x[5], x[7], sign)
    half = math.sqrt(0.5)
    o1, o3 = odd[1], odd[3]
    t1 = add(o1, turn(o1, sign))
    t3 = sub(turn(o3, sign), o3)
    odd = [
        odd[0],
        (t1[0] * half, t1[1] * half),
        turn(odd[2], sign),
        (t3[0] * half, t3[1] * half),
    ]
    return [add(e, o) for e, o in zip(even, odd)] + [sub(e, o) for e, o in zip(even, odd)]


def two_parts(value):
    high = value.astype(jnp.bfloat16)
    low = (value - high.astype(jnp.float32)).astype(jnp.bfloat16)
    return high, low


def three_products(left_high, left_low, right_high, right_low, contract):
    def product(left, right):
        return lax.dot_general(
            left, right, (contract, ((), ())), preferred_element_type=jnp.float32
        )

    return (
        product(left_high, right_high)
        + product(left_high, right_low)
        + product(left_low, right_high)
    )


def host_parts(table):
    table = np.asarray(table, np.float64)
    high = table.astype(np.float32).astype(ml_dtypes.bfloat16)
    low = (table - high.astype(np.float64)).astype(np.float32).astype(ml_dtypes.bfloat16)
    return high, low


def unit(exponent, size, sign):
    angle = sign * 2.0 * np.pi / size * (exponent % size)
    return np.cos(angle), np.sin(angle)


def real_form(cosine, sine):
    top = np.concatenate([cosine, sine], axis=-1)
    bottom = np.concatenate([-sine, cosine], axis=-1)
    return np.concatenate([top, bottom], axis=-2)


class Plan:
    def __init__(self, strips, epochs, pulses, samples):
        self.strips, self.epochs = strips, epochs
        self.pulses, self.samples = pulses, samples
        self.azimuth = pulses * strips
        self.base = samples // RADIX
        self.owned = samples // (strips * epochs)
        self.parts = 2 if self.owned % (2 * LOOK * ROWS) == 0 else 1
        self.rows = self.owned // self.parts
        self.looks = self.rows // LOOK
        self.planes = self.looks % ROWS == 0
        self.blocks = self.base // self.owned
        self.lanes = self.azimuth // RADIX
        self.azimuth_looks = self.azimuth // LOOK

    def tile_shift(self, part, block, tile):
        start = block * self.owned + part * self.rows
        if self.planes:
            plane, look = divmod(tile * ROWS, self.looks)
            return start + LOOK * look + plane
        return start + tile * ROWS

    def tile_stride(self):
        return LOOK if self.planes else 1


def lag_tables(plan):
    base, samples = plan.base, plan.samples
    index = np.arange(base)
    table = host_parts(real_form(*unit(index[:, None] * index[None, :], samples, -1.0)) / samples)
    block = np.arange(RADIX)[:, None]
    turns = np.stack(
        unit(block * index[None, :], RADIX, -1.0)
        + tuple(np.broadcast_to(part, (RADIX, base)) for part in unit(block, RADIX, 1.0))
    )
    return table + (turns.astype(np.float32),)


def lag_vectors(plan, filter_ref, table_high, table_low, turn_ref):
    base = plan.base
    lane = lax.broadcasted_iota(jnp.int32, (RADIX, base), 1)
    chosen = lane % RADIX == lax.broadcasted_iota(jnp.int32, (RADIX, base), 0)
    rows = []
    for e in range(RADIX):
        both = []
        for c in range(2):
            block = jnp.broadcast_to(filter_ref[c : c + 1, e * base : (e + 1) * base], (RADIX, base))
            both.append(jnp.where(chosen, block, 0.0))
        rows.append(jnp.concatenate(both, axis=1))
    high, low = two_parts(jnp.concatenate(rows, axis=0))
    sums = three_products(high, low, table_high[...], table_low[...], ((1,), (0,)))
    real, imag = 0.0, 0.0
    for e in range(RADIX):
        part_real = sums[e * RADIX : (e + 1) * RADIX, :base]
        part_imag = sums[e * RADIX : (e + 1) * RADIX, base:]
        cosine, sine = turn_ref[0, e : e + 1, :], turn_ref[1, e : e + 1, :]
        real = real + part_real * cosine - part_imag * sine
        imag = imag + part_real * sine + part_imag * cosine
    cosine, sine = turn_ref[2], turn_ref[3]
    return (
        jnp.concatenate([real, real * cosine - imag * sine], axis=1),
        jnp.concatenate([imag, real * sine + imag * cosine], axis=1),
    )


def fetch(copies):
    for copy in copies:
        copy.start()
    return copies


def compress_kernel(
    plan, part, filter_ref, table_high, table_low, turn_ref, raw_ref, out_ref,
    raw, t_high, t_low, y_high, y_low, z_ref, sems,
):
    base, blocks = plan.base, plan.blocks
    tiles = plan.rows // ROWS
    chunk = blocks * plan.rows
    pieces = sems.shape[0]
    piece = plan.pulses // pieces

    def raw_copy(at):
        rows = pl.ds(at * piece, piece)
        return pltpu.make_async_copy(raw_ref.at[:, rows, :], raw.at[:, rows, :], sems.at[at])

    fetch([raw_copy(at) for at in range(pieces)])
    lags = lag_vectors(plan, filter_ref, table_high, table_low, turn_ref)

    for d in range(RADIX):
        spread = [
            pltpu.roll(
                jnp.broadcast_to(lag[d : d + 1, :], (ROWS, 2 * base)),
                0,
                1,
                stride=plan.tile_stride(),
                stride_axis=0,
            )
            for lag in lags
        ]
        for pair in range(blocks * tiles // 2):
            real, imag = [], []
            for at in (2 * pair, 2 * pair + 1):
                shift = plan.tile_shift(part, at // tiles, at % tiles)
                real.append(pltpu.roll(spread[0], shift, 1)[:, :base])
                imag.append(pltpu.roll(spread[1], shift, 1)[:, :base])
            real_high, real_low = two_parts(jnp.concatenate(real, axis=0))
            imag_high, imag_low = two_parts(jnp.concatenate(imag, axis=0))
            top = pl.ds(pair * 2 * ROWS, 2 * ROWS)
            bottom = pl.ds(chunk + pair * 2 * ROWS, 2 * ROWS)
            t_high[d, top, :base] = real_high
            t_high[d, top, base:] = -imag_high
            t_high[d, bottom, :base] = imag_high
            t_high[d, bottom, base:] = real_high
            t_low[d, top, :base] = real_low
            t_low[d, top, base:] = -imag_low
            t_low[d, bottom, :base] = imag_low
            t_low[d, bottom, base:] = real_low

    def spread_pulses(at, carry):
        rows = pl.ds(pl.multiple_of(at * 2 * ROWS, 2 * ROWS), 2 * ROWS)
        x = [
            tuple(raw[c, rows, a * base : (a + 1) * base] for c in range(2))
            for a in range(RADIX)
        ]
        for d, value in enumerate(dft8(x, -1.0)):
            for c in range(2):
                high, low = two_parts(value[c])
                y_high[d, rows, c * base : (c + 1) * base] = high
                y_low[d, rows, c * base : (c + 1) * base] = low
        return carry

    steps = piece // (2 * ROWS)
    for at in range(pieces):
        raw_copy(at).wait()
        lax.fori_loop(at * steps, (at + 1) * steps, spread_pulses, 0)

    for d in range(RADIX):
        z_ref[d] = three_products(t_high[d], t_low[d], y_high[d], y_low[d], ((1,), (1,)))

    for block in range(blocks):
        for tile in range(tiles):
            top = (block * tiles + tile) * ROWS
            z = [
                (z_ref[d, top : top + ROWS, :], z_ref[d, chunk + top : chunk + top + ROWS, :])
                for d in range(RADIX)
            ]
            for a, value in enumerate(dft8(z, 1.0)):
                for c in range(2):
                    out_ref[a * blocks + block, c, tile * ROWS : (tile + 1) * ROWS, :] = value[c]


def compress(plan, part, range_filter, raw):
    chunk = plan.blocks * plan.rows
    whole = pl.BlockSpec(memory_space=pltpu.VMEM)
    bytes_moved = 4 * (raw.size + raw.size // plan.parts)
    return pl.pallas_call(
        functools.partial(compress_kernel, plan, part),
        out_shape=jax.ShapeDtypeStruct(
            (plan.strips * plan.epochs, 2, plan.rows, plan.pulses), jnp.float32
        ),
        in_specs=[whole] * 4 + [pl.BlockSpec(memory_space=pl.ANY)],
        out_specs=whole,
        scratch_shapes=[
            pltpu.VMEM(raw.shape, jnp.float32),
            pltpu.VMEM((RADIX, 2 * chunk, 2 * plan.base), jnp.bfloat16),
            pltpu.VMEM((RADIX, 2 * chunk, 2 * plan.base), jnp.bfloat16),
            pltpu.VMEM((RADIX, plan.pulses, 2 * plan.base), jnp.bfloat16),
            pltpu.VMEM((RADIX, plan.pulses, 2 * plan.base), jnp.bfloat16),
            pltpu.VMEM((RADIX, 2 * chunk, plan.pulses), jnp.float32),
            pltpu.SemaphoreType.DMA((4,)),
        ],
        compiler_params=pltpu.CompilerParams(vmem_limit_bytes=VMEM_BYTES),
        cost_estimate=pl.CostEstimate(
            flops=6 * RADIX * 4 * chunk * plan.base * plan.pulses,
            bytes_accessed=bytes_moved,
            transcendentals=0,
        ),
        name="range_compress",
    )(range_filter, *lag_tables(plan), raw)


def focus_kernel(plan, part, final, *refs):
    field_any, filter_any, fh_any, fl_any, bh_any, bl_any, sum_any = refs[:7]
    if final:
        weight_ref, before_ref, halo_ref, out_ref = refs[7:11]
    else:
        (out_ref,) = refs[7:8]
    scratch = refs[11 if final else 8 :]
    (
        field_ref, filter_ref, fh_ref, fl_ref, bh_ref, bl_ref, sum_ref,
        z_ref, scene_ref, product_ref, field_sems, table_sems,
    ) = scratch[:12]
    rows, lanes, epochs, looks = plan.rows, plan.lanes, plan.epochs, plan.looks
    per_block = field_ref.shape[-1] // lanes

    def field_copy(j):
        return pltpu.make_async_copy(field_any.at[:, j], field_ref.at[:, j], field_sems.at[j])

    fetch([field_copy(j) for j in range(epochs)])
    tables = fetch(
        [
            pltpu.make_async_copy(source, target, table_sems.at[at])
            for at, (source, target) in enumerate(
                (
                    (fh_any, fh_ref),
                    (fl_any, fl_ref),
                    (filter_any.at[part], filter_ref),
                    (bh_any, bh_ref),
                    (bl_any, bl_ref),
                    (sum_any, sum_ref),
                )
            )
        ]
    )

    def forward(j, carry):
        field_copy(j).wait()
        for top in range(0, rows, ROWS):
            x = []
            for a in range(RADIX):
                strip, start = a // per_block, a % per_block * lanes
                x.append(
                    tuple(
                        field_ref[strip, j, c, top : top + ROWS, start : start + lanes]
                        for c in range(2)
                    )
                )
            for d, value in enumerate(dft8(x, -1.0)):
                for c in range(2):
                    at = pl.ds(pl.multiple_of(j * rows + top, ROWS), ROWS)
                    z_ref[d, at, c * lanes : (c + 1) * lanes] = value[c]
        return carry

    lax.fori_loop(0, epochs, forward, 0)
    for copy in tables:
        copy.wait()

    for d in range(RADIX):
        high, low = two_parts(z_ref[d])
        spectrum = three_products(high, low, fh_ref[d], fl_ref[d], ((1,), (0,)))
        spectrum = spectrum.reshape(epochs, rows, 2 * lanes)
        real, imag = spectrum[:, :, :lanes], spectrum[:, :, lanes:]
        by_real, by_imag = filter_ref[0, d][None], filter_ref[1, d][None]
        spectrum = jnp.concatenate(
            [real * by_real - imag * by_imag, real * by_imag + imag * by_real], axis=2
        )
        high, low = two_parts(spectrum.reshape(epochs * rows, 2 * lanes))
        z_ref[d] = three_products(high, low, bh_ref[d], bl_ref[d], ((1,), (0,)))

    scene_ref[0] = jnp.zeros_like(scene_ref[0])
    scene_ref[1] = jnp.zeros_like(scene_ref[1])

    def backward(j, carry):
        for top in range(0, rows, ROWS):
            at = pl.ds(pl.multiple_of(j * rows + top, ROWS), ROWS)
            z = [
                tuple(z_ref[d, at, c * lanes : (c + 1) * lanes] for c in range(2))
                for d in range(RADIX)
            ]
            for a, value in enumerate(dft8(z, 1.0)):
                for c in range(2):
                    scene_ref[j + 2, c, top : top + ROWS, a * lanes : (a + 1) * lanes] = value[c]
        return carry

    lax.fori_loop(0, epochs, backward, 0)

    def look(value):
        if plan.planes:
            return sum(value[q * looks : (q + 1) * looks] for q in range(1, LOOK)) + value[:looks]
        return value.reshape(looks, LOOK, value.shape[-1]).sum(axis=1)

    def interfere(j, carry):
        for a in range(RADIX):
            columns = pl.ds(a * lanes, lanes)
            later = (scene_ref[j + 2, 0, :, columns], scene_ref[j + 2, 1, :, columns])
            for lag in (1, 2):
                earlier = (
                    scene_ref[j + 2 - lag, 0, :, columns],
                    scene_ref[j + 2 - lag, 1, :, columns],
                )
                real = earlier[0] * later[0] + earlier[1] * later[1]
                imag = earlier[1] * later[0] - earlier[0] * later[1]
                product_ref[j, lag - 1, 0, :, columns] = look(real)
                product_ref[j, lag - 1, 1, :, columns] = look(imag)
        return carry

    lax.fori_loop(0, epochs, interfere, 0)

    total = epochs * 4 * looks
    products = product_ref[...].reshape(total, plan.azimuth)
    high, low = two_parts(products)
    weights = sum_ref[...]
    looked = jnp.dot(high, weights, preferred_element_type=jnp.float32) + jnp.dot(
        low, weights, preferred_element_type=jnp.float32
    )
    looked = looked.reshape(epochs, 2, 2, looks, plan.azimuth_looks)
    if final:
        looked_ref, slope_ref = scratch[12:]
        for at, before in enumerate(before_ref):
            looked_ref[:, :, :, at * looks : (at + 1) * looks, :] = before[...]
        looked_ref[:, :, :, part * looks :, :] = looked
        slopes_and_sums(plan, weight_ref, looked_ref, halo_ref, out_ref, slope_ref)
    else:
        out_ref[...] = looked


def slopes_and_sums(plan, weight_ref, looked_ref, halo_ref, out_ref, slope_ref):
    epochs = plan.epochs
    columns = plan.azimuth_looks
    inner = lax.broadcasted_iota(jnp.int32, (plan.looks * plan.parts, columns), 1) < columns - 1

    def slopes(at, carry):
        j, lag = at // 2, at % 2
        real, imag = looked_ref[j, lag, 0], looked_ref[j, lag, 1]
        next_real = pltpu.roll(real, columns - 1, 1)
        next_imag = pltpu.roll(imag, columns - 1, 1)
        slope_ref[at, 0] = jnp.where(inner, next_imag * real - next_real * imag, 0.0)
        next_real = jnp.concatenate([real[1:], halo_ref[j, lag, 0]], axis=0)
        next_imag = jnp.concatenate([imag[1:], halo_ref[j, lag, 1]], axis=0)
        slope_ref[at, 1] = next_imag * real - next_real * imag
        return carry

    lax.fori_loop(0, 2 * epochs, slopes, 0)

    def epoch(e, carry):
        total = weight_ref[e, 0] * slope_ref[0]
        for at in range(1, 2 * epochs):
            total = total + weight_ref[e, at] * slope_ref[at]
        out_ref[e] = total
        return carry

    lax.fori_loop(0, epochs, epoch, 0)


def focus_tables(plan):
    lanes = plan.lanes
    b = np.arange(lanes)[None, :, None]
    k = RADIX * np.arange(lanes)[None, None, :] + np.arange(RADIX)[:, None, None]
    cosine, sine = unit(b * k, plan.azimuth, -1.0)
    ahead = host_parts(real_form(cosine, sine))
    cosine, sine = cosine.swapaxes(1, 2), -sine.swapaxes(1, 2)
    back = host_parts(real_form(cosine, sine) / plan.azimuth)
    sums = (np.arange(plan.azimuth)[:, None] // LOOK == np.arange(plan.azimuth_looks)[None, :]) / LOOK
    return ahead + back + (sums.astype(ml_dtypes.bfloat16),)


def focus(plan, part, field, spectrum, finish=None):
    lanes = plan.lanes
    total = plan.epochs * plan.rows
    tables = focus_tables(plan)
    whole = pl.BlockSpec(memory_space=pltpu.VMEM)
    looked = (plan.epochs, 2, 2, plan.looks, plan.azimuth_looks)
    gradients = (plan.epochs, 2, plan.looks * plan.parts, plan.azimuth_looks)
    operands = [field, spectrum, *tables]
    in_specs = [pl.BlockSpec(memory_space=pl.ANY)] * 7
    scratch = [
        pltpu.VMEM(field.shape, jnp.float32),
        pltpu.VMEM(spectrum.shape[1:], jnp.float32),
        *[pltpu.VMEM(table.shape, jnp.bfloat16) for table in tables],
        pltpu.VMEM((RADIX, total, 2 * lanes), jnp.float32),
        pltpu.VMEM((plan.epochs + 2, 2, plan.rows, plan.azimuth), jnp.float32),
        pltpu.VMEM((plan.epochs, 2, 2, plan.looks, plan.azimuth), jnp.float32),
        pltpu.SemaphoreType.DMA((plan.epochs,)),
        pltpu.SemaphoreType.DMA((6,)),
    ]
    shape = looked
    if finish is not None:
        weights, before, halo = finish
        shape = gradients
        operands += [weights, before, halo]
        in_specs += [pl.BlockSpec(memory_space=pltpu.SMEM), [whole] * len(before), whole]
        scratch += [
            pltpu.VMEM((plan.epochs, 2, 2, plan.looks * plan.parts, plan.azimuth_looks), jnp.float32),
            pltpu.VMEM((2 * plan.epochs,) + gradients[1:], jnp.float32),
        ]
    return pl.pallas_call(
        functools.partial(focus_kernel_flat, plan, part, len(before) if finish else None),
        out_shape=jax.ShapeDtypeStruct(shape, jnp.float32),
        in_specs=jax.tree.leaves(in_specs),
        out_specs=whole,
        scratch_shapes=scratch,
        compiler_params=pltpu.CompilerParams(vmem_limit_bytes=VMEM_BYTES),
        cost_estimate=pl.CostEstimate(
            flops=2 * 6 * RADIX * total * 4 * lanes * lanes,
            bytes_accessed=4 * field.size + 4 * 1024 * 1024,
            transcendentals=0,
        ),
        name="azimuth_focus",
    )(*jax.tree.leaves(operands))


def focus_kernel_flat(plan, part, count, *refs):
    if count is None:
        focus_kernel(plan, part, False, *refs)
        return
    before = refs[8 : 8 + count]
    focus_kernel(plan, part, True, *refs[:8], before, *refs[8 + count :])


def slope_kernel(plan, weight_ref, looked_ref, halo_ref, out_ref, slope_ref):
    slopes_and_sums(plan, weight_ref, looked_ref, halo_ref, out_ref, slope_ref)


def slopes_to_epochs(plan, weights, looked, halo):
    whole = pl.BlockSpec(memory_space=pltpu.VMEM)
    looks = plan.looks * plan.parts
    return pl.pallas_call(
        functools.partial(slope_kernel, plan),
        out_shape=jax.ShapeDtypeStruct(
            (plan.epochs, 2, looks, plan.azimuth_looks), jnp.float32
        ),
        in_specs=[pl.BlockSpec(memory_space=pltpu.SMEM), whole, whole],
        out_specs=whole,
        scratch_shapes=[
            pltpu.VMEM((2 * plan.epochs, 2, looks, plan.azimuth_looks), jnp.float32)
        ],
        compiler_params=pltpu.CompilerParams(vmem_limit_bytes=VMEM_BYTES),
        cost_estimate=pl.CostEstimate(
            flops=8 * looked.size * plan.epochs, bytes_accessed=5 * looked.size, transcendentals=0
        ),
        name="slopes_to_epochs",
    )(weights, looked, halo)


def own_filter(plan, azimuth_filter):
    start = lax.axis_index("acq") * plan.owned
    own = lax.dynamic_slice_in_dim(azimuth_filter, start, plan.owned, axis=2)
    own = own.reshape(2, plan.lanes, RADIX, plan.parts, plan.looks, LOOK)
    order = (3, 0, 2, 5, 4, 1) if plan.planes else (3, 0, 2, 4, 5, 1)
    return own.transpose(order).reshape(plan.parts, 2, RADIX, plan.rows, plan.lanes)


def exchange(plan, block):
    received = lax.all_to_all(block, OWNERS, split_axis=0, concat_axis=0, tiled=True)
    join = max(1, plan.lanes // plan.pulses)
    received = received.reshape(
        plan.strips // join, join, plan.epochs, 2, plan.rows, plan.pulses
    )
    if join > 1:
        received = received.transpose(0, 2, 3, 4, 1, 5)
    return received.reshape(
        plan.strips // join, plan.epochs, 2, plan.rows, join * plan.pulses
    )


def per_device(raw_echoes, range_filter, azimuth_filter, pair_mask, inversion):
    strips, epochs = lax.axis_size("strip"), lax.axis_size("acq")
    plan = Plan(strips, epochs, raw_echoes.shape[2], raw_echoes.shape[3])

    lags = jnp.array([1, 2], dtype=jnp.int32)
    usable = pair_mask[0].astype(jnp.float32) * (lax.axis_index("acq") >= lags).astype(jnp.float32)
    weights = lax.all_gather(inversion[:, 0, :] * usable[None, :], "acq", axis=1, tiled=False)
    weights = weights.reshape(epochs, 2 * epochs)

    spectrum = own_filter(plan, azimuth_filter)
    fields = [
        exchange(plan, compress(plan, part, range_filter, raw_echoes[0]))
        for part in range(plan.parts)
    ]
    before = [focus(plan, part, fields[part], spectrum) for part in range(max(1, plan.parts - 1))]

    owners = strips * epochs
    device = [i % epochs * strips + i // epochs for i in range(owners)]
    halo = lax.ppermute(
        before[0][:, :, :, :1, :],
        ("acq", "strip"),
        [(device[i], device[i - 1]) for i in range(1, owners)],
    )
    if plan.parts > 1:
        gradients = focus(plan, plan.parts - 1, fields[-1], spectrum, (weights, before, halo))
    else:
        gradients = slopes_to_epochs(plan, weights, before[0], halo)
    gathered = lax.all_to_all(gradients, "acq", split_axis=0, concat_axis=0, tiled=True)
    gathered = gathered.reshape(epochs, 2, plan.looks * plan.parts, plan.azimuth_looks)
    return gathered.swapaxes(0, 1).reshape(1, 2, -1, plan.azimuth_looks)


def solution(mesh):
    return jax.shard_map(
        per_device,
        mesh=mesh,
        in_specs=(
            P("acq", None, "strip", None),
            P(),
            P(None, None, "strip"),
            P("acq", None),
            P(None, "acq", None),
        ),
        out_specs=P("acq", None, "strip", None),
        check_vma=False,
    )
```

```python
import functools
import math

import jax
import jax.numpy as jnp
import ml_dtypes
import numpy as np
from jax import lax
from jax.experimental import pallas as pl
from jax.experimental.pallas import tpu as pltpu
from jax.sharding import PartitionSpec as P

LOOK = 4
RADIX = 8
ROWS = 8
VMEM_BYTES = 48 * 1024 * 1024
OWNERS = ("strip", "acq")


def add(left, right):
    return (left[0] + right[0], left[1] + right[1])


def sub(left, right):
    return (left[0] - right[0], left[1] - right[1])


def times(value, cosine, sine):
    return (value[0] * cosine - value[1] * sine, value[0] * sine + value[1] * cosine)


def turn(value, sign):
    if sign > 0:
        return (-value[1], value[0])
    return (value[1], -value[0])


def dft4(x0, x1, x2, x3, sign):
    a, b = add(x0, x2), sub(x0, x2)
    c, d = add(x1, x3), turn(sub(x1, x3), sign)
    return [add(a, c), add(b, d), sub(a, c), sub(b, d)]


def dft8(x, sign):
    even = dft4(x[0], x[2], x[4], x[6], sign)
    odd = dft4(x[1], x[3], x[5], x[7], sign)
    half = math.sqrt(0.5)
    o1, o3 = odd[1], odd[3]
    t1 = add(o1, turn(o1, sign))
    t3 = sub(turn(o3, sign), o3)
    odd = [
        odd[0],
        (t1[0] * half, t1[1] * half),
        turn(odd[2], sign),
        (t3[0] * half, t3[1] * half),
    ]
    return [add(e, o) for e, o in zip(even, odd)] + [sub(e, o) for e, o in zip(even, odd)]


def two_parts(value):
    high = value.astype(jnp.bfloat16)
    low = (value - high.astype(jnp.float32)).astype(jnp.bfloat16)
    return high, low


def three_products(left_high, left_low, right_high, right_low, contract):
    def product(left, right):
        return lax.dot_general(
            left, right, (contract, ((), ())), preferred_element_type=jnp.float32
        )

    return (
        product(left_high, right_high)
        + product(left_high, right_low)
        + product(left_low, right_high)
    )


def host_parts(table):
    table = np.asarray(table, np.float64)
    high = table.astype(np.float32).astype(ml_dtypes.bfloat16)
    low = (table - high.astype(np.float64)).astype(np.float32).astype(ml_dtypes.bfloat16)
    return high, low


def unit(exponent, size, sign):
    angle = sign * 2.0 * np.pi / size * (exponent % size)
    return np.cos(angle), np.sin(angle)


def real_form(cosine, sine):
    top = np.concatenate([cosine, sine], axis=-1)
    bottom = np.concatenate([-sine, cosine], axis=-1)
    return np.concatenate([top, bottom], axis=-2)


class Plan:
    def __init__(self, strips, epochs, pulses, samples):
        self.strips, self.epochs = strips, epochs
        self.pulses, self.samples = pulses, samples
        self.azimuth = pulses * strips
        self.base = samples // RADIX
        self.owned = samples // (strips * epochs)
        self.parts = 2 if self.owned % (2 * LOOK * ROWS) == 0 else 1
        self.rows = self.owned // self.parts
        self.looks = self.rows // LOOK
        self.planes = self.looks % ROWS == 0
        self.blocks = self.base // self.owned
        self.lanes = self.azimuth // RADIX
        self.azimuth_looks = self.azimuth // LOOK

    def tile_shift(self, part, block, tile):
        start = block * self.owned + part * self.rows
        if self.planes:
            plane, look = divmod(tile * ROWS, self.looks)
            return start + LOOK * look + plane
        return start + tile * ROWS

    def tile_stride(self):
        return LOOK if self.planes else 1


def lag_tables(plan):
    base, samples = plan.base, plan.samples
    index = np.arange(base)
    table = host_parts(
        np.concatenate(unit(index[:, None] * index[None, :], samples, -1.0), axis=1) / samples
    )
    block = np.arange(RADIX)[:, None]
    turns = np.stack(
        unit(block * index[None, :], RADIX, -1.0)
        + tuple(np.broadcast_to(part, (RADIX, base)) for part in unit(block, RADIX, 1.0))
    )
    return table + (turns.astype(np.float32),)


def lag_vectors(plan, filter_ref, table_high, table_low, turn_ref):
    base = plan.base
    lane = lax.broadcasted_iota(jnp.int32, (RADIX, base), 1)
    chosen = lane % RADIX == lax.broadcasted_iota(jnp.int32, (RADIX, base), 0)
    rows = []
    for c in range(2):
        for e in range(RADIX):
            block = jnp.broadcast_to(filter_ref[c : c + 1, e * base : (e + 1) * base], (RADIX, base))
            rows.append(jnp.where(chosen, block, 0.0))
    high, low = two_parts(jnp.concatenate(rows, axis=0))
    sums = three_products(high, low, table_high[...], table_low[...], ((1,), (0,)))
    real, imag = 0.0, 0.0
    for e in range(RADIX):
        by_real = sums[e * RADIX : (e + 1) * RADIX]
        by_imag = sums[(RADIX + e) * RADIX : (RADIX + e + 1) * RADIX]
        part_real = by_real[:, :base] - by_imag[:, base:]
        part_imag = by_real[:, base:] + by_imag[:, :base]
        cosine, sine = turn_ref[0, e : e + 1, :], turn_ref[1, e : e + 1, :]
        real = real + part_real * cosine - part_imag * sine
        imag = imag + part_real * sine + part_imag * cosine
    cosine, sine = turn_ref[2], turn_ref[3]
    return (
        jnp.concatenate([real, real * cosine - imag * sine], axis=1),
        jnp.concatenate([imag, real * sine + imag * cosine], axis=1),
    )


def fetch(copies):
    for copy in copies:
        copy.start()
    return copies


def compress_kernel(
    plan, part, filter_ref, high_any, low_any, turn_any, raw_ref, out_ref,
    table_high, table_low, turn_ref, raw, t_high, t_low, y_high, y_low, z_ref, sems, table_sems,
):
    base, blocks = plan.base, plan.blocks
    tiles = plan.rows // ROWS
    chunk = blocks * plan.rows
    pieces = sems.shape[0]
    piece = plan.pulses // pieces

    def raw_copy(at):
        rows = pl.ds(at * piece, piece)
        return pltpu.make_async_copy(raw_ref.at[:, rows, :], raw.at[:, rows, :], sems.at[at])

    tables = fetch(
        [
            pltpu.make_async_copy(source, target, table_sems.at[at])
            for at, (source, target) in enumerate(
                ((high_any, table_high), (low_any, table_low), (turn_any, turn_ref))
            )
        ]
    )
    fetch([raw_copy(at) for at in range(pieces)])
    for copy in tables:
        copy.wait()
    lags = lag_vectors(plan, filter_ref, table_high, table_low, turn_ref)

    for d in range(RADIX):
        spread = [
            pltpu.roll(
                jnp.broadcast_to(lag[d : d + 1, :], (ROWS, 2 * base)),
                0,
                1,
                stride=plan.tile_stride(),
                stride_axis=0,
            )
            for lag in lags
        ]
        for pair in range(blocks * tiles // 2):
            real, imag = [], []
            for at in (2 * pair, 2 * pair + 1):
                shift = plan.tile_shift(part, at // tiles, at % tiles)
                real.append(pltpu.roll(spread[0], shift, 1)[:, :base])
                imag.append(pltpu.roll(spread[1], shift, 1)[:, :base])
            real_high, real_low = two_parts(jnp.concatenate(real, axis=0))
            imag_high, imag_low = two_parts(jnp.concatenate(imag, axis=0))
            top = pl.ds(pair * 2 * ROWS, 2 * ROWS)
            bottom = pl.ds(chunk + pair * 2 * ROWS, 2 * ROWS)
            t_high[d, top, :base] = real_high
            t_high[d, top, base:] = -imag_high
            t_high[d, bottom, :base] = imag_high
            t_high[d, bottom, base:] = real_high
            t_low[d, top, :base] = real_low
            t_low[d, top, base:] = -imag_low
            t_low[d, bottom, :base] = imag_low
            t_low[d, bottom, base:] = real_low

    def spread_pulses(at, carry):
        rows = pl.ds(pl.multiple_of(at * 2 * ROWS, 2 * ROWS), 2 * ROWS)
        x = [
            tuple(raw[c, rows, a * base : (a + 1) * base] for c in range(2))
            for a in range(RADIX)
        ]
        for d, value in enumerate(dft8(x, -1.0)):
            for c in range(2):
                high, low = two_parts(value[c])
                y_high[d, rows, c * base : (c + 1) * base] = high
                y_low[d, rows, c * base : (c + 1) * base] = low
        return carry

    steps = piece // (2 * ROWS)
    for at in range(pieces):
        raw_copy(at).wait()
        lax.fori_loop(at * steps, (at + 1) * steps, spread_pulses, 0)

    for d in range(RADIX):
        z_ref[d] = three_products(t_high[d], t_low[d], y_high[d], y_low[d], ((1,), (1,)))

    for block in range(blocks):
        for tile in range(tiles):
            top = (block * tiles + tile) * ROWS
            z = [
                (z_ref[d, top : top + ROWS, :], z_ref[d, chunk + top : chunk + top + ROWS, :])
                for d in range(RADIX)
            ]
            for a, value in enumerate(dft8(z, 1.0)):
                for c in range(2):
                    out_ref[a * blocks + block, c, tile * ROWS : (tile + 1) * ROWS, :] = value[c]


def compress(plan, part, range_filter, raw):
    chunk = plan.blocks * plan.rows
    whole = pl.BlockSpec(memory_space=pltpu.VMEM)
    bytes_moved = 4 * (raw.size + raw.size // plan.parts)
    tables = lag_tables(plan)
    return pl.pallas_call(
        functools.partial(compress_kernel, plan, part),
        out_shape=jax.ShapeDtypeStruct(
            (plan.strips * plan.epochs, 2, plan.rows, plan.pulses), jnp.float32
        ),
        in_specs=[whole] + [pl.BlockSpec(memory_space=pltpu.HBM)] * 4,
        out_specs=whole,
        scratch_shapes=[
            *[pltpu.VMEM(table.shape, table.dtype) for table in tables],
            pltpu.VMEM(raw.shape, jnp.float32),
            pltpu.VMEM((RADIX, 2 * chunk, 2 * plan.base), jnp.bfloat16),
            pltpu.VMEM((RADIX, 2 * chunk, 2 * plan.base), jnp.bfloat16),
            pltpu.VMEM((RADIX, plan.pulses, 2 * plan.base), jnp.bfloat16),
            pltpu.VMEM((RADIX, plan.pulses, 2 * plan.base), jnp.bfloat16),
            pltpu.VMEM((RADIX, 2 * chunk, plan.pulses), jnp.float32),
            pltpu.SemaphoreType.DMA((4,)),
            pltpu.SemaphoreType.DMA((3,)),
        ],
        compiler_params=pltpu.CompilerParams(vmem_limit_bytes=VMEM_BYTES),
        cost_estimate=pl.CostEstimate(
            flops=6 * RADIX * 4 * chunk * plan.base * plan.pulses,
            bytes_accessed=bytes_moved,
            transcendentals=0,
        ),
        name="range_compress",
    )(range_filter, *tables, raw)


def focus_kernel(plan, part, final, *refs):
    field_any, filter_any, high_any, low_any, twiddle_any, sum_any = refs[:6]
    if final:
        weight_ref, before_ref, halo_ref, out_ref = refs[6:10]
    else:
        (out_ref,) = refs[6:7]
    scratch = refs[10 if final else 7 :]
    (
        field_ref, filter_ref, table_high, table_low, twiddle_ref, sum_ref,
        y_high, y_low, z_ref, scene_ref, product_ref, field_sems, table_sems,
    ) = scratch[:13]
    rows, lanes, epochs, looks = plan.rows, plan.lanes, plan.epochs, plan.looks
    step = 2 * ROWS
    group = max(1, step // rows)
    per_block = field_ref.shape[-1] // lanes

    def field_copy(j):
        return pltpu.make_async_copy(field_any.at[:, j], field_ref.at[:, j], field_sems.at[j])

    tables = [
        pltpu.make_async_copy(source, target, table_sems.at[at])
        for at, (source, target) in enumerate(
            (
                (twiddle_any, twiddle_ref),
                (high_any, table_high),
                (low_any, table_low),
                (filter_any.at[part], filter_ref),
                (sum_any, sum_ref),
            )
        )
    ]
    fetch(tables[:1])
    fetch([field_copy(j) for j in range(epochs)])
    fetch(tables[1:])
    tables[0].wait()

    def rows_of(strip, j, c, top, start):
        some = [
            field_ref[strip, j * group + g, c, top : top + min(rows, step), start : start + lanes]
            for g in range(group)
        ]
        return some[0] if group == 1 else jnp.concatenate(some, axis=0)

    def forward(j, carry):
        for g in range(group):
            field_copy(j * group + g).wait()
        for top in range(0, rows, step):
            x = []
            for a in range(RADIX):
                strip, start = a // per_block, a % per_block * lanes
                x.append(tuple(rows_of(strip, j, c, top, start) for c in range(2)))
            at = pl.ds(pl.multiple_of(j * group * rows + top, step), step)
            for d, value in enumerate(dft8(x, -1.0)):
                if d > 0:
                    value = times(value, twiddle_ref[0, d : d + 1, :], twiddle_ref[1, d : d + 1, :])
                for c in range(2):
                    high, low = two_parts(value[c])
                    y_high[d, at, c * lanes : (c + 1) * lanes] = high
                    y_low[d, at, c * lanes : (c + 1) * lanes] = low
        return carry

    lax.fori_loop(0, epochs // group, forward, 0)
    for copy in tables[1:]:
        copy.wait()

    for d in range(RADIX):
        spectrum = three_products(
            y_high[d], y_low[d], table_high[...], table_low[...], ((1,), (0,))
        )
        spectrum = spectrum.reshape(epochs, rows, 2 * lanes)
        real, imag = spectrum[:, :, :lanes], spectrum[:, :, lanes:]
        by_real, by_imag = filter_ref[0, d][None], filter_ref[1, d][None]
        spectrum = jnp.concatenate(
            [real * by_real - imag * by_imag, real * by_imag + imag * by_real], axis=2
        )
        high, low = two_parts(spectrum.reshape(epochs * rows, 2 * lanes))
        z_ref[d] = three_products(high, low, table_high[...], table_low[...], ((1,), (1,)))

    scene_ref[0] = jnp.zeros_like(scene_ref[0])
    scene_ref[1] = jnp.zeros_like(scene_ref[1])

    def backward(j, carry):
        for top in range(0, rows, ROWS):
            at = pl.ds(pl.multiple_of(j * rows + top, ROWS), ROWS)
            z = [
                times(
                    tuple(z_ref[d, at, c * lanes : (c + 1) * lanes] for c in range(2)),
                    twiddle_ref[2, d : d + 1, :],
                    twiddle_ref[3, d : d + 1, :],
                )
                for d in range(RADIX)
            ]
            for a, value in enumerate(dft8(z, 1.0)):
                for c in range(2):
                    scene_ref[j + 2, c, top : top + ROWS, a * lanes : (a + 1) * lanes] = value[c]
        return carry

    lax.fori_loop(0, epochs, backward, 0)

    def look(value):
        if plan.planes:
            return sum(value[q * looks : (q + 1) * looks] for q in range(1, LOOK)) + value[:looks]
        return value.reshape(looks, LOOK, value.shape[-1]).sum(axis=1)

    def interfere(j, carry):
        for a in range(RADIX):
            columns = pl.ds(a * lanes, lanes)
            later = (scene_ref[j + 2, 0, :, columns], scene_ref[j + 2, 1, :, columns])
            for lag in (1, 2):
                earlier = (
                    scene_ref[j + 2 - lag, 0, :, columns],
                    scene_ref[j + 2 - lag, 1, :, columns],
                )
                real = earlier[0] * later[0] + earlier[1] * later[1]
                imag = earlier[1] * later[0] - earlier[0] * later[1]
                product_ref[j, lag - 1, 0, :, columns] = look(real)
                product_ref[j, lag - 1, 1, :, columns] = look(imag)
        return carry

    lax.fori_loop(0, epochs, interfere, 0)

    total = epochs * 4 * looks
    products = product_ref[...].reshape(total, plan.azimuth)
    high, low = two_parts(products)
    weights = sum_ref[...]
    looked = []
    for start in range(0, plan.azimuth, weights.shape[0]):
        columns = slice(start, start + weights.shape[0])
        looked.append(
            jnp.dot(high[:, columns], weights, preferred_element_type=jnp.float32)
            + jnp.dot(low[:, columns], weights, preferred_element_type=jnp.float32)
        )
    looked = jnp.concatenate(looked, axis=1)
    looked = looked.reshape(epochs, 2, 2, looks, plan.azimuth_looks)
    if final:
        looked_ref, slope_ref = scratch[13:]
        for at, before in enumerate(before_ref):
            looked_ref[:, :, :, at * looks : (at + 1) * looks, :] = before[...]
        looked_ref[:, :, :, part * looks :, :] = looked
        slopes_and_sums(plan, weight_ref, looked_ref, halo_ref, out_ref, slope_ref)
    else:
        out_ref[...] = looked


def slopes_and_sums(plan, weight_ref, looked_ref, halo_ref, out_ref, slope_ref):
    epochs = plan.epochs
    columns = plan.azimuth_looks
    inner = lax.broadcasted_iota(jnp.int32, (plan.looks * plan.parts, columns), 1) < columns - 1

    def slopes(at, carry):
        j, lag = at // 2, at % 2
        real, imag = looked_ref[j, lag, 0], looked_ref[j, lag, 1]
        next_real = pltpu.roll(real, columns - 1, 1)
        next_imag = pltpu.roll(imag, columns - 1, 1)
        slope_ref[at, 0] = jnp.where(inner, next_imag * real - next_real * imag, 0.0)
        next_real = jnp.concatenate([real[1:], halo_ref[j, lag, 0]], axis=0)
        next_imag = jnp.concatenate([imag[1:], halo_ref[j, lag, 1]], axis=0)
        slope_ref[at, 1] = next_imag * real - next_real * imag
        return carry

    lax.fori_loop(0, 2 * epochs, slopes, 0)

    def epoch(e, carry):
        total = weight_ref[e, 0] * slope_ref[0]
        for at in range(1, 2 * epochs):
            total = total + weight_ref[e, at] * slope_ref[at]
        out_ref[e] = total
        return carry

    lax.fori_loop(0, epochs, epoch, 0)


def focus_tables(plan):
    lanes = plan.lanes
    index = np.arange(lanes)
    table = host_parts(real_form(*unit(index[:, None] * index[None, :], lanes, -1.0)))
    cosine, sine = unit(np.arange(RADIX)[:, None] * index[None, :], plan.azimuth, -1.0)
    twiddles = np.stack([cosine, sine, cosine / plan.azimuth, -sine / plan.azimuth])
    sums = np.arange(plan.azimuth // 2)[:, None] // LOOK == np.arange(plan.azimuth_looks // 2)[None, :]
    return table + (twiddles.astype(np.float32), (sums / LOOK).astype(ml_dtypes.bfloat16))


def focus(plan, part, field, spectrum, finish=None):
    lanes = plan.lanes
    total = plan.epochs * plan.rows
    tables = focus_tables(plan)
    whole = pl.BlockSpec(memory_space=pltpu.VMEM)
    looked = (plan.epochs, 2, 2, plan.looks, plan.azimuth_looks)
    gradients = (plan.epochs, 2, plan.looks * plan.parts, plan.azimuth_looks)
    operands = [field, spectrum, *tables]
    in_specs = [pl.BlockSpec(memory_space=pltpu.HBM)] * 6
    scratch = [
        pltpu.VMEM(field.shape, jnp.float32),
        pltpu.VMEM(spectrum.shape[1:], jnp.float32),
        *[pltpu.VMEM(table.shape, table.dtype) for table in tables],
        pltpu.VMEM((RADIX, total, 2 * lanes), jnp.bfloat16),
        pltpu.VMEM((RADIX, total, 2 * lanes), jnp.bfloat16),
        pltpu.VMEM((RADIX, total, 2 * lanes), jnp.float32),
        pltpu.VMEM((plan.epochs + 2, 2, plan.rows, plan.azimuth), jnp.float32),
        pltpu.VMEM((plan.epochs, 2, 2, plan.looks, plan.azimuth), jnp.float32),
        pltpu.SemaphoreType.DMA((plan.epochs,)),
        pltpu.SemaphoreType.DMA((5,)),
    ]
    shape = looked
    if finish is not None:
        weights, before, halo = finish
        shape = gradients
        operands += [weights, before, halo]
        in_specs += [pl.BlockSpec(memory_space=pltpu.SMEM), [whole] * len(before), whole]
        scratch += [
            pltpu.VMEM((plan.epochs, 2, 2, plan.looks * plan.parts, plan.azimuth_looks), jnp.float32),
            pltpu.VMEM((2 * plan.epochs,) + gradients[1:], jnp.float32),
        ]
    return pl.pallas_call(
        functools.partial(focus_kernel_flat, plan, part, len(before) if finish else None),
        out_shape=jax.ShapeDtypeStruct(shape, jnp.float32),
        in_specs=jax.tree.leaves(in_specs),
        out_specs=whole,
        scratch_shapes=scratch,
        compiler_params=pltpu.CompilerParams(vmem_limit_bytes=VMEM_BYTES),
        cost_estimate=pl.CostEstimate(
            flops=2 * 6 * RADIX * total * 4 * lanes * lanes,
            bytes_accessed=4 * field.size + 4 * 1024 * 1024,
            transcendentals=0,
        ),
        name="azimuth_focus",
    )(*jax.tree.leaves(operands))


def focus_kernel_flat(plan, part, count, *refs):
    if count is None:
        focus_kernel(plan, part, False, *refs)
        return
    before = refs[7 : 7 + count]
    focus_kernel(plan, part, True, *refs[:7], before, *refs[7 + count :])


def slope_kernel(plan, weight_ref, looked_ref, halo_ref, out_ref, slope_ref):
    slopes_and_sums(plan, weight_ref, looked_ref, halo_ref, out_ref, slope_ref)


def slopes_to_epochs(plan, weights, looked, halo):
    whole = pl.BlockSpec(memory_space=pltpu.VMEM)
    looks = plan.looks * plan.parts
    return pl.pallas_call(
        functools.partial(slope_kernel, plan),
        out_shape=jax.ShapeDtypeStruct(
            (plan.epochs, 2, looks, plan.azimuth_looks), jnp.float32
        ),
        in_specs=[pl.BlockSpec(memory_space=pltpu.SMEM), whole, whole],
        out_specs=whole,
        scratch_shapes=[
            pltpu.VMEM((2 * plan.epochs, 2, looks, plan.azimuth_looks), jnp.float32)
        ],
        compiler_params=pltpu.CompilerParams(vmem_limit_bytes=VMEM_BYTES),
        cost_estimate=pl.CostEstimate(
            flops=8 * looked.size * plan.epochs, bytes_accessed=5 * looked.size, transcendentals=0
        ),
        name="slopes_to_epochs",
    )(weights, looked, halo)


def own_filter(plan, azimuth_filter):
    start = lax.axis_index("acq") * plan.owned
    own = lax.dynamic_slice_in_dim(azimuth_filter, start, plan.owned, axis=2)
    own = own.reshape(2, plan.lanes, RADIX, plan.parts, plan.looks, LOOK)
    order = (3, 0, 2, 5, 4, 1) if plan.planes else (3, 0, 2, 4, 5, 1)
    return own.transpose(order).reshape(plan.parts, 2, RADIX, plan.rows, plan.lanes)


def exchange(plan, block):
    received = lax.all_to_all(block, OWNERS, split_axis=0, concat_axis=0, tiled=True)
    join = max(1, plan.lanes // plan.pulses)
    received = received.reshape(
        plan.strips // join, join, plan.epochs, 2, plan.rows, plan.pulses
    )
    if join > 1:
        received = received.transpose(0, 2, 3, 4, 1, 5)
    return received.reshape(
        plan.strips // join, plan.epochs, 2, plan.rows, join * plan.pulses
    )


def per_device(raw_echoes, range_filter, azimuth_filter, pair_mask, inversion):
    strips, epochs = lax.axis_size("strip"), lax.axis_size("acq")
    plan = Plan(strips, epochs, raw_echoes.shape[2], raw_echoes.shape[3])

    lags = jnp.array([1, 2], dtype=jnp.int32)
    usable = pair_mask[0].astype(jnp.float32) * (lax.axis_index("acq") >= lags).astype(jnp.float32)
    weights = lax.all_gather(inversion[:, 0, :] * usable[None, :], "acq", axis=1, tiled=False)
    weights = weights.reshape(epochs, 2 * epochs)

    spectrum = own_filter(plan, azimuth_filter)
    fields = [
        exchange(plan, compress(plan, part, range_filter, raw_echoes[0]))
        for part in range(plan.parts)
    ]
    before = [focus(plan, part, fields[part], spectrum) for part in range(max(1, plan.parts - 1))]

    owners = strips * epochs
    device = [i % epochs * strips + i // epochs for i in range(owners)]
    halo = lax.ppermute(
        before[0][:, :, :, :1, :],
        ("acq", "strip"),
        [(device[i], device[i - 1]) for i in range(1, owners)],
    )
    if plan.parts > 1:
        gradients = focus(plan, plan.parts - 1, fields[-1], spectrum, (weights, before, halo))
    else:
        gradients = slopes_to_epochs(plan, weights, before[0], halo)
    gathered = lax.all_to_all(gradients, "acq", split_axis=0, concat_axis=0, tiled=True)
    gathered = gathered.reshape(epochs, 2, plan.looks * plan.parts, plan.azimuth_looks)
    return gathered.swapaxes(0, 1).reshape(1, 2, -1, plan.azimuth_looks)


def solution(mesh):
    return jax.shard_map(
        per_device,
        mesh=mesh,
        in_specs=(
            P("acq", None, "strip", None),
            P(),
            P(None, None, "strip"),
            P("acq", None),
            P(None, "acq", None),
        ),
        out_specs=P("acq", None, "strip", None),
        check_vma=False,
    )
```

```python
import functools
import math

import jax
import jax.numpy as jnp
import ml_dtypes
import numpy as np
from jax import lax
from jax.experimental import pallas as pl
from jax.experimental.pallas import tpu as pltpu
from jax.sharding import PartitionSpec as P

LOOK = 4
RADIX = 8
ROWS = 8
VMEM_BYTES = 60 * 1024 * 1024
OWNERS = ("strip", "acq")


def add(left, right):
    return (left[0] + right[0], left[1] + right[1])


def sub(left, right):
    return (left[0] - right[0], left[1] - right[1])


def times(value, cosine, sine):
    return (value[0] * cosine - value[1] * sine, value[0] * sine + value[1] * cosine)


def turn(value, sign):
    if sign > 0:
        return (-value[1], value[0])
    return (value[1], -value[0])


def dft4(x0, x1, x2, x3, sign):
    a, b = add(x0, x2), sub(x0, x2)
    c, d = add(x1, x3), turn(sub(x1, x3), sign)
    return [add(a, c), add(b, d), sub(a, c), sub(b, d)]


def dft8(x, sign):
    even = dft4(x[0], x[2], x[4], x[6], sign)
    odd = dft4(x[1], x[3], x[5], x[7], sign)
    half = math.sqrt(0.5)
    o1, o3 = odd[1], odd[3]
    t1 = add(o1, turn(o1, sign))
    t3 = sub(turn(o3, sign), o3)
    odd = [
        odd[0],
        (t1[0] * half, t1[1] * half),
        turn(odd[2], sign),
        (t3[0] * half, t3[1] * half),
    ]
    return [add(e, o) for e, o in zip(even, odd)] + [sub(e, o) for e, o in zip(even, odd)]


def two_parts(value):
    high = value.astype(jnp.bfloat16)
    low = (value - high.astype(jnp.float32)).astype(jnp.bfloat16)
    return high, low


def three_products(left_high, left_low, right_high, right_low, contract):
    def product(left, right):
        return lax.dot_general(
            left, right, (contract, ((), ())), preferred_element_type=jnp.float32
        )

    return (
        product(left_high, right_high)
        + product(left_high, right_low)
        + product(left_low, right_high)
    )


def host_parts(table):
    table = np.asarray(table, np.float64)
    high = table.astype(np.float32).astype(ml_dtypes.bfloat16)
    low = (table - high.astype(np.float64)).astype(np.float32).astype(ml_dtypes.bfloat16)
    return high, low


def unit(exponent, size, sign):
    angle = sign * 2.0 * np.pi / size * (exponent % size)
    return np.cos(angle), np.sin(angle)


def real_form(cosine, sine):
    top = np.concatenate([cosine, sine], axis=-1)
    bottom = np.concatenate([-sine, cosine], axis=-1)
    return np.concatenate([top, bottom], axis=-2)


class Plan:
    def __init__(self, strips, epochs, pulses, samples):
        self.strips, self.epochs = strips, epochs
        self.pulses, self.samples = pulses, samples
        self.azimuth = pulses * strips
        self.base = samples // RADIX
        self.owned = samples // (strips * epochs)
        self.parts = 2 if self.owned % (2 * LOOK * ROWS) == 0 else 1
        self.rows = self.owned // self.parts
        self.looks = self.rows // LOOK
        self.planes = self.looks % ROWS == 0
        self.blocks = self.base // self.owned
        self.lanes = self.azimuth // RADIX
        self.azimuth_looks = self.azimuth // LOOK

    def outputs(self, form):
        return self.strips if form == "slots" else 1

    def tile_shift(self, part, block, tile):
        start = block * self.owned + part * self.rows
        if self.planes:
            plane, look = divmod(tile * ROWS, self.looks)
            return start + LOOK * look + plane
        return start + tile * ROWS

    def tile_stride(self):
        return LOOK if self.planes else 1


def lag_tables(plan):
    base, samples = plan.base, plan.samples
    index = np.arange(base)
    table = host_parts(
        np.concatenate(unit(index[:, None] * index[None, :], samples, -1.0), axis=1) / samples
    )
    block = np.arange(RADIX)[:, None]
    turns = np.stack(
        unit(block * index[None, :], RADIX, -1.0)
        + tuple(np.broadcast_to(part, (RADIX, base)) for part in unit(block, RADIX, 1.0))
    )
    return table + (turns.astype(np.float32),)


def lag_vectors(plan, filter_ref, table_high, table_low, turn_ref):
    base = plan.base
    lane = lax.broadcasted_iota(jnp.int32, (RADIX, base), 1)
    chosen = lane % RADIX == lax.broadcasted_iota(jnp.int32, (RADIX, base), 0)
    rows = []
    for c in range(2):
        for e in range(RADIX):
            block = jnp.broadcast_to(filter_ref[c : c + 1, e * base : (e + 1) * base], (RADIX, base))
            rows.append(jnp.where(chosen, block, 0.0))
    high, low = two_parts(jnp.concatenate(rows, axis=0))
    sums = three_products(high, low, table_high[...], table_low[...], ((1,), (0,)))
    real, imag = 0.0, 0.0
    for e in range(RADIX):
        by_real = sums[e * RADIX : (e + 1) * RADIX]
        by_imag = sums[(RADIX + e) * RADIX : (RADIX + e + 1) * RADIX]
        part_real = by_real[:, :base] - by_imag[:, base:]
        part_imag = by_real[:, base:] + by_imag[:, :base]
        cosine, sine = turn_ref[0, e : e + 1, :], turn_ref[1, e : e + 1, :]
        real = real + part_real * cosine - part_imag * sine
        imag = imag + part_real * sine + part_imag * cosine
    cosine, sine = turn_ref[2], turn_ref[3]
    return (
        jnp.concatenate([real, real * cosine - imag * sine], axis=1),
        jnp.concatenate([imag, real * sine + imag * cosine], axis=1),
    )


def fetch(copies):
    for copy in copies:
        copy.start()
    return copies


def compress_kernel(
    plan, part, form, filter_ref, high_any, low_any, turn_any, raw_ref, *refs
):
    outs, scratch = refs[: plan.outputs(form)], refs[plan.outputs(form) :]
    (
        table_high, table_low, turn_ref, raw, t_high, t_low, y_high, y_low, z_ref, sems, table_sems,
    ) = scratch
    base, blocks = plan.base, plan.blocks
    tiles = plan.rows // ROWS
    chunk = blocks * plan.rows
    pieces = sems.shape[0]
    piece = plan.pulses // pieces

    def raw_copy(at):
        rows = pl.ds(at * piece, piece)
        return pltpu.make_async_copy(raw_ref.at[:, rows, :], raw.at[:, rows, :], sems.at[at])

    tables = fetch(
        [
            pltpu.make_async_copy(source, target, table_sems.at[at])
            for at, (source, target) in enumerate(
                ((high_any, table_high), (low_any, table_low), (turn_any, turn_ref))
            )
        ]
    )
    fetch([raw_copy(at) for at in range(pieces)])
    for copy in tables:
        copy.wait()
    lags = lag_vectors(plan, filter_ref, table_high, table_low, turn_ref)

    for d in range(RADIX):
        spread = [
            pltpu.roll(
                jnp.broadcast_to(lag[d : d + 1, :], (ROWS, 2 * base)),
                0,
                1,
                stride=plan.tile_stride(),
                stride_axis=0,
            )
            for lag in lags
        ]
        for pair in range(blocks * tiles // 2):
            real, imag = [], []
            for at in (2 * pair, 2 * pair + 1):
                shift = plan.tile_shift(part, at // tiles, at % tiles)
                real.append(pltpu.roll(spread[0], shift, 1)[:, :base])
                imag.append(pltpu.roll(spread[1], shift, 1)[:, :base])
            real_high, real_low = two_parts(jnp.concatenate(real, axis=0))
            imag_high, imag_low = two_parts(jnp.concatenate(imag, axis=0))
            top = pl.ds(pair * 2 * ROWS, 2 * ROWS)
            bottom = pl.ds(chunk + pair * 2 * ROWS, 2 * ROWS)
            t_high[d, top, :base] = real_high
            t_high[d, top, base:] = -imag_high
            t_high[d, bottom, :base] = imag_high
            t_high[d, bottom, base:] = real_high
            t_low[d, top, :base] = real_low
            t_low[d, top, base:] = -imag_low
            t_low[d, bottom, :base] = imag_low
            t_low[d, bottom, base:] = real_low

    def spread_pulses(at, carry):
        rows = pl.ds(pl.multiple_of(at * 2 * ROWS, 2 * ROWS), 2 * ROWS)
        x = [
            tuple(raw[c, rows, a * base : (a + 1) * base] for c in range(2))
            for a in range(RADIX)
        ]
        for d, value in enumerate(dft8(x, -1.0)):
            for c in range(2):
                high, low = two_parts(value[c])
                y_high[d, rows, c * base : (c + 1) * base] = high
                y_low[d, rows, c * base : (c + 1) * base] = low
        return carry

    steps = piece // (2 * ROWS)
    for at in range(pieces):
        raw_copy(at).wait()
        lax.fori_loop(at * steps, (at + 1) * steps, spread_pulses, 0)

    for d in range(RADIX):
        z_ref[d] = three_products(t_high[d], t_low[d], y_high[d], y_low[d], ((1,), (1,)))

    for block in range(blocks):
        for tile in range(tiles):
            top = (block * tiles + tile) * ROWS
            z = [
                (z_ref[d, top : top + ROWS, :], z_ref[d, chunk + top : chunk + top + ROWS, :])
                for d in range(RADIX)
            ]
            for a, value in enumerate(dft8(z, 1.0)):
                for c in range(2):
                    slot, owner = divmod(a * blocks + block, plan.epochs)
                    rows = slice(tile * ROWS, (tile + 1) * ROWS)
                    if form == "slots":
                        outs[slot][owner, c, rows, :] = value[c]
                    elif form == "owners":
                        outs[0][owner, slot, c, rows, :] = value[c]
                    else:
                        outs[0][slot, owner, c, rows, :] = value[c]


def compress(plan, part, form, range_filter, raw):
    chunk = plan.blocks * plan.rows
    whole = pl.BlockSpec(memory_space=pltpu.VMEM)
    bytes_moved = 4 * (raw.size + raw.size // plan.parts)
    tables = lag_tables(plan)
    slab = (2, plan.rows, plan.pulses)
    shape = {
        "slots": (plan.epochs,) + slab,
        "owners": (plan.epochs, plan.strips) + slab,
        "all": (plan.strips, plan.epochs) + slab,
    }[form]
    return pl.pallas_call(
        functools.partial(compress_kernel, plan, part, form),
        out_shape=[jax.ShapeDtypeStruct(shape, jnp.float32)] * plan.outputs(form),
        in_specs=[whole] + [pl.BlockSpec(memory_space=pltpu.HBM)] * 4,
        out_specs=[whole] * plan.outputs(form),
        scratch_shapes=[
            *[pltpu.VMEM(table.shape, table.dtype) for table in tables],
            pltpu.VMEM(raw.shape, jnp.float32),
            pltpu.VMEM((RADIX, 2 * chunk, 2 * plan.base), jnp.bfloat16),
            pltpu.VMEM((RADIX, 2 * chunk, 2 * plan.base), jnp.bfloat16),
            pltpu.VMEM((RADIX, plan.pulses, 2 * plan.base), jnp.bfloat16),
            pltpu.VMEM((RADIX, plan.pulses, 2 * plan.base), jnp.bfloat16),
            pltpu.VMEM((RADIX, 2 * chunk, plan.pulses), jnp.float32),
            pltpu.SemaphoreType.DMA((4,)),
            pltpu.SemaphoreType.DMA((3,)),
        ],
        compiler_params=pltpu.CompilerParams(vmem_limit_bytes=VMEM_BYTES),
        cost_estimate=pl.CostEstimate(
            flops=6 * RADIX * 4 * chunk * plan.base * plan.pulses,
            bytes_accessed=bytes_moved,
            transcendentals=0,
        ),
        name="range_compress",
    )(range_filter, *tables, raw)


def focus_kernel(plan, part, final, field_at, *refs):
    filter_any, high_any, low_any, twiddle_any, sum_any = refs[:5]
    if final:
        weight_ref, before_ref, halo_ref, out_ref = refs[5:9]
    else:
        (out_ref,) = refs[5:6]
    scratch = refs[9 if final else 6 :]
    (
        field_ref, filter_ref, table_high, table_low, twiddle_ref, sum_ref,
        y_high, y_low, z_ref, scene_ref, product_ref, field_sems, table_sems,
    ) = scratch[:13]
    rows, lanes, epochs, looks = plan.rows, plan.lanes, plan.epochs, plan.looks
    step = 2 * ROWS
    group = max(1, step // rows)
    per_block = field_ref.shape[-1] // lanes

    def field_copies(j):
        return [
            pltpu.make_async_copy(field_at(j, at), field_ref.at[at, j], field_sems.at[j, at])
            for at in range(field_ref.shape[0])
        ]

    tables = [
        pltpu.make_async_copy(source, target, table_sems.at[at])
        for at, (source, target) in enumerate(
            (
                (twiddle_any, twiddle_ref),
                (high_any, table_high),
                (low_any, table_low),
                (filter_any.at[part], filter_ref),
                (sum_any, sum_ref),
            )
        )
    ]
    fetch(tables[:1])
    for j in range(epochs):
        fetch(field_copies(j))
    fetch(tables[1:])
    tables[0].wait()

    def rows_of(strip, j, c, top, start):
        some = [
            field_ref[strip, j * group + g, c, top : top + min(rows, step), start : start + lanes]
            for g in range(group)
        ]
        return some[0] if group == 1 else jnp.concatenate(some, axis=0)

    def forward(j, carry):
        for g in range(group):
            for copy in field_copies(j * group + g):
                copy.wait()
        for top in range(0, rows, step):
            x = []
            for a in range(RADIX):
                strip, start = a // per_block, a % per_block * lanes
                x.append(tuple(rows_of(strip, j, c, top, start) for c in range(2)))
            at = pl.ds(pl.multiple_of(j * group * rows + top, step), step)
            for d, value in enumerate(dft8(x, -1.0)):
                if d > 0:
                    value = times(value, twiddle_ref[0, d : d + 1, :], twiddle_ref[1, d : d + 1, :])
                for c in range(2):
                    high, low = two_parts(value[c])
                    y_high[d, at, c * lanes : (c + 1) * lanes] = high
                    y_low[d, at, c * lanes : (c + 1) * lanes] = low
        return carry

    lax.fori_loop(0, epochs // group, forward, 0)
    for copy in tables[1:]:
        copy.wait()

    for d in range(RADIX):
        spectrum = three_products(
            y_high[d], y_low[d], table_high[...], table_low[...], ((1,), (0,))
        )
        spectrum = spectrum.reshape(epochs, rows, 2 * lanes)
        real, imag = spectrum[:, :, :lanes], spectrum[:, :, lanes:]
        by_real, by_imag = filter_ref[0, d][None], filter_ref[1, d][None]
        spectrum = jnp.concatenate(
            [real * by_real - imag * by_imag, real * by_imag + imag * by_real], axis=2
        )
        high, low = two_parts(spectrum.reshape(epochs * rows, 2 * lanes))
        z_ref[d] = three_products(high, low, table_high[...], table_low[...], ((1,), (1,)))

    scene_ref[0] = jnp.zeros_like(scene_ref[0])
    scene_ref[1] = jnp.zeros_like(scene_ref[1])

    def backward(j, carry):
        for top in range(0, rows, ROWS):
            at = pl.ds(pl.multiple_of(j * rows + top, ROWS), ROWS)
            z = [
                times(
                    tuple(z_ref[d, at, c * lanes : (c + 1) * lanes] for c in range(2)),
                    twiddle_ref[2, d : d + 1, :],
                    twiddle_ref[3, d : d + 1, :],
                )
                for d in range(RADIX)
            ]
            for a, value in enumerate(dft8(z, 1.0)):
                for c in range(2):
                    scene_ref[j + 2, c, top : top + ROWS, a * lanes : (a + 1) * lanes] = value[c]
        return carry

    lax.fori_loop(0, epochs, backward, 0)

    def look(value):
        if plan.planes:
            return sum(value[q * looks : (q + 1) * looks] for q in range(1, LOOK)) + value[:looks]
        return value.reshape(looks, LOOK, value.shape[-1]).sum(axis=1)

    def interfere(j, carry):
        for a in range(RADIX):
            columns = pl.ds(a * lanes, lanes)
            later = (scene_ref[j + 2, 0, :, columns], scene_ref[j + 2, 1, :, columns])
            for lag in (1, 2):
                earlier = (
                    scene_ref[j + 2 - lag, 0, :, columns],
                    scene_ref[j + 2 - lag, 1, :, columns],
                )
                real = earlier[0] * later[0] + earlier[1] * later[1]
                imag = earlier[1] * later[0] - earlier[0] * later[1]
                product_ref[j, lag - 1, 0, :, columns] = look(real)
                product_ref[j, lag - 1, 1, :, columns] = look(imag)
        return carry

    lax.fori_loop(0, epochs, interfere, 0)

    total = epochs * 4 * looks
    products = product_ref[...].reshape(total, plan.azimuth)
    high, low = two_parts(products)
    weights = sum_ref[...]
    looked = []
    for start in range(0, plan.azimuth, weights.shape[0]):
        columns = slice(start, start + weights.shape[0])
        looked.append(
            jnp.dot(high[:, columns], weights, preferred_element_type=jnp.float32)
            + jnp.dot(low[:, columns], weights, preferred_element_type=jnp.float32)
        )
    looked = jnp.concatenate(looked, axis=1)
    looked = looked.reshape(epochs, 2, 2, looks, plan.azimuth_looks)
    if final:
        looked_ref, slope_ref = scratch[13:]
        for at, before in enumerate(before_ref):
            looked_ref[:, :, :, at * looks : (at + 1) * looks, :] = before[...]
        looked_ref[:, :, :, part * looks :, :] = looked
        slopes_and_sums(plan, weight_ref, looked_ref, halo_ref, out_ref, slope_ref)
    else:
        out_ref[...] = looked


def slopes_and_sums(plan, weight_ref, looked_ref, halo_ref, out_ref, slope_ref):
    epochs = plan.epochs
    columns = plan.azimuth_looks
    inner = lax.broadcasted_iota(jnp.int32, (plan.looks * plan.parts, columns), 1) < columns - 1

    def slopes(at, carry):
        j, lag = at // 2, at % 2
        real, imag = looked_ref[j, lag, 0], looked_ref[j, lag, 1]
        next_real = pltpu.roll(real, columns - 1, 1)
        next_imag = pltpu.roll(imag, columns - 1, 1)
        slope_ref[at, 0] = jnp.where(inner, next_imag * real - next_real * imag, 0.0)
        next_real = jnp.concatenate([real[1:], halo_ref[j, lag, 0]], axis=0)
        next_imag = jnp.concatenate([imag[1:], halo_ref[j, lag, 1]], axis=0)
        slope_ref[at, 1] = next_imag * real - next_real * imag
        return carry

    lax.fori_loop(0, 2 * epochs, slopes, 0)

    def epoch(e, carry):
        total = weight_ref[e, 0] * slope_ref[0]
        for at in range(1, 2 * epochs):
            total = total + weight_ref[e, at] * slope_ref[at]
        out_ref[e] = total
        return carry

    lax.fori_loop(0, epochs, epoch, 0)


def focus_tables(plan):
    lanes = plan.lanes
    index = np.arange(lanes)
    table = host_parts(real_form(*unit(index[:, None] * index[None, :], lanes, -1.0)))
    cosine, sine = unit(np.arange(RADIX)[:, None] * index[None, :], plan.azimuth, -1.0)
    twiddles = np.stack([cosine, sine, cosine / plan.azimuth, -sine / plan.azimuth])
    sums = np.arange(plan.azimuth // 2)[:, None] // LOOK == np.arange(plan.azimuth_looks // 2)[None, :]
    return table + (twiddles.astype(np.float32), (sums / LOOK).astype(ml_dtypes.bfloat16))


def focus(plan, part, fields, by_owner, spectrum, finish=None):
    lanes = plan.lanes
    total = plan.epochs * plan.rows
    tables = focus_tables(plan)
    whole = pl.BlockSpec(memory_space=pltpu.VMEM)
    looked = (plan.epochs, 2, 2, plan.looks, plan.azimuth_looks)
    gradients = (plan.epochs, 2, plan.looks * plan.parts, plan.azimuth_looks)
    operands = [*fields, spectrum, *tables]
    in_specs = [pl.BlockSpec(memory_space=pltpu.HBM)] * len(operands)
    blocks = plan.azimuth // fields[0].shape[-1]
    before = ()
    scratch = [
        pltpu.VMEM((blocks, plan.epochs) + fields[0].shape[-3:], jnp.float32),
        pltpu.VMEM(spectrum.shape[1:], jnp.float32),
        *[pltpu.VMEM(table.shape, table.dtype) for table in tables],
        pltpu.VMEM((RADIX, total, 2 * lanes), jnp.bfloat16),
        pltpu.VMEM((RADIX, total, 2 * lanes), jnp.bfloat16),
        pltpu.VMEM((RADIX, total, 2 * lanes), jnp.float32),
        pltpu.VMEM((plan.epochs + 2, 2, plan.rows, plan.azimuth), jnp.float32),
        pltpu.VMEM((plan.epochs, 2, 2, plan.looks, plan.azimuth), jnp.float32),
        pltpu.SemaphoreType.DMA((plan.epochs, blocks)),
        pltpu.SemaphoreType.DMA((5,)),
    ]
    shape = looked
    if finish is not None:
        weights, before, halo = finish
        shape = gradients
        operands += [weights, *before, halo]
        in_specs += [pl.BlockSpec(memory_space=pltpu.SMEM)] + [whole] * (len(before) + 1)
        scratch += [
            pltpu.VMEM((plan.epochs, 2, 2, plan.looks * plan.parts, plan.azimuth_looks), jnp.float32),
            pltpu.VMEM((2 * plan.epochs,) + gradients[1:], jnp.float32),
        ]

    def kernel(*refs):
        some, refs = refs[: len(fields)], refs[len(fields) :]

        def field_at(j, at):
            if len(some) > 1:
                return some[at].at[j]
            return some[0].at[j, at] if by_owner else some[0].at[at, j]

        if finish is None:
            focus_kernel(plan, part, False, field_at, *refs)
        else:
            count = len(before)
            focus_kernel(
                plan, part, True, field_at, *refs[:6], refs[6 : 6 + count], *refs[6 + count :]
            )

    return pl.pallas_call(
        kernel,
        out_shape=jax.ShapeDtypeStruct(shape, jnp.float32),
        in_specs=in_specs,
        out_specs=whole,
        scratch_shapes=scratch,
        compiler_params=pltpu.CompilerParams(vmem_limit_bytes=VMEM_BYTES),
        cost_estimate=pl.CostEstimate(
            flops=2 * 6 * RADIX * total * 4 * lanes * lanes,
            bytes_accessed=4 * blocks * fields[0].size + 4 * 1024 * 1024,
            transcendentals=0,
        ),
        name="azimuth_focus",
    )(*operands)


def slope_kernel(plan, weight_ref, looked_ref, halo_ref, out_ref, slope_ref):
    slopes_and_sums(plan, weight_ref, looked_ref, halo_ref, out_ref, slope_ref)


def slopes_to_epochs(plan, weights, looked, halo):
    whole = pl.BlockSpec(memory_space=pltpu.VMEM)
    looks = plan.looks * plan.parts
    return pl.pallas_call(
        functools.partial(slope_kernel, plan),
        out_shape=jax.ShapeDtypeStruct(
            (plan.epochs, 2, looks, plan.azimuth_looks), jnp.float32
        ),
        in_specs=[pl.BlockSpec(memory_space=pltpu.SMEM), whole, whole],
        out_specs=whole,
        scratch_shapes=[
            pltpu.VMEM((2 * plan.epochs, 2, looks, plan.azimuth_looks), jnp.float32)
        ],
        compiler_params=pltpu.CompilerParams(vmem_limit_bytes=VMEM_BYTES),
        cost_estimate=pl.CostEstimate(
            flops=8 * looked.size * plan.epochs, bytes_accessed=5 * looked.size, transcendentals=0
        ),
        name="slopes_to_epochs",
    )(weights, looked, halo)


def strip_turn(length, sign):
    strips = lax.axis_size("strip")
    step = lax.axis_index("strip") * jnp.arange(length, dtype=jnp.int32) % strips
    angle = sign * 2.0 * math.pi / strips * step.astype(jnp.float32)
    return jnp.cos(angle), jnp.sin(angle)


def own_filter(plan, azimuth_filter, shifted):
    start = lax.axis_index("acq") * plan.owned
    own = lax.dynamic_slice_in_dim(azimuth_filter, start, plan.owned, axis=2)
    if shifted:
        cosine, sine = strip_turn(plan.azimuth, -1.0)
        own = jnp.stack(times(own, cosine[:, None], sine[:, None]))
    own = own.reshape(2, plan.lanes, RADIX, plan.parts, plan.looks, LOOK)
    order = (3, 0, 2, 5, 4, 1) if plan.planes else (3, 0, 2, 4, 5, 1)
    return own.transpose(order).reshape(plan.parts, 2, RADIX, plan.rows, plan.lanes)


def exchange_all(plan, block):
    shape = block.shape
    block = block.reshape((plan.strips * plan.epochs,) + shape[2:])
    received = lax.all_to_all(block, OWNERS, split_axis=0, concat_axis=0, tiled=True)
    join = max(1, plan.lanes // plan.pulses)
    received = received.reshape((plan.strips // join, join) + shape[1:])
    if join > 1:
        received = received.transpose(0, 2, 3, 4, 1, 5)
    return received.reshape(plan.strips // join, plan.epochs, 2, plan.rows, join * plan.pulses)


def to_owners(block):
    return lax.all_to_all(block, "acq", split_axis=0, concat_axis=0, tiled=True)


def to_strips(plan, slots):
    strips = plan.strips
    moved = [slots[0]]
    for k in range(1, strips):
        route = [(i, (i + k) % strips) for i in range(strips)]
        moved.append(lax.ppermute(slots[k], "strip", route))
    return [moved[-place % strips] for place in range(strips)]


def per_device(raw_echoes, range_filter, azimuth_filter, pair_mask, inversion):
    strips, epochs = lax.axis_size("strip"), lax.axis_size("acq")
    plan = Plan(strips, epochs, raw_echoes.shape[2], raw_echoes.shape[3])

    lags = jnp.array([1, 2], dtype=jnp.int32)
    usable = pair_mask[0].astype(jnp.float32) * (lax.axis_index("acq") >= lags).astype(jnp.float32)
    weights = lax.all_gather(inversion[:, 0, :] * usable[None, :], "acq", axis=1, tiled=False)
    weights = weights.reshape(epochs, 2 * epochs)

    raw = raw_echoes[0]
    if plan.parts == 1:
        spectrum = own_filter(plan, azimuth_filter, False)
        (block,) = compress(plan, 0, "all", range_filter, raw)
        before = [focus(plan, 0, [exchange_all(plan, block)], False, spectrum)]
    else:
        spectrum = own_filter(plan, azimuth_filter, True)
        turned = jnp.stack(times(range_filter, *strip_turn(plan.samples, 1.0)))
        slots = compress(plan, 0, "slots", turned, raw)
        (block,) = compress(plan, 1, "owners", turned, raw)
        first = to_strips(plan, slots)
        block = to_owners(block)
        second = to_strips(plan, [block[:, k] for k in range(strips)])
        first = to_owners(jnp.stack(first, axis=1))
        before = [focus(plan, 0, [first], True, spectrum)]

    owners = strips * epochs
    device = [i % epochs * strips + i // epochs for i in range(owners)]
    halo = lax.ppermute(
        before[0][:, :, :, :1, :],
        ("acq", "strip"),
        [(device[i], device[i - 1]) for i in range(1, owners)],
    )
    if plan.parts > 1:
        gradients = focus(plan, 1, second, True, spectrum, (weights, before, halo))
    else:
        gradients = slopes_to_epochs(plan, weights, before[0], halo)
    gathered = lax.all_to_all(gradients, "acq", split_axis=0, concat_axis=0, tiled=True)
    gathered = gathered.reshape(epochs, 2, plan.looks * plan.parts, plan.azimuth_looks)
    return gathered.swapaxes(0, 1).reshape(1, 2, -1, plan.azimuth_looks)


def solution(mesh):
    return jax.shard_map(
        per_device,
        mesh=mesh,
        in_specs=(
            P("acq", None, "strip", None),
            P(),
            P(None, None, "strip"),
            P("acq", None),
            P(None, "acq", None),
        ),
        out_specs=P("acq", None, "strip", None),
        check_vma=False,
    )
```

```python
import functools
import math

import jax
import jax.numpy as jnp
import ml_dtypes
import numpy as np
from jax import lax
from jax.experimental import pallas as pl
from jax.experimental.pallas import tpu as pltpu
from jax.sharding import PartitionSpec as P

LOOK = 4
RADIX = 8
ROWS = 8
VMEM_BYTES = 60 * 1024 * 1024
OWNERS = ("strip", "acq")


def add(left, right):
    return (left[0] + right[0], left[1] + right[1])


def sub(left, right):
    return (left[0] - right[0], left[1] - right[1])


def times(value, cosine, sine):
    return (value[0] * cosine - value[1] * sine, value[0] * sine + value[1] * cosine)


def turn(value, sign):
    if sign > 0:
        return (-value[1], value[0])
    return (value[1], -value[0])


def dft4(x0, x1, x2, x3, sign):
    a, b = add(x0, x2), sub(x0, x2)
    c, d = add(x1, x3), turn(sub(x1, x3), sign)
    return [add(a, c), add(b, d), sub(a, c), sub(b, d)]


def dft8(x, sign):
    even = dft4(x[0], x[2], x[4], x[6], sign)
    odd = dft4(x[1], x[3], x[5], x[7], sign)
    half = math.sqrt(0.5)
    o1, o3 = odd[1], odd[3]
    t1 = add(o1, turn(o1, sign))
    t3 = sub(turn(o3, sign), o3)
    odd = [
        odd[0],
        (t1[0] * half, t1[1] * half),
        turn(odd[2], sign),
        (t3[0] * half, t3[1] * half),
    ]
    return [add(e, o) for e, o in zip(even, odd)] + [sub(e, o) for e, o in zip(even, odd)]


def two_parts(value):
    high = value.astype(jnp.bfloat16)
    low = (value - high.astype(jnp.float32)).astype(jnp.bfloat16)
    return high, low


def three_products(left_high, left_low, right_high, right_low, contract):
    def product(left, right):
        return lax.dot_general(
            left, right, (contract, ((), ())), preferred_element_type=jnp.float32
        )

    return (
        product(left_high, right_high)
        + product(left_high, right_low)
        + product(left_low, right_high)
    )


def host_parts(table):
    table = np.asarray(table, np.float64)
    high = table.astype(np.float32).astype(ml_dtypes.bfloat16)
    low = (table - high.astype(np.float64)).astype(np.float32).astype(ml_dtypes.bfloat16)
    return high, low


def unit(exponent, size, sign):
    angle = sign * 2.0 * np.pi / size * (exponent % size)
    return np.cos(angle), np.sin(angle)


def real_form(cosine, sine):
    top = np.concatenate([cosine, sine], axis=-1)
    bottom = np.concatenate([-sine, cosine], axis=-1)
    return np.concatenate([top, bottom], axis=-2)


class Plan:
    def __init__(self, strips, epochs, pulses, samples):
        self.strips, self.epochs = strips, epochs
        self.pulses, self.samples = pulses, samples
        self.azimuth = pulses * strips
        self.base = samples // RADIX
        self.owned = samples // (strips * epochs)
        even = all(size & (size - 1) == 0 for size in (strips, epochs))
        self.parts = 2 if even and self.owned % (2 * LOOK * ROWS) == 0 else 1
        self.rows = self.owned // self.parts
        self.looks = self.rows // LOOK
        self.planes = self.looks % ROWS == 0
        self.blocks = self.base // self.owned
        self.lanes = self.azimuth // RADIX
        self.azimuth_looks = self.azimuth // LOOK

    def tile_shift(self, part, block, tile):
        start = block * self.owned + part * self.rows
        if self.planes:
            plane, look = divmod(tile * ROWS, self.looks)
            return start + LOOK * look + plane
        return start + tile * ROWS

    def tile_stride(self):
        return LOOK if self.planes else 1


def lag_tables(plan):
    base, samples = plan.base, plan.samples
    index = np.arange(base)
    table = host_parts(
        np.concatenate(unit(index[:, None] * index[None, :], samples, -1.0), axis=1) / samples
    )
    block = np.arange(RADIX)[:, None]
    turns = np.stack(
        unit(block * index[None, :], RADIX, -1.0)
        + tuple(np.broadcast_to(part, (RADIX, base)) for part in unit(block, RADIX, 1.0))
    )
    return table + (turns.astype(np.float32),)


def lag_vectors(plan, filter_ref, table_high, table_low, turn_ref):
    base = plan.base
    lane = lax.broadcasted_iota(jnp.int32, (RADIX, base), 1)
    chosen = lane % RADIX == lax.broadcasted_iota(jnp.int32, (RADIX, base), 0)
    rows = []
    for c in range(2):
        for e in range(RADIX):
            block = jnp.broadcast_to(filter_ref[c : c + 1, e * base : (e + 1) * base], (RADIX, base))
            rows.append(jnp.where(chosen, block, 0.0))
    high, low = two_parts(jnp.concatenate(rows, axis=0))
    sums = three_products(high, low, table_high[...], table_low[...], ((1,), (0,)))
    real, imag = 0.0, 0.0
    for e in range(RADIX):
        by_real = sums[e * RADIX : (e + 1) * RADIX]
        by_imag = sums[(RADIX + e) * RADIX : (RADIX + e + 1) * RADIX]
        part_real = by_real[:, :base] - by_imag[:, base:]
        part_imag = by_real[:, base:] + by_imag[:, :base]
        cosine, sine = turn_ref[0, e : e + 1, :], turn_ref[1, e : e + 1, :]
        real = real + part_real * cosine - part_imag * sine
        imag = imag + part_real * sine + part_imag * cosine
    cosine, sine = turn_ref[2], turn_ref[3]
    return (
        jnp.concatenate([real, real * cosine - imag * sine], axis=1),
        jnp.concatenate([imag, real * sine + imag * cosine], axis=1),
    )


def fetch(copies):
    for copy in copies:
        copy.start()
    return copies


def compress_kernel(
    plan, part, relative, filter_ref, high_any, low_any, turn_any, raw_ref, out_ref,
    table_high, table_low, turn_ref, raw, t_high, t_low, y_high, y_low, z_ref, sems, table_sems,
):
    base, blocks = plan.base, plan.blocks
    tiles = plan.rows // ROWS
    chunk = blocks * plan.rows
    pieces = sems.shape[0]
    piece = plan.pulses // pieces

    def raw_copy(at):
        rows = pl.ds(at * piece, piece)
        return pltpu.make_async_copy(raw_ref.at[:, rows, :], raw.at[:, rows, :], sems.at[at])

    tables = fetch(
        [
            pltpu.make_async_copy(source, target, table_sems.at[at])
            for at, (source, target) in enumerate(
                ((high_any, table_high), (low_any, table_low), (turn_any, turn_ref))
            )
        ]
    )
    fetch([raw_copy(at) for at in range(pieces)])
    for copy in tables:
        copy.wait()
    lags = lag_vectors(plan, filter_ref, table_high, table_low, turn_ref)

    for d in range(RADIX):
        spread = [
            pltpu.roll(
                jnp.broadcast_to(lag[d : d + 1, :], (ROWS, 2 * base)),
                0,
                1,
                stride=plan.tile_stride(),
                stride_axis=0,
            )
            for lag in lags
        ]
        for pair in range(blocks * tiles // 2):
            real, imag = [], []
            for at in (2 * pair, 2 * pair + 1):
                shift = plan.tile_shift(part, at // tiles, at % tiles)
                real.append(pltpu.roll(spread[0], shift, 1)[:, :base])
                imag.append(pltpu.roll(spread[1], shift, 1)[:, :base])
            real_high, real_low = two_parts(jnp.concatenate(real, axis=0))
            imag_high, imag_low = two_parts(jnp.concatenate(imag, axis=0))
            top = pl.ds(pair * 2 * ROWS, 2 * ROWS)
            bottom = pl.ds(chunk + pair * 2 * ROWS, 2 * ROWS)
            t_high[d, top, :base] = real_high
            t_high[d, top, base:] = -imag_high
            t_high[d, bottom, :base] = imag_high
            t_high[d, bottom, base:] = real_high
            t_low[d, top, :base] = real_low
            t_low[d, top, base:] = -imag_low
            t_low[d, bottom, :base] = imag_low
            t_low[d, bottom, base:] = real_low

    def spread_pulses(at, carry):
        rows = pl.ds(pl.multiple_of(at * 2 * ROWS, 2 * ROWS), 2 * ROWS)
        x = [
            tuple(raw[c, rows, a * base : (a + 1) * base] for c in range(2))
            for a in range(RADIX)
        ]
        for d, value in enumerate(dft8(x, -1.0)):
            for c in range(2):
                high, low = two_parts(value[c])
                y_high[d, rows, c * base : (c + 1) * base] = high
                y_low[d, rows, c * base : (c + 1) * base] = low
        return carry

    steps = piece // (2 * ROWS)
    for at in range(pieces):
        raw_copy(at).wait()
        lax.fori_loop(at * steps, (at + 1) * steps, spread_pulses, 0)

    for d in range(RADIX):
        z_ref[d] = three_products(t_high[d], t_low[d], y_high[d], y_low[d], ((1,), (1,)))

    for block in range(blocks):
        for tile in range(tiles):
            top = (block * tiles + tile) * ROWS
            z = [
                (z_ref[d, top : top + ROWS, :], z_ref[d, chunk + top : chunk + top + ROWS, :])
                for d in range(RADIX)
            ]
            for a, value in enumerate(dft8(z, 1.0)):
                for c in range(2):
                    strip, owner = divmod(a * blocks + block, plan.epochs)
                    rows = slice(tile * ROWS, (tile + 1) * ROWS)
                    if relative:
                        place = owner ^ lax.axis_index("acq"), strip ^ lax.axis_index("strip")
                    else:
                        place = strip, owner
                    out_ref[place[0], place[1], c, rows, :] = value[c]


def compress(plan, part, relative, range_filter, raw):
    chunk = plan.blocks * plan.rows
    whole = pl.BlockSpec(memory_space=pltpu.VMEM)
    bytes_moved = 4 * (raw.size + raw.size // plan.parts)
    tables = lag_tables(plan)
    places = (plan.strips, plan.epochs)
    places = places[::-1] if relative else places
    return pl.pallas_call(
        functools.partial(compress_kernel, plan, part, relative),
        out_shape=jax.ShapeDtypeStruct(places + (2, plan.rows, plan.pulses), jnp.float32),
        in_specs=[whole] + [pl.BlockSpec(memory_space=pltpu.HBM)] * 4,
        out_specs=whole,
        scratch_shapes=[
            *[pltpu.VMEM(table.shape, table.dtype) for table in tables],
            pltpu.VMEM(raw.shape, jnp.float32),
            pltpu.VMEM((RADIX, 2 * chunk, 2 * plan.base), jnp.bfloat16),
            pltpu.VMEM((RADIX, 2 * chunk, 2 * plan.base), jnp.bfloat16),
            pltpu.VMEM((RADIX, plan.pulses, 2 * plan.base), jnp.bfloat16),
            pltpu.VMEM((RADIX, plan.pulses, 2 * plan.base), jnp.bfloat16),
            pltpu.VMEM((RADIX, 2 * chunk, plan.pulses), jnp.float32),
            pltpu.SemaphoreType.DMA((4,)),
            pltpu.SemaphoreType.DMA((3,)),
        ],
        compiler_params=pltpu.CompilerParams(vmem_limit_bytes=VMEM_BYTES),
        cost_estimate=pl.CostEstimate(
            flops=6 * RADIX * 4 * chunk * plan.base * plan.pulses,
            bytes_accessed=bytes_moved,
            transcendentals=0,
        ),
        name="range_compress",
    )(range_filter, *tables, raw)


def focus_kernel(plan, part, final, field_at, own, *refs):
    filter_any, high_any, low_any, twiddle_any, sum_any = refs[:5]
    if final:
        weight_ref, before_ref, halo_ref, out_ref = refs[5:9]
    else:
        (out_ref,) = refs[5:6]
    scratch = refs[9 if final else 6 :]
    (
        field_ref, filter_ref, table_high, table_low, twiddle_ref, sum_ref,
        y_high, y_low, z_ref, scene_ref, product_ref, field_sems, table_sems,
    ) = scratch[:13]
    rows, lanes, epochs, looks = plan.rows, plan.lanes, plan.epochs, plan.looks
    step = 2 * ROWS
    group = max(1, step // rows)
    per_block = field_ref.shape[-1] // lanes

    def field_copies(slot):
        return [
            pltpu.make_async_copy(
                field_at(slot, at), field_ref.at[at ^ own[1], slot ^ own[0]], field_sems.at[slot, at]
            )
            for at in range(field_ref.shape[0])
        ]

    tables = [
        pltpu.make_async_copy(source, target, table_sems.at[at])
        for at, (source, target) in enumerate(
            (
                (twiddle_any, twiddle_ref),
                (high_any, table_high),
                (low_any, table_low),
                (filter_any.at[part], filter_ref),
                (sum_any, sum_ref),
            )
        )
    ]
    fetch(tables[:1])
    for j in range(epochs):
        fetch(field_copies(j))
    fetch(tables[1:])
    tables[0].wait()

    def rows_of(strip, j, c, top, start):
        some = [
            field_ref[strip, j + g, c, top : top + min(rows, step), start : start + lanes]
            for g in range(group)
        ]
        return some[0] if group == 1 else jnp.concatenate(some, axis=0)

    def forward(at, carry):
        for g in range(group):
            for copy in field_copies(at * group + g):
                copy.wait()
        j = at * group ^ own[0]
        for top in range(0, rows, step):
            x = []
            for a in range(RADIX):
                strip, start = a // per_block, a % per_block * lanes
                x.append(tuple(rows_of(strip, j, c, top, start) for c in range(2)))
            at = pl.ds(pl.multiple_of(j * rows + top, step), step)
            for d, value in enumerate(dft8(x, -1.0)):
                if d > 0:
                    value = times(value, twiddle_ref[0, d : d + 1, :], twiddle_ref[1, d : d + 1, :])
                for c in range(2):
                    high, low = two_parts(value[c])
                    y_high[d, at, c * lanes : (c + 1) * lanes] = high
                    y_low[d, at, c * lanes : (c + 1) * lanes] = low
        return carry

    lax.fori_loop(0, epochs // group, forward, 0)
    for copy in tables[1:]:
        copy.wait()

    for d in range(RADIX):
        spectrum = three_products(
            y_high[d], y_low[d], table_high[...], table_low[...], ((1,), (0,))
        )
        spectrum = spectrum.reshape(epochs, rows, 2 * lanes)
        real, imag = spectrum[:, :, :lanes], spectrum[:, :, lanes:]
        by_real, by_imag = filter_ref[0, d][None], filter_ref[1, d][None]
        spectrum = jnp.concatenate(
            [real * by_real - imag * by_imag, real * by_imag + imag * by_real], axis=2
        )
        high, low = two_parts(spectrum.reshape(epochs * rows, 2 * lanes))
        z_ref[d] = three_products(high, low, table_high[...], table_low[...], ((1,), (1,)))

    scene_ref[0] = jnp.zeros_like(scene_ref[0])
    scene_ref[1] = jnp.zeros_like(scene_ref[1])

    def backward(j, carry):
        for top in range(0, rows, ROWS):
            at = pl.ds(pl.multiple_of(j * rows + top, ROWS), ROWS)
            z = [
                times(
                    tuple(z_ref[d, at, c * lanes : (c + 1) * lanes] for c in range(2)),
                    twiddle_ref[2, d : d + 1, :],
                    twiddle_ref[3, d : d + 1, :],
                )
                for d in range(RADIX)
            ]
            for a, value in enumerate(dft8(z, 1.0)):
                for c in range(2):
                    scene_ref[j + 2, c, top : top + ROWS, a * lanes : (a + 1) * lanes] = value[c]
        return carry

    lax.fori_loop(0, epochs, backward, 0)

    def look(value):
        if plan.planes:
            return sum(value[q * looks : (q + 1) * looks] for q in range(1, LOOK)) + value[:looks]
        return value.reshape(looks, LOOK, value.shape[-1]).sum(axis=1)

    def interfere(j, carry):
        for a in range(RADIX):
            columns = pl.ds(a * lanes, lanes)
            later = (scene_ref[j + 2, 0, :, columns], scene_ref[j + 2, 1, :, columns])
            for lag in (1, 2):
                earlier = (
                    scene_ref[j + 2 - lag, 0, :, columns],
                    scene_ref[j + 2 - lag, 1, :, columns],
                )
                real = earlier[0] * later[0] + earlier[1] * later[1]
                imag = earlier[1] * later[0] - earlier[0] * later[1]
                product_ref[j, lag - 1, 0, :, columns] = look(real)
                product_ref[j, lag - 1, 1, :, columns] = look(imag)
        return carry

    lax.fori_loop(0, epochs, interfere, 0)

    total = epochs * 4 * looks
    products = product_ref[...].reshape(total, plan.azimuth)
    high, low = two_parts(products)
    weights = sum_ref[...]
    looked = []
    for start in range(0, plan.azimuth, weights.shape[0]):
        columns = slice(start, start + weights.shape[0])
        looked.append(
            jnp.dot(high[:, columns], weights, preferred_element_type=jnp.float32)
            + jnp.dot(low[:, columns], weights, preferred_element_type=jnp.float32)
        )
    looked = jnp.concatenate(looked, axis=1)
    looked = looked.reshape(epochs, 2, 2, looks, plan.azimuth_looks)
    if final:
        looked_ref, slope_ref = scratch[13:]
        for at, before in enumerate(before_ref):
            looked_ref[:, :, :, at * looks : (at + 1) * looks, :] = before[...]
        looked_ref[:, :, :, part * looks :, :] = looked
        slopes_and_sums(plan, weight_ref, looked_ref, halo_ref, out_ref, slope_ref)
    else:
        out_ref[...] = looked


def slopes_and_sums(plan, weight_ref, looked_ref, halo_ref, out_ref, slope_ref):
    epochs = plan.epochs
    columns = plan.azimuth_looks
    inner = lax.broadcasted_iota(jnp.int32, (plan.looks * plan.parts, columns), 1) < columns - 1

    def slopes(at, carry):
        j, lag = at // 2, at % 2
        real, imag = looked_ref[j, lag, 0], looked_ref[j, lag, 1]
        next_real = pltpu.roll(real, columns - 1, 1)
        next_imag = pltpu.roll(imag, columns - 1, 1)
        slope_ref[at, 0] = jnp.where(inner, next_imag * real - next_real * imag, 0.0)
        next_real = jnp.concatenate([real[1:], halo_ref[j, lag, 0]], axis=0)
        next_imag = jnp.concatenate([imag[1:], halo_ref[j, lag, 1]], axis=0)
        slope_ref[at, 1] = next_imag * real - next_real * imag
        return carry

    lax.fori_loop(0, 2 * epochs, slopes, 0)

    def epoch(e, carry):
        total = weight_ref[e, 0] * slope_ref[0]
        for at in range(1, 2 * epochs):
            total = total + weight_ref[e, at] * slope_ref[at]
        out_ref[e] = total
        return carry

    lax.fori_loop(0, epochs, epoch, 0)


def focus_tables(plan):
    lanes = plan.lanes
    index = np.arange(lanes)
    table = host_parts(real_form(*unit(index[:, None] * index[None, :], lanes, -1.0)))
    cosine, sine = unit(np.arange(RADIX)[:, None] * index[None, :], plan.azimuth, -1.0)
    twiddles = np.stack([cosine, sine, cosine / plan.azimuth, -sine / plan.azimuth])
    sums = np.arange(plan.azimuth // 2)[:, None] // LOOK == np.arange(plan.azimuth_looks // 2)[None, :]
    return table + (twiddles.astype(np.float32), (sums / LOOK).astype(ml_dtypes.bfloat16))


def focus(plan, part, fields, spectrum, finish=None):
    lanes = plan.lanes
    total = plan.epochs * plan.rows
    tables = focus_tables(plan)
    whole = pl.BlockSpec(memory_space=pltpu.VMEM)
    looked = (plan.epochs, 2, 2, plan.looks, plan.azimuth_looks)
    gradients = (plan.epochs, 2, plan.looks * plan.parts, plan.azimuth_looks)
    operands = [*fields, spectrum, *tables]
    in_specs = [pl.BlockSpec(memory_space=pltpu.HBM)] * len(operands)
    blocks = plan.azimuth // fields[0].shape[-1]
    before = ()
    scratch = [
        pltpu.VMEM((blocks, plan.epochs) + fields[0].shape[-3:], jnp.float32),
        pltpu.VMEM(spectrum.shape[1:], jnp.float32),
        *[pltpu.VMEM(table.shape, table.dtype) for table in tables],
        pltpu.VMEM((RADIX, total, 2 * lanes), jnp.bfloat16),
        pltpu.VMEM((RADIX, total, 2 * lanes), jnp.bfloat16),
        pltpu.VMEM((RADIX, total, 2 * lanes), jnp.float32),
        pltpu.VMEM((plan.epochs + 2, 2, plan.rows, plan.azimuth), jnp.float32),
        pltpu.VMEM((plan.epochs, 2, 2, plan.looks, plan.azimuth), jnp.float32),
        pltpu.SemaphoreType.DMA((plan.epochs, blocks)),
        pltpu.SemaphoreType.DMA((5,)),
    ]
    shape = looked
    if finish is not None:
        weights, before, halo = finish
        shape = gradients
        operands += [weights, *before, halo]
        in_specs += [pl.BlockSpec(memory_space=pltpu.SMEM)] + [whole] * (len(before) + 1)
        scratch += [
            pltpu.VMEM((plan.epochs, 2, 2, plan.looks * plan.parts, plan.azimuth_looks), jnp.float32),
            pltpu.VMEM((2 * plan.epochs,) + gradients[1:], jnp.float32),
        ]

    def kernel(*refs):
        some, refs = refs[: len(fields)], refs[len(fields) :]

        relative = len(some) > 1
        own = (lax.axis_index("acq"), lax.axis_index("strip")) if relative else (0, 0)

        def field_at(j, at):
            return some[at].at[j] if relative else some[0].at[at, j]

        if finish is None:
            focus_kernel(plan, part, False, field_at, own, *refs)
        else:
            count = len(before)
            focus_kernel(
                plan, part, True, field_at, own, *refs[:6], refs[6 : 6 + count], *refs[6 + count :]
            )

    return pl.pallas_call(
        kernel,
        out_shape=jax.ShapeDtypeStruct(shape, jnp.float32),
        in_specs=in_specs,
        out_specs=whole,
        scratch_shapes=scratch,
        compiler_params=pltpu.CompilerParams(vmem_limit_bytes=VMEM_BYTES),
        cost_estimate=pl.CostEstimate(
            flops=2 * 6 * RADIX * total * 4 * lanes * lanes,
            bytes_accessed=4 * blocks * fields[0].size + 4 * 1024 * 1024,
            transcendentals=0,
        ),
        name="azimuth_focus",
    )(*operands)


def slope_kernel(plan, weight_ref, looked_ref, halo_ref, out_ref, slope_ref):
    slopes_and_sums(plan, weight_ref, looked_ref, halo_ref, out_ref, slope_ref)


def slopes_to_epochs(plan, weights, looked, halo):
    whole = pl.BlockSpec(memory_space=pltpu.VMEM)
    looks = plan.looks * plan.parts
    return pl.pallas_call(
        functools.partial(slope_kernel, plan),
        out_shape=jax.ShapeDtypeStruct(
            (plan.epochs, 2, looks, plan.azimuth_looks), jnp.float32
        ),
        in_specs=[pl.BlockSpec(memory_space=pltpu.SMEM), whole, whole],
        out_specs=whole,
        scratch_shapes=[
            pltpu.VMEM((2 * plan.epochs, 2, looks, plan.azimuth_looks), jnp.float32)
        ],
        compiler_params=pltpu.CompilerParams(vmem_limit_bytes=VMEM_BYTES),
        cost_estimate=pl.CostEstimate(
            flops=8 * looked.size * plan.epochs, bytes_accessed=5 * looked.size, transcendentals=0
        ),
        name="slopes_to_epochs",
    )(weights, looked, halo)


def own_filter(plan, azimuth_filter):
    start = lax.axis_index("acq") * plan.owned
    own = lax.dynamic_slice_in_dim(azimuth_filter, start, plan.owned, axis=2)
    own = own.reshape(2, plan.lanes, RADIX, plan.parts, plan.looks, LOOK)
    order = (3, 0, 2, 5, 4, 1) if plan.planes else (3, 0, 2, 4, 5, 1)
    return own.transpose(order).reshape(plan.parts, 2, RADIX, plan.rows, plan.lanes)


def exchange_all(plan, block):
    shape = block.shape
    block = block.reshape((plan.strips * plan.epochs,) + shape[2:])
    received = lax.all_to_all(block, OWNERS, split_axis=0, concat_axis=0, tiled=True)
    join = max(1, plan.lanes // plan.pulses)
    received = received.reshape((plan.strips // join, join) + shape[1:])
    if join > 1:
        received = received.transpose(0, 2, 3, 4, 1, 5)
    return received.reshape(plan.strips // join, plan.epochs, 2, plan.rows, join * plan.pulses)


def partners(slots, axis):
    size = lax.axis_size(axis)
    routes = [[(i, i ^ k) for i in range(size)] for k in range(size)]
    return slots[:1] + [lax.ppermute(slots[k], axis, routes[k]) for k in range(1, size)]


def all_weights(pair_mask, inversion):
    lags = jnp.array([1, 2], dtype=jnp.int32)
    usable = pair_mask[0].astype(jnp.float32) * (lax.axis_index("acq") >= lags).astype(jnp.float32)
    weights = lax.all_gather(inversion[:, 0, :] * usable[None, :], "acq", axis=1, tiled=False)
    return weights.reshape(weights.shape[0], -1)


def per_device(raw_echoes, range_filter, azimuth_filter, pair_mask, inversion):
    strips, epochs = lax.axis_size("strip"), lax.axis_size("acq")
    plan = Plan(strips, epochs, raw_echoes.shape[2], raw_echoes.shape[3])

    raw = raw_echoes[0]
    block = compress(plan, 0, False, range_filter, raw)
    if plan.parts > 1:
        range_filter, block = lax.optimization_barrier((range_filter, block))
        other = compress(plan, 1, True, range_filter, raw)
        other, azimuth_filter, pair_mask, inversion = lax.optimization_barrier(
            (other, azimuth_filter, pair_mask, inversion)
        )
    weights = all_weights(pair_mask, inversion)
    spectrum = own_filter(plan, azimuth_filter)
    field = exchange_all(plan, block)
    if plan.parts > 1:
        other = partners([other[k] for k in range(epochs)], "acq")
        *other, weights, spectrum = lax.optimization_barrier((*other, weights, spectrum))
        slots = [jnp.stack([part[k] for part in other]) for k in range(strips)]
        slots = partners(slots, "strip")
    before = [focus(plan, 0, [field], spectrum)]

    owners = strips * epochs
    device = [i % epochs * strips + i // epochs for i in range(owners)]
    halo = lax.ppermute(
        before[0][:, :, :, :1, :],
        ("acq", "strip"),
        [(device[i], device[i - 1]) for i in range(1, owners)],
    )
    if plan.parts > 1:
        gradients = focus(plan, 1, slots, spectrum, (weights, before, halo))
    else:
        gradients = slopes_to_epochs(plan, weights, before[0], halo)
    gathered = lax.all_to_all(gradients, "acq", split_axis=0, concat_axis=0, tiled=True)
    gathered = gathered.reshape(epochs, 2, plan.looks * plan.parts, plan.azimuth_looks)
    return gathered.swapaxes(0, 1).reshape(1, 2, -1, plan.azimuth_looks)


def solution(mesh):
    return jax.shard_map(
        per_device,
        mesh=mesh,
        in_specs=(
            P("acq", None, "strip", None),
            P(),
            P(None, None, "strip"),
            P("acq", None),
            P(None, "acq", None),
        ),
        out_specs=P("acq", None, "strip", None),
        check_vma=False,
    )
```

```python
import functools
import math

import jax
import jax.numpy as jnp
import ml_dtypes
import numpy as np
from jax import lax
from jax.experimental import pallas as pl
from jax.experimental.pallas import tpu as pltpu
from jax.sharding import PartitionSpec as P

LOOK = 4
RADIX = 8
ROWS = 8
RANGE_VMEM = 60 * 1024 * 1024
FOCUS_VMEM = 28 * 1024 * 1024
OWNERS = ("strip", "acq")


def add(left, right):
    return (left[0] + right[0], left[1] + right[1])


def sub(left, right):
    return (left[0] - right[0], left[1] - right[1])


def times(value, cosine, sine):
    return (value[0] * cosine - value[1] * sine, value[0] * sine + value[1] * cosine)


def turn(value, sign):
    if sign > 0:
        return (-value[1], value[0])
    return (value[1], -value[0])


def dft4(x0, x1, x2, x3, sign):
    a, b = add(x0, x2), sub(x0, x2)
    c, d = add(x1, x3), turn(sub(x1, x3), sign)
    return [add(a, c), add(b, d), sub(a, c), sub(b, d)]


def dft8(x, sign):
    even = dft4(x[0], x[2], x[4], x[6], sign)
    odd = dft4(x[1], x[3], x[5], x[7], sign)
    half = math.sqrt(0.5)
    o1, o3 = odd[1], odd[3]
    t1 = add(o1, turn(o1, sign))
    t3 = sub(turn(o3, sign), o3)
    odd = [
        odd[0],
        (t1[0] * half, t1[1] * half),
        turn(odd[2], sign),
        (t3[0] * half, t3[1] * half),
    ]
    return [add(e, o) for e, o in zip(even, odd)] + [sub(e, o) for e, o in zip(even, odd)]


def two_parts(value):
    high = value.astype(jnp.bfloat16)
    low = (value - high.astype(jnp.float32)).astype(jnp.bfloat16)
    return high, low


def three_products(left_high, left_low, right_high, right_low, contract):
    def product(left, right):
        return lax.dot_general(
            left, right, (contract, ((), ())), preferred_element_type=jnp.float32
        )

    return (
        product(left_high, right_high)
        + product(left_high, right_low)
        + product(left_low, right_high)
    )


def host_parts(table):
    table = np.asarray(table, np.float64)
    high = table.astype(np.float32).astype(ml_dtypes.bfloat16)
    low = (table - high.astype(np.float64)).astype(np.float32).astype(ml_dtypes.bfloat16)
    return high, low


def unit(exponent, size, sign):
    angle = sign * 2.0 * np.pi / size * (exponent % size)
    return np.cos(angle), np.sin(angle)


def real_form(cosine, sine):
    top = np.concatenate([cosine, sine], axis=-1)
    bottom = np.concatenate([-sine, cosine], axis=-1)
    return np.concatenate([top, bottom], axis=-2)


class Plan:
    def __init__(self, strips, epochs, pulses, samples):
        self.strips, self.epochs = strips, epochs
        self.pulses, self.samples = pulses, samples
        self.azimuth = pulses * strips
        self.base = samples // RADIX
        self.owned = samples // (strips * epochs)
        even = all(size & (size - 1) == 0 for size in (strips, epochs))
        self.parts = 2 if even and self.owned % (2 * LOOK * ROWS) == 0 else 1
        self.rows = self.owned // self.parts
        self.looks = self.rows // LOOK
        self.planes = self.looks % ROWS == 0
        self.blocks = self.base // self.owned
        self.lanes = self.azimuth // RADIX
        self.azimuth_looks = self.azimuth // LOOK

    def tile_shift(self, part, block, tile):
        start = block * self.owned + part * self.rows
        if self.planes:
            plane, look = divmod(tile * ROWS, self.looks)
            return start + LOOK * look + plane
        return start + tile * ROWS

    def tile_stride(self):
        return LOOK if self.planes else 1


def lag_tables(plan):
    base, samples = plan.base, plan.samples
    index = np.arange(base)
    table = host_parts(
        np.concatenate(unit(index[:, None] * index[None, :], samples, -1.0), axis=1) / samples
    )
    block = np.arange(RADIX)[:, None]
    turns = np.stack(
        unit(block * index[None, :], RADIX, -1.0)
        + tuple(np.broadcast_to(part, (RADIX, base)) for part in unit(block, RADIX, 1.0))
    )
    return table + (turns.astype(np.float32),)


def lag_vectors(plan, filter_ref, table_high, table_low, turn_ref):
    base = plan.base
    lane = lax.broadcasted_iota(jnp.int32, (RADIX, base), 1)
    chosen = lane % RADIX == lax.broadcasted_iota(jnp.int32, (RADIX, base), 0)
    rows = []
    for c in range(2):
        for e in range(RADIX):
            block = jnp.broadcast_to(filter_ref[c : c + 1, e * base : (e + 1) * base], (RADIX, base))
            rows.append(jnp.where(chosen, block, 0.0))
    high, low = two_parts(jnp.concatenate(rows, axis=0))
    sums = three_products(high, low, table_high[...], table_low[...], ((1,), (0,)))
    real, imag = 0.0, 0.0
    for e in range(RADIX):
        by_real = sums[e * RADIX : (e + 1) * RADIX]
        by_imag = sums[(RADIX + e) * RADIX : (RADIX + e + 1) * RADIX]
        part_real = by_real[:, :base] - by_imag[:, base:]
        part_imag = by_real[:, base:] + by_imag[:, :base]
        cosine, sine = turn_ref[0, e : e + 1, :], turn_ref[1, e : e + 1, :]
        real = real + part_real * cosine - part_imag * sine
        imag = imag + part_real * sine + part_imag * cosine
    cosine, sine = turn_ref[2], turn_ref[3]
    return (
        jnp.concatenate([real, real * cosine - imag * sine], axis=1),
        jnp.concatenate([imag, real * sine + imag * cosine], axis=1),
    )


def fetch(copies):
    for copy in copies:
        copy.start()
    return copies


def compress_kernel(
    plan, part, relative, filter_ref, high_any, low_any, turn_any, raw_ref, out_ref,
    table_high, table_low, turn_ref, raw, t_high, t_low, y_high, y_low, z_ref, sems, table_sems,
):
    base, blocks = plan.base, plan.blocks
    tiles = plan.rows // ROWS
    chunk = blocks * plan.rows
    pieces = sems.shape[0]
    piece = plan.pulses // pieces

    def raw_copy(at):
        rows = pl.ds(at * piece, piece)
        return pltpu.make_async_copy(raw_ref.at[:, rows, :], raw.at[:, rows, :], sems.at[at])

    tables = fetch(
        [
            pltpu.make_async_copy(source, target, table_sems.at[at])
            for at, (source, target) in enumerate(
                ((high_any, table_high), (low_any, table_low), (turn_any, turn_ref))
            )
        ]
    )
    fetch([raw_copy(at) for at in range(pieces)])
    def spread_pulses(at, carry):
        rows = pl.ds(pl.multiple_of(at * 2 * ROWS, 2 * ROWS), 2 * ROWS)
        x = [
            tuple(raw[c, rows, a * base : (a + 1) * base] for c in range(2))
            for a in range(RADIX)
        ]
        for d, value in enumerate(dft8(x, -1.0)):
            for c in range(2):
                high, low = two_parts(value[c])
                y_high[d, rows, c * base : (c + 1) * base] = high
                y_low[d, rows, c * base : (c + 1) * base] = low
        return carry

    steps = piece // (2 * ROWS)
    for at in range(pieces):
        raw_copy(at).wait()
        lax.fori_loop(at * steps, (at + 1) * steps, spread_pulses, 0)

    for copy in tables:
        copy.wait()
    lags = lag_vectors(plan, filter_ref, table_high, table_low, turn_ref)

    for d in range(RADIX):
        spread = [
            pltpu.roll(
                jnp.broadcast_to(lag[d : d + 1, :], (ROWS, 2 * base)),
                0,
                1,
                stride=plan.tile_stride(),
                stride_axis=0,
            )
            for lag in lags
        ]
        for pair in range(blocks * tiles // 2):
            real, imag = [], []
            for at in (2 * pair, 2 * pair + 1):
                shift = plan.tile_shift(part, at // tiles, at % tiles)
                real.append(pltpu.roll(spread[0], shift, 1)[:, :base])
                imag.append(pltpu.roll(spread[1], shift, 1)[:, :base])
            real_high, real_low = two_parts(jnp.concatenate(real, axis=0))
            imag_high, imag_low = two_parts(jnp.concatenate(imag, axis=0))
            top = pl.ds(pair * 2 * ROWS, 2 * ROWS)
            bottom = pl.ds(chunk + pair * 2 * ROWS, 2 * ROWS)
            t_high[d, top, :base] = real_high
            t_high[d, top, base:] = -imag_high
            t_high[d, bottom, :base] = imag_high
            t_high[d, bottom, base:] = real_high
            t_low[d, top, :base] = real_low
            t_low[d, top, base:] = -imag_low
            t_low[d, bottom, :base] = imag_low
            t_low[d, bottom, base:] = real_low
        z_ref[d] = three_products(t_high[d], t_low[d], y_high[d], y_low[d], ((1,), (1,)))

    for block in range(blocks):
        for tile in range(tiles):
            top = (block * tiles + tile) * ROWS
            z = [
                (z_ref[d, top : top + ROWS, :], z_ref[d, chunk + top : chunk + top + ROWS, :])
                for d in range(RADIX)
            ]
            for a, value in enumerate(dft8(z, 1.0)):
                for c in range(2):
                    strip, owner = divmod(a * blocks + block, plan.epochs)
                    rows = slice(tile * ROWS, (tile + 1) * ROWS)
                    if relative:
                        place = owner ^ lax.axis_index("acq"), strip ^ lax.axis_index("strip")
                    else:
                        place = strip, owner
                    out_ref[place[0], place[1], c, rows, :] = value[c]


def compress(plan, part, relative, range_filter, raw):
    chunk = plan.blocks * plan.rows
    whole = pl.BlockSpec(memory_space=pltpu.VMEM)
    bytes_moved = 4 * (raw.size + raw.size // plan.parts)
    tables = lag_tables(plan)
    places = (plan.strips, plan.epochs)
    places = places[::-1] if relative else places
    return pl.pallas_call(
        functools.partial(compress_kernel, plan, part, relative),
        out_shape=jax.ShapeDtypeStruct(places + (2, plan.rows, plan.pulses), jnp.float32),
        in_specs=[whole] + [pl.BlockSpec(memory_space=pltpu.HBM)] * 4,
        out_specs=whole,
        scratch_shapes=[
            *[pltpu.VMEM(table.shape, table.dtype) for table in tables],
            pltpu.VMEM(raw.shape, jnp.float32),
            pltpu.VMEM((RADIX, 2 * chunk, 2 * plan.base), jnp.bfloat16),
            pltpu.VMEM((RADIX, 2 * chunk, 2 * plan.base), jnp.bfloat16),
            pltpu.VMEM((RADIX, plan.pulses, 2 * plan.base), jnp.bfloat16),
            pltpu.VMEM((RADIX, plan.pulses, 2 * plan.base), jnp.bfloat16),
            pltpu.VMEM((RADIX, 2 * chunk, plan.pulses), jnp.float32),
            pltpu.SemaphoreType.DMA((4,)),
            pltpu.SemaphoreType.DMA((3,)),
        ],
        compiler_params=pltpu.CompilerParams(vmem_limit_bytes=RANGE_VMEM),
        cost_estimate=pl.CostEstimate(
            flops=6 * RADIX * 4 * chunk * plan.base * plan.pulses,
            bytes_accessed=bytes_moved,
            transcendentals=0,
        ),
        name="range_compress",
    )(range_filter, *tables, raw)


def focus_kernel(plan, part, final, field_at, own, *refs):
    filter_any, high_any, low_any, twiddle_any, sum_any = refs[:5]
    if final:
        weight_ref, before_ref, halo_ref, out_ref = refs[5:9]
    else:
        (out_ref,) = refs[5:6]
    scratch = refs[9 if final else 6 :]
    (
        field_ref, filter_ref, table_high, table_low, twiddle_ref, sum_ref,
        y_high, y_low, z_ref, scene_ref, product_ref, field_sems, table_sems,
    ) = scratch[:13]
    rows, lanes, epochs, looks = plan.rows, plan.lanes, plan.epochs, plan.looks
    step = 2 * ROWS
    group = max(1, step // rows)
    per_block = field_ref.shape[-1] // lanes

    def field_copies(slot):
        return [
            pltpu.make_async_copy(
                field_at(slot, at), field_ref.at[at ^ own[1], slot ^ own[0]], field_sems.at[slot, at]
            )
            for at in range(field_ref.shape[0])
        ]

    tables = [
        pltpu.make_async_copy(source, target, table_sems.at[at])
        for at, (source, target) in enumerate(
            (
                (twiddle_any, twiddle_ref),
                (high_any, table_high),
                (low_any, table_low),
                (filter_any.at[part], filter_ref),
                (sum_any, sum_ref),
            )
        )
    ]
    fetch(tables[:1])
    for j in range(epochs):
        fetch(field_copies(j))
    fetch(tables[1:])
    tables[0].wait()

    def rows_of(strip, j, c, top, start):
        some = [
            field_ref[strip, j + g, c, top : top + min(rows, step), start : start + lanes]
            for g in range(group)
        ]
        return some[0] if group == 1 else jnp.concatenate(some, axis=0)

    def forward(at, carry):
        for g in range(group):
            for block in range(field_ref.shape[0]):
                place = field_ref.at[block, at * group + g]
                pltpu.make_async_copy(place, place, field_sems.at[at * group + g, block]).wait()
        j = at * group ^ own[0]
        for top in range(0, rows, step):
            x = []
            for a in range(RADIX):
                strip, start = a // per_block, a % per_block * lanes
                x.append(tuple(rows_of(strip, j, c, top, start) for c in range(2)))
            at = pl.ds(pl.multiple_of(j * rows + top, step), step)
            for d, value in enumerate(dft8(x, -1.0)):
                if d > 0:
                    value = times(value, twiddle_ref[0, d : d + 1, :], twiddle_ref[1, d : d + 1, :])
                for c in range(2):
                    high, low = two_parts(value[c])
                    y_high[d, at, c * lanes : (c + 1) * lanes] = high
                    y_low[d, at, c * lanes : (c + 1) * lanes] = low
        return carry

    lax.fori_loop(0, epochs // group, forward, 0)
    for copy in tables[1:]:
        copy.wait()

    for d in range(RADIX):
        spectrum = three_products(
            y_high[d], y_low[d], table_high[...], table_low[...], ((1,), (0,))
        )
        spectrum = spectrum.reshape(epochs, rows, 2 * lanes)
        real, imag = spectrum[:, :, :lanes], spectrum[:, :, lanes:]
        by_real, by_imag = filter_ref[0, d][None], filter_ref[1, d][None]
        spectrum = jnp.concatenate(
            [real * by_real - imag * by_imag, real * by_imag + imag * by_real], axis=2
        )
        high, low = two_parts(spectrum.reshape(epochs * rows, 2 * lanes))
        z_ref[d] = three_products(high, low, table_high[...], table_low[...], ((1,), (1,)))

    scene_ref[0] = jnp.zeros_like(scene_ref[0])
    scene_ref[1] = jnp.zeros_like(scene_ref[1])

    def backward(j, carry):
        for top in range(0, rows, ROWS):
            at = pl.ds(pl.multiple_of(j * rows + top, ROWS), ROWS)
            z = [
                times(
                    tuple(z_ref[d, at, c * lanes : (c + 1) * lanes] for c in range(2)),
                    twiddle_ref[2, d : d + 1, :],
                    twiddle_ref[3, d : d + 1, :],
                )
                for d in range(RADIX)
            ]
            for a, value in enumerate(dft8(z, 1.0)):
                for c in range(2):
                    scene_ref[j + 2, c, top : top + ROWS, a * lanes : (a + 1) * lanes] = value[c]
        return carry

    lax.fori_loop(0, epochs, backward, 0)

    def look(value):
        if plan.planes:
            return sum(value[q * looks : (q + 1) * looks] for q in range(1, LOOK)) + value[:looks]
        return value.reshape(looks, LOOK, value.shape[-1]).sum(axis=1)

    def interfere(j, carry):
        for a in range(RADIX):
            columns = pl.ds(a * lanes, lanes)
            later = (scene_ref[j + 2, 0, :, columns], scene_ref[j + 2, 1, :, columns])
            for lag in (1, 2):
                earlier = (
                    scene_ref[j + 2 - lag, 0, :, columns],
                    scene_ref[j + 2 - lag, 1, :, columns],
                )
                real = earlier[0] * later[0] + earlier[1] * later[1]
                imag = earlier[1] * later[0] - earlier[0] * later[1]
                product_ref[j, lag - 1, 0, :, columns] = look(real)
                product_ref[j, lag - 1, 1, :, columns] = look(imag)
        return carry

    lax.fori_loop(0, epochs, interfere, 0)

    total = epochs * 4 * looks
    products = product_ref[...].reshape(total, plan.azimuth)
    high, low = two_parts(products)
    weights = sum_ref[...]
    looked = []
    for start in range(0, plan.azimuth, weights.shape[0]):
        columns = slice(start, start + weights.shape[0])
        looked.append(
            jnp.dot(high[:, columns], weights, preferred_element_type=jnp.float32)
            + jnp.dot(low[:, columns], weights, preferred_element_type=jnp.float32)
        )
    looked = jnp.concatenate(looked, axis=1)
    looked = looked.reshape(epochs, 2, 2, looks, plan.azimuth_looks)
    if final:
        looked_ref, slope_ref = scratch[13:]
        for at, before in enumerate(before_ref):
            looked_ref[:, :, :, at * looks : (at + 1) * looks, :] = before[...]
        looked_ref[:, :, :, part * looks :, :] = looked
        slopes_and_sums(plan, weight_ref, looked_ref, halo_ref, out_ref, slope_ref)
    else:
        out_ref[...] = looked


def slopes_and_sums(plan, weight_ref, looked_ref, halo_ref, out_ref, slope_ref):
    epochs = plan.epochs
    columns = plan.azimuth_looks
    inner = lax.broadcasted_iota(jnp.int32, (plan.looks * plan.parts, columns), 1) < columns - 1

    def slopes(at, carry):
        j, lag = at // 2, at % 2
        real, imag = looked_ref[j, lag, 0], looked_ref[j, lag, 1]
        next_real = pltpu.roll(real, columns - 1, 1)
        next_imag = pltpu.roll(imag, columns - 1, 1)
        slope_ref[at, 0] = jnp.where(inner, next_imag * real - next_real * imag, 0.0)
        next_real = jnp.concatenate([real[1:], halo_ref[j, lag, 0]], axis=0)
        next_imag = jnp.concatenate([imag[1:], halo_ref[j, lag, 1]], axis=0)
        slope_ref[at, 1] = next_imag * real - next_real * imag
        return carry

    lax.fori_loop(0, 2 * epochs, slopes, 0)

    def epoch(e, carry):
        total = weight_ref[e, 0] * slope_ref[0]
        for at in range(1, 2 * epochs):
            total = total + weight_ref[e, at] * slope_ref[at]
        out_ref[e] = total
        return carry

    lax.fori_loop(0, epochs, epoch, 0)


def focus_tables(plan):
    lanes = plan.lanes
    index = np.arange(lanes)
    table = host_parts(real_form(*unit(index[:, None] * index[None, :], lanes, -1.0)))
    cosine, sine = unit(np.arange(RADIX)[:, None] * index[None, :], plan.azimuth, -1.0)
    twiddles = np.stack([cosine, sine, cosine / plan.azimuth, -sine / plan.azimuth])
    sums = np.arange(plan.azimuth // 2)[:, None] // LOOK == np.arange(plan.azimuth_looks // 2)[None, :]
    return table + (twiddles.astype(np.float32), (sums / LOOK).astype(ml_dtypes.bfloat16))


def focus(plan, part, fields, spectrum, finish=None):
    lanes = plan.lanes
    total = plan.epochs * plan.rows
    tables = focus_tables(plan)
    whole = pl.BlockSpec(memory_space=pltpu.VMEM)
    looked = (plan.epochs, 2, 2, plan.looks, plan.azimuth_looks)
    gradients = (plan.epochs, 2, plan.looks * plan.parts, plan.azimuth_looks)
    operands = [*fields, spectrum, *tables]
    in_specs = [pl.BlockSpec(memory_space=pltpu.HBM)] * len(operands)
    blocks = plan.azimuth // fields[0].shape[-1]
    before = ()
    scratch = [
        pltpu.VMEM((blocks, plan.epochs) + fields[0].shape[-3:], jnp.float32),
        pltpu.VMEM(spectrum.shape[1:], jnp.float32),
        *[pltpu.VMEM(table.shape, table.dtype) for table in tables],
        pltpu.VMEM((RADIX, total, 2 * lanes), jnp.bfloat16),
        pltpu.VMEM((RADIX, total, 2 * lanes), jnp.bfloat16),
        pltpu.VMEM((RADIX, total, 2 * lanes), jnp.float32),
        pltpu.VMEM((plan.epochs + 2, 2, plan.rows, plan.azimuth), jnp.float32),
        pltpu.VMEM((plan.epochs, 2, 2, plan.looks, plan.azimuth), jnp.float32),
        pltpu.SemaphoreType.DMA((plan.epochs, blocks)),
        pltpu.SemaphoreType.DMA((5,)),
    ]
    shape = looked
    if finish is not None:
        weights, before, halo = finish
        shape = gradients
        operands += [weights, *before, halo]
        in_specs += [pl.BlockSpec(memory_space=pltpu.SMEM)] + [whole] * (len(before) + 1)
        scratch += [
            pltpu.VMEM((plan.epochs, 2, 2, plan.looks * plan.parts, plan.azimuth_looks), jnp.float32),
            pltpu.VMEM((2 * plan.epochs,) + gradients[1:], jnp.float32),
        ]

    def kernel(*refs):
        some, refs = refs[: len(fields)], refs[len(fields) :]

        relative = len(some) > 1
        own = (lax.axis_index("acq"), lax.axis_index("strip")) if relative else (0, 0)

        def field_at(j, at):
            if not relative:
                return some[0].at[at, j]
            return some[j].at[0] if at == 0 else some[plan.epochs + at - 1].at[j]

        if finish is None:
            focus_kernel(plan, part, False, field_at, own, *refs)
        else:
            count = len(before)
            focus_kernel(
                plan, part, True, field_at, own, *refs[:6], refs[6 : 6 + count], *refs[6 + count :]
            )

    return pl.pallas_call(
        kernel,
        out_shape=jax.ShapeDtypeStruct(shape, jnp.float32),
        in_specs=in_specs,
        out_specs=whole,
        scratch_shapes=scratch,
        compiler_params=pltpu.CompilerParams(vmem_limit_bytes=FOCUS_VMEM),
        cost_estimate=pl.CostEstimate(
            flops=2 * 6 * RADIX * total * 4 * lanes * lanes,
            bytes_accessed=4 * total * 2 * plan.azimuth + 4 * 1024 * 1024,
            transcendentals=0,
        ),
        name="azimuth_focus",
    )(*operands)


def slope_kernel(plan, weight_ref, looked_ref, halo_ref, out_ref, slope_ref):
    slopes_and_sums(plan, weight_ref, looked_ref, halo_ref, out_ref, slope_ref)


def slopes_to_epochs(plan, weights, looked, halo):
    whole = pl.BlockSpec(memory_space=pltpu.VMEM)
    looks = plan.looks * plan.parts
    return pl.pallas_call(
        functools.partial(slope_kernel, plan),
        out_shape=jax.ShapeDtypeStruct(
            (plan.epochs, 2, looks, plan.azimuth_looks), jnp.float32
        ),
        in_specs=[pl.BlockSpec(memory_space=pltpu.SMEM), whole, whole],
        out_specs=whole,
        scratch_shapes=[
            pltpu.VMEM((2 * plan.epochs, 2, looks, plan.azimuth_looks), jnp.float32)
        ],
        compiler_params=pltpu.CompilerParams(vmem_limit_bytes=FOCUS_VMEM),
        cost_estimate=pl.CostEstimate(
            flops=8 * looked.size * plan.epochs, bytes_accessed=5 * looked.size, transcendentals=0
        ),
        name="slopes_to_epochs",
    )(weights, looked, halo)


def own_filter(plan, azimuth_filter):
    start = lax.axis_index("acq") * plan.owned
    own = lax.dynamic_slice_in_dim(azimuth_filter, start, plan.owned, axis=2)
    own = own.reshape(2, plan.lanes, RADIX, plan.parts, plan.looks, LOOK)
    order = (3, 0, 2, 5, 4, 1) if plan.planes else (3, 0, 2, 4, 5, 1)
    return own.transpose(order).reshape(plan.parts, 2, RADIX, plan.rows, plan.lanes)


def exchange_all(plan, block):
    shape = block.shape
    block = block.reshape((plan.strips * plan.epochs,) + shape[2:])
    received = lax.all_to_all(block, OWNERS, split_axis=0, concat_axis=0, tiled=True)
    join = max(1, plan.lanes // plan.pulses)
    received = received.reshape((plan.strips // join, join) + shape[1:])
    if join > 1:
        received = received.transpose(0, 2, 3, 4, 1, 5)
    return received.reshape(plan.strips // join, plan.epochs, 2, plan.rows, join * plan.pulses)


def partners(slots, axis, first=0):
    size = lax.axis_size(axis)
    moved = []
    for k, slot in enumerate(slots, first):
        moved.append(slot if k == 0 else lax.ppermute(slot, axis, [(i, i ^ k) for i in range(size)]))
    return moved


def regroup(plan, others):
    far = range(1, plan.strips)

    def kernel(*refs):
        ins, outs, sems = refs[: plan.epochs], refs[plan.epochs : -1], refs[-1]
        copies = fetch(
            [
                pltpu.make_async_copy(ins[m].at[k], outs[k - 1].at[m], sems.at[m, k])
                for k in far
                for m in range(plan.epochs)
            ]
        )
        for copy in copies:
            copy.wait()

    shape = jax.ShapeDtypeStruct((plan.epochs,) + others[0].shape[1:], jnp.float32)
    place = pl.BlockSpec(memory_space=pltpu.HBM)
    return pl.pallas_call(
        kernel,
        out_shape=[shape for _ in far],
        in_specs=[place] * plan.epochs,
        out_specs=[place for _ in far],
        scratch_shapes=[pltpu.SemaphoreType.DMA((plan.epochs, plan.strips))],
        name="regroup",
    )(*others)


def all_weights(pair_mask, inversion):
    lags = jnp.array([1, 2], dtype=jnp.int32)
    usable = pair_mask[0].astype(jnp.float32) * (lax.axis_index("acq") >= lags).astype(jnp.float32)
    weights = lax.all_gather(inversion[:, 0, :] * usable[None, :], "acq", axis=1, tiled=False)
    return weights.reshape(weights.shape[0], -1)


def per_device(raw_echoes, range_filter, azimuth_filter, pair_mask, inversion):
    strips, epochs = lax.axis_size("strip"), lax.axis_size("acq")
    plan = Plan(strips, epochs, raw_echoes.shape[2], raw_echoes.shape[3])

    raw = raw_echoes[0]
    block = compress(plan, 0, False, range_filter, raw)
    if plan.parts > 1:
        range_filter, block = lax.optimization_barrier((range_filter, block))
        other = compress(plan, 1, True, range_filter, raw)
        other, azimuth_filter = lax.optimization_barrier((other, azimuth_filter))
    spectrum = own_filter(plan, azimuth_filter)
    field = exchange_all(plan, block)
    if plan.parts > 1:
        other = partners([other[k] for k in range(epochs)], "acq")
        *other, spectrum = lax.optimization_barrier((*other, spectrum))
        slots = partners(regroup(plan, other), "strip", 1)
    before = [focus(plan, 0, [field], spectrum)]
    before[0], pair_mask, inversion = lax.optimization_barrier((before[0], pair_mask, inversion))
    weights = all_weights(pair_mask, inversion)

    owners = strips * epochs
    device = [i % epochs * strips + i // epochs for i in range(owners)]
    halo = lax.ppermute(
        before[0][:, :, :, :1, :],
        ("acq", "strip"),
        [(device[i], device[i - 1]) for i in range(1, owners)],
    )
    if plan.parts > 1:
        gradients = focus(plan, 1, other + slots, spectrum, (weights, before, halo))
    else:
        gradients = slopes_to_epochs(plan, weights, before[0], halo)
    gathered = lax.all_to_all(gradients, "acq", split_axis=0, concat_axis=0, tiled=True)
    gathered = gathered.reshape(epochs, 2, plan.looks * plan.parts, plan.azimuth_looks)
    return gathered.swapaxes(0, 1).reshape(1, 2, -1, plan.azimuth_looks)


def solution(mesh):
    return jax.shard_map(
        per_device,
        mesh=mesh,
        in_specs=(
            P("acq", None, "strip", None),
            P(),
            P(None, None, "strip"),
            P("acq", None),
            P(None, "acq", None),
        ),
        out_specs=P("acq", None, "strip", None),
        check_vma=False,
    )
```

```python
import functools
import math

import jax
import jax.numpy as jnp
import ml_dtypes
import numpy as np
from jax import lax
from jax.experimental import pallas as pl
from jax.experimental.pallas import tpu as pltpu
from jax.sharding import PartitionSpec as P

LOOK = 4
RADIX = 8
ROWS = 8
RANGE_VMEM = 60 * 1024 * 1024
LAYOUT_VMEM = 8 * 1024 * 1024
FOCUS_VMEM = 60 * 1024 * 1024
OWNERS = ("strip", "acq")


def add(left, right):
    return (left[0] + right[0], left[1] + right[1])


def sub(left, right):
    return (left[0] - right[0], left[1] - right[1])


def times(value, cosine, sine):
    return (value[0] * cosine - value[1] * sine, value[0] * sine + value[1] * cosine)


def turn(value, sign):
    if sign > 0:
        return (-value[1], value[0])
    return (value[1], -value[0])


def dft4(x0, x1, x2, x3, sign):
    a, b = add(x0, x2), sub(x0, x2)
    c, d = add(x1, x3), turn(sub(x1, x3), sign)
    return [add(a, c), add(b, d), sub(a, c), sub(b, d)]


def dft8(x, sign):
    even = dft4(x[0], x[2], x[4], x[6], sign)
    odd = dft4(x[1], x[3], x[5], x[7], sign)
    half = math.sqrt(0.5)
    o1, o3 = odd[1], odd[3]
    t1 = add(o1, turn(o1, sign))
    t3 = sub(turn(o3, sign), o3)
    odd = [
        odd[0],
        (t1[0] * half, t1[1] * half),
        turn(odd[2], sign),
        (t3[0] * half, t3[1] * half),
    ]
    return [add(e, o) for e, o in zip(even, odd)] + [sub(e, o) for e, o in zip(even, odd)]


def two_parts(value):
    high = value.astype(jnp.bfloat16)
    low = (value - high.astype(jnp.float32)).astype(jnp.bfloat16)
    return high, low


def three_products(left_high, left_low, right_high, right_low, contract):
    def product(left, right):
        return lax.dot_general(
            left, right, (contract, ((), ())), preferred_element_type=jnp.float32
        )

    return (
        product(left_high, right_high)
        + product(left_high, right_low)
        + product(left_low, right_high)
    )


def host_parts(table):
    table = np.asarray(table, np.float64)
    high = table.astype(np.float32).astype(ml_dtypes.bfloat16)
    low = (table - high.astype(np.float64)).astype(np.float32).astype(ml_dtypes.bfloat16)
    return high, low


def unit(exponent, size, sign):
    angle = sign * 2.0 * np.pi / size * (exponent % size)
    return np.cos(angle), np.sin(angle)


def real_form(cosine, sine):
    top = np.concatenate([cosine, sine], axis=-1)
    bottom = np.concatenate([-sine, cosine], axis=-1)
    return np.concatenate([top, bottom], axis=-2)


class Plan:
    def __init__(self, strips, epochs, pulses, samples):
        self.strips, self.epochs = strips, epochs
        self.pulses, self.samples = pulses, samples
        self.azimuth = pulses * strips
        self.base = samples // RADIX
        self.owned = samples // (strips * epochs)
        even = all(size & (size - 1) == 0 for size in (strips, epochs))
        self.parts = 2 if even and self.owned in (64, 128) else 1
        self.rows = self.owned // self.parts
        self.looks = self.rows // LOOK
        self.planes = self.looks % ROWS == 0
        self.blocks = self.base // self.owned
        self.lanes = self.azimuth // RADIX
        self.azimuth_looks = self.azimuth // LOOK

    def tile_shift(self, part, block, tile):
        start = block * self.owned + part * self.rows
        if self.planes:
            plane, look = divmod(tile * ROWS, self.looks)
            return start + LOOK * look + plane
        return start + tile * ROWS

    def tile_stride(self):
        return LOOK if self.planes else 1


def lag_tables(plan):
    base, samples = plan.base, plan.samples
    index = np.arange(base)
    table = host_parts(
        np.concatenate(unit(index[:, None] * index[None, :], samples, -1.0), axis=1) / samples
    )
    block = np.arange(RADIX)[:, None]
    turns = np.stack(
        unit(block * index[None, :], RADIX, -1.0)
        + tuple(np.broadcast_to(part, (RADIX, base)) for part in unit(block, RADIX, 1.0))
    )
    return table + (turns.astype(np.float32),)


def lag_vectors(plan, filter_ref, table_high, table_low, turn_ref):
    base = plan.base
    lane = lax.broadcasted_iota(jnp.int32, (RADIX, base), 1)
    chosen = lane % RADIX == lax.broadcasted_iota(jnp.int32, (RADIX, base), 0)
    rows = []
    for c in range(2):
        for e in range(RADIX):
            block = jnp.broadcast_to(filter_ref[c : c + 1, e * base : (e + 1) * base], (RADIX, base))
            rows.append(jnp.where(chosen, block, 0.0))
    high, low = two_parts(jnp.concatenate(rows, axis=0))
    sums = three_products(high, low, table_high[...], table_low[...], ((1,), (0,)))
    real, imag = 0.0, 0.0
    for e in range(RADIX):
        by_real = sums[e * RADIX : (e + 1) * RADIX]
        by_imag = sums[(RADIX + e) * RADIX : (RADIX + e + 1) * RADIX]
        part_real = by_real[:, :base] - by_imag[:, base:]
        part_imag = by_real[:, base:] + by_imag[:, :base]
        cosine, sine = turn_ref[0, e : e + 1, :], turn_ref[1, e : e + 1, :]
        real = real + part_real * cosine - part_imag * sine
        imag = imag + part_real * sine + part_imag * cosine
    cosine, sine = turn_ref[2], turn_ref[3]
    return (
        jnp.concatenate([real, real * cosine - imag * sine], axis=1),
        jnp.concatenate([imag, real * sine + imag * cosine], axis=1),
    )


def fetch(copies):
    for copy in copies:
        copy.start()
    return copies


def compress_kernel(
    plan, part, relative, filter_ref, high_any, low_any, turn_any, raw_ref, *refs
):
    outs = refs[: plan.epochs if relative else 1]
    (
        table_high, table_low, turn_ref, raw, t_high, t_low, y_high, y_low, z_ref, sems, table_sems,
    ) = refs[len(outs) :][:11]
    out_ref = refs[-2] if relative else outs[0]
    base, blocks = plan.base, plan.blocks
    tiles = plan.rows // ROWS
    chunk = blocks * plan.rows
    pieces = sems.shape[0]
    piece = plan.pulses // pieces

    def raw_copy(at):
        rows = pl.ds(at * piece, piece)
        return pltpu.make_async_copy(raw_ref.at[:, rows, :], raw.at[:, rows, :], sems.at[at])

    tables = fetch(
        [
            pltpu.make_async_copy(source, target, table_sems.at[at])
            for at, (source, target) in enumerate(
                ((high_any, table_high), (low_any, table_low), (turn_any, turn_ref))
            )
        ]
    )
    fetch([raw_copy(at) for at in range(pieces)])
    def spread_pulses(at, carry):
        rows = pl.ds(pl.multiple_of(at * 2 * ROWS, 2 * ROWS), 2 * ROWS)
        x = [
            tuple(raw[c, rows, a * base : (a + 1) * base] for c in range(2))
            for a in range(RADIX)
        ]
        for d, value in enumerate(dft8(x, -1.0)):
            for c in range(2):
                high, low = two_parts(value[c])
                y_high[d, rows, c * base : (c + 1) * base] = high
                y_low[d, rows, c * base : (c + 1) * base] = low
        return carry

    steps = piece // (2 * ROWS)
    for at in range(pieces):
        raw_copy(at).wait()
        lax.fori_loop(at * steps, (at + 1) * steps, spread_pulses, 0)

    for copy in tables:
        copy.wait()
    lags = lag_vectors(plan, filter_ref, table_high, table_low, turn_ref)

    for d in range(RADIX):
        spread = [
            pltpu.roll(
                jnp.broadcast_to(lag[d : d + 1, :], (ROWS, 2 * base)),
                0,
                1,
                stride=plan.tile_stride(),
                stride_axis=0,
            )
            for lag in lags
        ]
        for pair in range(blocks * tiles // 2):
            real, imag = [], []
            for at in (2 * pair, 2 * pair + 1):
                shift = plan.tile_shift(part, at // tiles, at % tiles)
                real.append(pltpu.roll(spread[0], shift, 1)[:, :base])
                imag.append(pltpu.roll(spread[1], shift, 1)[:, :base])
            real_high, real_low = two_parts(jnp.concatenate(real, axis=0))
            imag_high, imag_low = two_parts(jnp.concatenate(imag, axis=0))
            top = pl.ds(pair * 2 * ROWS, 2 * ROWS)
            bottom = pl.ds(chunk + pair * 2 * ROWS, 2 * ROWS)
            t_high[d, top, :base] = real_high
            t_high[d, top, base:] = -imag_high
            t_high[d, bottom, :base] = imag_high
            t_high[d, bottom, base:] = real_high
            t_low[d, top, :base] = real_low
            t_low[d, top, base:] = -imag_low
            t_low[d, bottom, :base] = imag_low
            t_low[d, bottom, base:] = real_low
        z_ref[d] = three_products(t_high[d], t_low[d], y_high[d], y_low[d], ((1,), (1,)))

    for block in range(blocks):
        for tile in range(tiles):
            top = (block * tiles + tile) * ROWS
            z = [
                (z_ref[d, top : top + ROWS, :], z_ref[d, chunk + top : chunk + top + ROWS, :])
                for d in range(RADIX)
            ]
            for a, value in enumerate(dft8(z, 1.0)):
                for c in range(2):
                    strip, owner = divmod(a * blocks + block, plan.epochs)
                    rows = slice(tile * ROWS, (tile + 1) * ROWS)
                    if relative:
                        place = owner ^ lax.axis_index("acq"), strip ^ lax.axis_index("strip")
                    else:
                        place = strip, owner
                    out_ref[place[0], place[1], c, rows, :] = value[c]
    if relative:
        copies = fetch(
            [
                pltpu.make_async_copy(out_ref.at[m], out, refs[-1].at[m])
                for m, out in enumerate(outs)
            ]
        )
        for copy in copies:
            copy.wait()


def compress(plan, part, relative, range_filter, raw):
    chunk = plan.blocks * plan.rows
    whole = pl.BlockSpec(memory_space=pltpu.VMEM)
    bytes_moved = 4 * (raw.size + raw.size // plan.parts)
    tables = lag_tables(plan)
    slab = (2, plan.rows, plan.pulses)
    shape = (plan.strips,) + (slab if relative else (plan.epochs,) + slab)
    scratch, out_specs = [], whole
    if relative:
        out_specs = [pl.BlockSpec(memory_space=pltpu.HBM)] * plan.epochs
        scratch = [
            pltpu.VMEM((plan.epochs,) + shape, jnp.float32),
            pltpu.SemaphoreType.DMA((plan.epochs,)),
        ]
    shape = jax.ShapeDtypeStruct(shape, jnp.float32)
    return pl.pallas_call(
        functools.partial(compress_kernel, plan, part, relative),
        out_shape=[shape] * plan.epochs if relative else shape,
        in_specs=[whole] + [pl.BlockSpec(memory_space=pltpu.HBM)] * 4,
        out_specs=out_specs,
        scratch_shapes=[
            *[pltpu.VMEM(table.shape, table.dtype) for table in tables],
            pltpu.VMEM(raw.shape, jnp.float32),
            pltpu.VMEM((RADIX, 2 * chunk, 2 * plan.base), jnp.bfloat16),
            pltpu.VMEM((RADIX, 2 * chunk, 2 * plan.base), jnp.bfloat16),
            pltpu.VMEM((RADIX, plan.pulses, 2 * plan.base), jnp.bfloat16),
            pltpu.VMEM((RADIX, plan.pulses, 2 * plan.base), jnp.bfloat16),
            pltpu.VMEM((RADIX, 2 * chunk, plan.pulses), jnp.float32),
            pltpu.SemaphoreType.DMA((4,)),
            pltpu.SemaphoreType.DMA((3,)),
            *scratch,
        ],
        compiler_params=pltpu.CompilerParams(vmem_limit_bytes=RANGE_VMEM),
        cost_estimate=pl.CostEstimate(
            flops=6 * RADIX * 4 * chunk * plan.base * plan.pulses,
            bytes_accessed=bytes_moved,
            transcendentals=0,
        ),
        name="range_compress",
    )(range_filter, *tables, raw)


def focus_kernel(plan, part, final, field_at, own, *refs):
    filter_any, high_any, low_any, twiddle_any, sum_any = refs[:5]
    if final:
        weight_ref, before_any, halo_any, out_ref = refs[5:9]
    else:
        (out_ref,) = refs[5:6]
    scratch = refs[9 if final else 6 :]
    (
        field_ref, filter_ref, table_high, table_low, twiddle_ref, sum_ref,
        y_high, y_low, z_ref, scene_ref, product_ref, field_sems, table_sems,
    ) = scratch[:13]
    rows, lanes, epochs, looks = plan.rows, plan.lanes, plan.epochs, plan.looks
    step = 2 * ROWS
    group = max(1, step // rows)
    per_block = field_ref.shape[-1] // lanes

    half = epochs // 2
    fields = [
        [
            pltpu.make_async_copy(
                field_at(at).at[pl.ds(side * half, half)],
                field_ref.at[at, pl.ds(side * half, half)],
                field_sems.at[at, side],
            )
            for at in range(field_ref.shape[0])
        ]
        for side in range(2)
    ]
    tables = [
        pltpu.make_async_copy(source, target, table_sems.at[at])
        for at, (source, target) in enumerate(
            (
                (twiddle_any, twiddle_ref),
                (high_any, table_high),
                (low_any, table_low),
                (filter_any.at[part], filter_ref),
                (sum_any, sum_ref),
            )
        )
    ]
    fetch(tables[:1])
    for copies in fields:
        fetch(copies)
    fetch(tables[1:])
    if final:
        looked_ref, slope_ref, halo_ref, late_sems = scratch[13:]
        late = [
            pltpu.make_async_copy(
                before, looked_ref.at[:, :, :, pl.ds(at * looks, looks), :], late_sems.at[at]
            )
            for at, before in enumerate(before_any)
        ]
        late = fetch(late + [pltpu.make_async_copy(halo_any, halo_ref, late_sems.at[part])])
    tables[0].wait()

    def rows_of(strip, slot, c, top, start):
        some = [
            field_ref[strip, slot + g, c, top : top + min(rows, step), start : start + lanes]
            for g in range(group)
        ]
        return some[0] if group == 1 else jnp.concatenate(some, axis=0)

    def forward(at, carry):
        slot = at * group
        j = slot ^ own[0]
        for top in range(0, rows, step):
            x = []
            for a in range(RADIX):
                strip, start = a // per_block, a % per_block * lanes
                x.append(tuple(rows_of(strip ^ own[1], slot, c, top, start) for c in range(2)))
            at = pl.ds(pl.multiple_of(j * rows + top, step), step)
            for d, value in enumerate(dft8(x, -1.0)):
                if d > 0:
                    value = times(value, twiddle_ref[0, d : d + 1, :], twiddle_ref[1, d : d + 1, :])
                for c in range(2):
                    high, low = two_parts(value[c])
                    y_high[d, at, c * lanes : (c + 1) * lanes] = high
                    y_low[d, at, c * lanes : (c + 1) * lanes] = low
        return carry

    for side, copies in enumerate(fields):
        for copy in copies:
            copy.wait()
        lax.fori_loop(side * half // group, (side + 1) * half // group, forward, 0)
    for copy in tables[1:]:
        copy.wait()

    for d in range(RADIX):
        spectrum = three_products(
            y_high[d], y_low[d], table_high[...], table_low[...], ((1,), (0,))
        )
        spectrum = spectrum.reshape(epochs, rows, 2 * lanes)
        real, imag = spectrum[:, :, :lanes], spectrum[:, :, lanes:]
        by_real, by_imag = filter_ref[0, d][None], filter_ref[1, d][None]
        spectrum = jnp.concatenate(
            [real * by_real - imag * by_imag, real * by_imag + imag * by_real], axis=2
        )
        high, low = two_parts(spectrum.reshape(epochs * rows, 2 * lanes))
        z_ref[d] = three_products(high, low, table_high[...], table_low[...], ((1,), (1,)))

    scene_ref[0] = jnp.zeros_like(scene_ref[0])
    scene_ref[1] = jnp.zeros_like(scene_ref[1])

    def backward(j, carry):
        for top in range(0, rows, ROWS):
            at = pl.ds(pl.multiple_of(j * rows + top, ROWS), ROWS)
            z = [
                times(
                    tuple(z_ref[d, at, c * lanes : (c + 1) * lanes] for c in range(2)),
                    twiddle_ref[2, d : d + 1, :],
                    twiddle_ref[3, d : d + 1, :],
                )
                for d in range(RADIX)
            ]
            for a, value in enumerate(dft8(z, 1.0)):
                for c in range(2):
                    scene_ref[j + 2, c, top : top + ROWS, a * lanes : (a + 1) * lanes] = value[c]
        return carry

    lax.fori_loop(0, epochs, backward, 0)

    def look(value):
        if plan.planes:
            return sum(value[q * looks : (q + 1) * looks] for q in range(1, LOOK)) + value[:looks]
        return value.reshape(looks, LOOK, value.shape[-1]).sum(axis=1)

    def interfere(j, carry):
        for a in range(RADIX):
            columns = pl.ds(a * lanes, lanes)
            later = (scene_ref[j + 2, 0, :, columns], scene_ref[j + 2, 1, :, columns])
            for lag in (1, 2):
                earlier = (
                    scene_ref[j + 2 - lag, 0, :, columns],
                    scene_ref[j + 2 - lag, 1, :, columns],
                )
                real = earlier[0] * later[0] + earlier[1] * later[1]
                imag = earlier[1] * later[0] - earlier[0] * later[1]
                product_ref[j, lag - 1, 0, :, columns] = look(real)
                product_ref[j, lag - 1, 1, :, columns] = look(imag)
        return carry

    lax.fori_loop(0, epochs, interfere, 0)

    total = epochs * 4 * looks
    products = product_ref[...].reshape(total, plan.azimuth)
    high, low = two_parts(products)
    weights = sum_ref[...]
    looked = []
    for start in range(0, plan.azimuth, weights.shape[0]):
        columns = slice(start, start + weights.shape[0])
        looked.append(
            jnp.dot(high[:, columns], weights, preferred_element_type=jnp.float32)
            + jnp.dot(low[:, columns], weights, preferred_element_type=jnp.float32)
        )
    looked = jnp.concatenate(looked, axis=1)
    looked = looked.reshape(epochs, 2, 2, looks, plan.azimuth_looks)
    if final:
        for copy in late:
            copy.wait()
        looked_ref[:, :, :, part * looks :, :] = looked
        slopes_and_sums(plan, weight_ref, looked_ref, halo_ref, out_ref, slope_ref)
    else:
        out_ref[...] = looked


def slopes_and_sums(plan, weight_ref, looked_ref, halo_ref, out_ref, slope_ref):
    epochs = plan.epochs
    columns = plan.azimuth_looks
    inner = lax.broadcasted_iota(jnp.int32, (plan.looks * plan.parts, columns), 1) < columns - 1

    def slopes(at, carry):
        j, lag = at // 2, at % 2
        real, imag = looked_ref[j, lag, 0], looked_ref[j, lag, 1]
        next_real = pltpu.roll(real, columns - 1, 1)
        next_imag = pltpu.roll(imag, columns - 1, 1)
        slope_ref[at, 0] = jnp.where(inner, next_imag * real - next_real * imag, 0.0)
        next_real = jnp.concatenate([real[1:], halo_ref[j, lag, 0]], axis=0)
        next_imag = jnp.concatenate([imag[1:], halo_ref[j, lag, 1]], axis=0)
        slope_ref[at, 1] = next_imag * real - next_real * imag
        return carry

    lax.fori_loop(0, 2 * epochs, slopes, 0)

    def epoch(e, carry):
        total = weight_ref[e, 0] * slope_ref[0]
        for at in range(1, 2 * epochs):
            total = total + weight_ref[e, at] * slope_ref[at]
        out_ref[e] = total
        return carry

    lax.fori_loop(0, epochs, epoch, 0)


def focus_tables(plan):
    lanes = plan.lanes
    index = np.arange(lanes)
    table = host_parts(real_form(*unit(index[:, None] * index[None, :], lanes, -1.0)))
    cosine, sine = unit(np.arange(RADIX)[:, None] * index[None, :], plan.azimuth, -1.0)
    twiddles = np.stack([cosine, sine, cosine / plan.azimuth, -sine / plan.azimuth])
    sums = np.arange(plan.azimuth // 2)[:, None] // LOOK == np.arange(plan.azimuth_looks // 2)[None, :]
    return table + (twiddles.astype(np.float32), (sums / LOOK).astype(ml_dtypes.bfloat16))


def focus(plan, part, fields, spectrum, finish=None):
    lanes = plan.lanes
    total = plan.epochs * plan.rows
    tables = focus_tables(plan)
    whole = pl.BlockSpec(memory_space=pltpu.VMEM)
    looked = (plan.epochs, 2, 2, plan.looks, plan.azimuth_looks)
    gradients = (plan.epochs, 2, plan.looks * plan.parts, plan.azimuth_looks)
    operands = [*fields, spectrum, *tables]
    in_specs = [pl.BlockSpec(memory_space=pltpu.HBM)] * len(operands)
    blocks = plan.azimuth // fields[0].shape[-1]
    before = ()
    scratch = [
        pltpu.VMEM((blocks, plan.epochs) + fields[0].shape[-3:], jnp.float32),
        pltpu.VMEM(spectrum.shape[1:], jnp.float32),
        *[pltpu.VMEM(table.shape, table.dtype) for table in tables],
        pltpu.VMEM((RADIX, total, 2 * lanes), jnp.bfloat16),
        pltpu.VMEM((RADIX, total, 2 * lanes), jnp.bfloat16),
        pltpu.VMEM((RADIX, total, 2 * lanes), jnp.float32),
        pltpu.VMEM((plan.epochs + 2, 2, plan.rows, plan.azimuth), jnp.float32),
        pltpu.VMEM((plan.epochs, 2, 2, plan.looks, plan.azimuth), jnp.float32),
        pltpu.SemaphoreType.DMA((blocks, 2)),
        pltpu.SemaphoreType.DMA((5,)),
    ]
    shape = looked
    if finish is not None:
        weights, before, halo = finish
        shape = gradients
        operands += [weights, *before, halo]
        in_specs += [pl.BlockSpec(memory_space=pltpu.SMEM)]
        in_specs += [pl.BlockSpec(memory_space=pltpu.HBM)] * (len(before) + 1)
        scratch += [
            pltpu.VMEM((plan.epochs, 2, 2, plan.looks * plan.parts, plan.azimuth_looks), jnp.float32),
            pltpu.VMEM((2 * plan.epochs,) + gradients[1:], jnp.float32),
            pltpu.VMEM(halo.shape, jnp.float32),
            pltpu.SemaphoreType.DMA((plan.parts,)),
        ]

    def kernel(*refs):
        some, refs = refs[: len(fields)], refs[len(fields) :]

        relative = len(some) > 1
        own = (lax.axis_index("acq"), lax.axis_index("strip")) if relative else (0, 0)

        def field_at(at):
            return some[at] if relative else some[0].at[at]

        if finish is None:
            focus_kernel(plan, part, False, field_at, own, *refs)
        else:
            count = len(before)
            focus_kernel(
                plan, part, True, field_at, own, *refs[:6], refs[6 : 6 + count], *refs[6 + count :]
            )

    return pl.pallas_call(
        kernel,
        out_shape=jax.ShapeDtypeStruct(shape, jnp.float32),
        in_specs=in_specs,
        out_specs=whole,
        scratch_shapes=scratch,
        compiler_params=pltpu.CompilerParams(vmem_limit_bytes=FOCUS_VMEM),
        cost_estimate=pl.CostEstimate(
            flops=2 * 6 * RADIX * total * 4 * lanes * lanes,
            bytes_accessed=4 * total * 2 * plan.azimuth + 4 * 1024 * 1024,
            transcendentals=0,
        ),
        name="azimuth_focus",
    )(*operands)


def slope_kernel(plan, weight_ref, looked_ref, halo_ref, out_ref, slope_ref):
    slopes_and_sums(plan, weight_ref, looked_ref, halo_ref, out_ref, slope_ref)


def slopes_to_epochs(plan, weights, looked, halo):
    whole = pl.BlockSpec(memory_space=pltpu.VMEM)
    looks = plan.looks * plan.parts
    return pl.pallas_call(
        functools.partial(slope_kernel, plan),
        out_shape=jax.ShapeDtypeStruct(
            (plan.epochs, 2, looks, plan.azimuth_looks), jnp.float32
        ),
        in_specs=[pl.BlockSpec(memory_space=pltpu.SMEM), whole, whole],
        out_specs=whole,
        scratch_shapes=[
            pltpu.VMEM((2 * plan.epochs, 2, looks, plan.azimuth_looks), jnp.float32)
        ],
        compiler_params=pltpu.CompilerParams(vmem_limit_bytes=FOCUS_VMEM),
        cost_estimate=pl.CostEstimate(
            flops=8 * looked.size * plan.epochs, bytes_accessed=5 * looked.size, transcendentals=0
        ),
        name="slopes_to_epochs",
    )(weights, looked, halo)


def own_filter(plan, azimuth_filter):
    start = lax.axis_index("acq") * plan.owned
    own = lax.dynamic_slice_in_dim(azimuth_filter, start, plan.owned, axis=2)
    own = own.reshape(2, plan.lanes, RADIX, plan.parts, plan.looks, LOOK)
    order = (3, 0, 2, 5, 4, 1) if plan.planes else (3, 0, 2, 4, 5, 1)
    return own.transpose(order).reshape(plan.parts, 2, RADIX, plan.rows, plan.lanes)


def own_filter_kernel(plan, filter_any, out_ref, block_ref, turned_ref, sem):
    width = block_ref.shape[-1]
    acq = lax.axis_index("acq")
    start = acq * plan.owned // width * width
    inside = acq * plan.owned % width
    copy = pltpu.make_async_copy(
        filter_any.at[:, :, pl.ds(pl.multiple_of(start, width), width)], block_ref, sem
    )
    copy.start()
    copy.wait()
    for c in range(2):
        for d in range(RADIX):
            turned_ref[...] = block_ref[c, pl.ds(d, plan.lanes, stride=RADIX), :].T
            for part in range(plan.parts):
                for tile in range(plan.rows // ROWS):
                    row = plan.tile_shift(part, 0, tile)
                    rows = pl.ds(inside + row, ROWS, stride=plan.tile_stride())
                    out_ref[part, c, d, tile * ROWS : (tile + 1) * ROWS, :] = turned_ref[rows, :]


def own_filter_by_kernel(plan, azimuth_filter):
    width = 128
    return pl.pallas_call(
        functools.partial(own_filter_kernel, plan),
        out_shape=jax.ShapeDtypeStruct(
            (plan.parts, 2, RADIX, plan.rows, plan.lanes), jnp.float32
        ),
        in_specs=[pl.BlockSpec(memory_space=pltpu.HBM)],
        out_specs=pl.BlockSpec(memory_space=pltpu.VMEM),
        scratch_shapes=[
            pltpu.VMEM((2, plan.azimuth, width), jnp.float32),
            pltpu.VMEM((width, plan.lanes), jnp.float32),
            pltpu.SemaphoreType.DMA,
        ],
        compiler_params=pltpu.CompilerParams(vmem_limit_bytes=LAYOUT_VMEM),
        cost_estimate=pl.CostEstimate(flops=0, bytes_accessed=1024, transcendentals=0),
        name="own_filter",
    )(azimuth_filter)


def exchange_all(plan, block):
    shape = block.shape
    block = block.reshape((plan.strips * plan.epochs,) + shape[2:])
    received = lax.all_to_all(block, OWNERS, split_axis=0, concat_axis=0, tiled=True)
    join = max(1, plan.lanes // plan.pulses)
    received = received.reshape((plan.strips // join, join) + shape[1:])
    if join > 1:
        received = received.transpose(0, 2, 3, 4, 1, 5)
    return received.reshape(plan.strips // join, plan.epochs, 2, plan.rows, join * plan.pulses)


def partners(slots, axis):
    size = lax.axis_size(axis)
    moved = []
    for k, slot in enumerate(slots):
        moved.append(slot if k == 0 else lax.ppermute(slot, axis, [(i, i ^ k) for i in range(size)]))
    return moved


def regroup(plan, others):
    def kernel(*refs):
        ins, outs = refs[: plan.epochs], refs[plan.epochs : plan.epochs + plan.strips]
        stage, in_sems, out_sems = refs[plan.epochs + plan.strips :]
        inward = fetch(
            [
                pltpu.make_async_copy(ins[m].at[k], stage.at[k, m], in_sems.at[k, m])
                for k in range(plan.strips)
                for m in range(plan.epochs)
            ]
        )
        outward = []
        for k in range(plan.strips):
            for copy in inward[k * plan.epochs : (k + 1) * plan.epochs]:
                copy.wait()
            outward += fetch([pltpu.make_async_copy(stage.at[k], outs[k], out_sems.at[k])])
        for copy in outward:
            copy.wait()

    slab = (plan.epochs,) + others[0].shape[1:]
    place = pl.BlockSpec(memory_space=pltpu.HBM)
    return pl.pallas_call(
        kernel,
        out_shape=[jax.ShapeDtypeStruct(slab, jnp.float32)] * plan.strips,
        in_specs=[place] * plan.epochs,
        out_specs=[place] * plan.strips,
        scratch_shapes=[
            pltpu.VMEM((plan.strips,) + slab, jnp.float32),
            pltpu.SemaphoreType.DMA((plan.strips, plan.epochs)),
            pltpu.SemaphoreType.DMA((plan.strips,)),
        ],
        compiler_params=pltpu.CompilerParams(vmem_limit_bytes=LAYOUT_VMEM),
        cost_estimate=pl.CostEstimate(flops=0, bytes_accessed=1024, transcendentals=0),
        name="regroup",
    )(*others)


def all_weights(pair_mask, inversion):
    lags = jnp.array([1, 2], dtype=jnp.int32)
    usable = pair_mask[0].astype(jnp.float32) * (lax.axis_index("acq") >= lags).astype(jnp.float32)
    weights = lax.all_gather(inversion[:, 0, :] * usable[None, :], "acq", axis=1, tiled=False)
    return weights.reshape(weights.shape[0], -1)


def per_device(raw_echoes, range_filter, azimuth_filter, pair_mask, inversion):
    strips, epochs = lax.axis_size("strip"), lax.axis_size("acq")
    plan = Plan(strips, epochs, raw_echoes.shape[2], raw_echoes.shape[3])

    raw = raw_echoes[0]
    block = compress(plan, 0, False, range_filter, raw)
    if plan.parts > 1:
        range_filter, block = lax.optimization_barrier((range_filter, block))
        other = compress(plan, 1, True, range_filter, raw)
        *other, azimuth_filter = lax.optimization_barrier((*other, azimuth_filter))
        spectrum = own_filter_by_kernel(plan, azimuth_filter)
    else:
        spectrum = own_filter(plan, azimuth_filter)
    field = exchange_all(plan, block)
    if plan.parts > 1:
        other = partners(other, "acq")
        *other, spectrum = lax.optimization_barrier((*other, spectrum))
        slots = partners(regroup(plan, other), "strip")
    before = [focus(plan, 0, [field], spectrum)]
    before[0], pair_mask, inversion = lax.optimization_barrier((before[0], pair_mask, inversion))
    weights = all_weights(pair_mask, inversion)

    owners = strips * epochs
    device = [i % epochs * strips + i // epochs for i in range(owners)]
    halo = lax.ppermute(
        before[0][:, :, :, :1, :],
        ("acq", "strip"),
        [(device[i], device[i - 1]) for i in range(1, owners)],
    )
    if plan.parts > 1:
        gradients = focus(plan, 1, slots, spectrum, (weights, before, halo))
    else:
        gradients = slopes_to_epochs(plan, weights, before[0], halo)
    gathered = lax.all_to_all(gradients, "acq", split_axis=0, concat_axis=0, tiled=True)
    gathered = gathered.reshape(epochs, 2, plan.looks * plan.parts, plan.azimuth_looks)
    return gathered.swapaxes(0, 1).reshape(1, 2, -1, plan.azimuth_looks)


def solution(mesh):
    return jax.shard_map(
        per_device,
        mesh=mesh,
        in_specs=(
            P("acq", None, "strip", None),
            P(),
            P(None, None, "strip"),
            P("acq", None),
            P(None, "acq", None),
        ),
        out_specs=P("acq", None, "strip", None),
        check_vma=False,
    )
```

```python
import functools
import math

import jax
import jax.numpy as jnp
import ml_dtypes
import numpy as np
from jax import lax
from jax.experimental import pallas as pl
from jax.experimental.pallas import tpu as pltpu
from jax.sharding import PartitionSpec as P

LOOK = 4
RADIX = 8
ROWS = 8
RANGE_VMEM = 63 * 1024 * 1024
LAYOUT_VMEM = 8 * 1024 * 1024
FOCUS_VMEM = 32 * 1024 * 1024
OWNERS = ("strip", "acq")


def add(left, right):
    return (left[0] + right[0], left[1] + right[1])


def sub(left, right):
    return (left[0] - right[0], left[1] - right[1])


def times(value, cosine, sine):
    return (value[0] * cosine - value[1] * sine, value[0] * sine + value[1] * cosine)


def turn(value, sign):
    if sign > 0:
        return (-value[1], value[0])
    return (value[1], -value[0])


def dft4(x0, x1, x2, x3, sign):
    a, b = add(x0, x2), sub(x0, x2)
    c, d = add(x1, x3), turn(sub(x1, x3), sign)
    return [add(a, c), add(b, d), sub(a, c), sub(b, d)]


def dft8(x, sign):
    even = dft4(x[0], x[2], x[4], x[6], sign)
    odd = dft4(x[1], x[3], x[5], x[7], sign)
    half = math.sqrt(0.5)
    o1, o3 = odd[1], odd[3]
    t1 = add(o1, turn(o1, sign))
    t3 = sub(turn(o3, sign), o3)
    odd = [
        odd[0],
        (t1[0] * half, t1[1] * half),
        turn(odd[2], sign),
        (t3[0] * half, t3[1] * half),
    ]
    return [add(e, o) for e, o in zip(even, odd)] + [sub(e, o) for e, o in zip(even, odd)]


def two_parts(value):
    high = value.astype(jnp.bfloat16)
    low = (value - high.astype(jnp.float32)).astype(jnp.bfloat16)
    return high, low


def three_products(left_high, left_low, right_high, right_low, contract):
    def product(left, right):
        return lax.dot_general(
            left, right, (contract, ((), ())), preferred_element_type=jnp.float32
        )

    return (
        product(left_high, right_high)
        + product(left_high, right_low)
        + product(left_low, right_high)
    )


def host_parts(table):
    table = np.asarray(table, np.float64)
    high = table.astype(np.float32).astype(ml_dtypes.bfloat16)
    low = (table - high.astype(np.float64)).astype(np.float32).astype(ml_dtypes.bfloat16)
    return high, low


def unit(exponent, size, sign):
    angle = sign * 2.0 * np.pi / size * (exponent % size)
    return np.cos(angle), np.sin(angle)


def real_form(cosine, sine):
    top = np.concatenate([cosine, sine], axis=-1)
    bottom = np.concatenate([-sine, cosine], axis=-1)
    return np.concatenate([top, bottom], axis=-2)


class Plan:
    def __init__(self, strips, epochs, pulses, samples):
        self.strips, self.epochs = strips, epochs
        self.pulses, self.samples = pulses, samples
        self.azimuth = pulses * strips
        self.base = samples // RADIX
        self.owned = samples // (strips * epochs)
        even = strips != epochs and all(size & (size - 1) == 0 for size in (strips, epochs))
        self.parts = 2 if even and self.owned in (64, 128) else 1
        self.rows = self.owned // self.parts
        self.looks = self.rows // LOOK
        self.planes = self.looks % ROWS == 0
        self.blocks = self.base // self.owned
        self.lanes = self.azimuth // RADIX
        self.azimuth_looks = self.azimuth // LOOK

    def tile_shift(self, part, block, tile):
        start = block * self.owned + part * self.rows
        if self.planes:
            plane, look = divmod(tile * ROWS, self.looks)
            return start + LOOK * look + plane
        return start + tile * ROWS

    def tile_stride(self):
        return LOOK if self.planes else 1


def lag_tables(plan):
    base, samples = plan.base, plan.samples
    index = np.arange(base)
    table = host_parts(
        np.concatenate(unit(index[:, None] * index[None, :], samples, -1.0), axis=1) / samples
    )
    block = np.arange(RADIX)[:, None]
    turns = np.stack(
        unit(block * index[None, :], RADIX, -1.0)
        + tuple(np.broadcast_to(part, (RADIX, base)) for part in unit(block, RADIX, 1.0))
    )
    return table + (turns.astype(np.float32),)


def lag_vectors(plan, filter_ref, table_high, table_low, turn_ref):
    base = plan.base
    lane = lax.broadcasted_iota(jnp.int32, (RADIX, base), 1)
    chosen = lane % RADIX == lax.broadcasted_iota(jnp.int32, (RADIX, base), 0)
    rows = []
    for c in range(2):
        for e in range(RADIX):
            block = jnp.broadcast_to(filter_ref[c : c + 1, e * base : (e + 1) * base], (RADIX, base))
            rows.append(jnp.where(chosen, block, 0.0))
    high, low = two_parts(jnp.concatenate(rows, axis=0))
    sums = three_products(high, low, table_high[...], table_low[...], ((1,), (0,)))
    real, imag = 0.0, 0.0
    for e in range(RADIX):
        by_real = sums[e * RADIX : (e + 1) * RADIX]
        by_imag = sums[(RADIX + e) * RADIX : (RADIX + e + 1) * RADIX]
        part_real = by_real[:, :base] - by_imag[:, base:]
        part_imag = by_real[:, base:] + by_imag[:, :base]
        cosine, sine = turn_ref[0, e : e + 1, :], turn_ref[1, e : e + 1, :]
        real = real + part_real * cosine - part_imag * sine
        imag = imag + part_real * sine + part_imag * cosine
    cosine, sine = turn_ref[2], turn_ref[3]
    return (
        jnp.concatenate([real, real * cosine - imag * sine], axis=1),
        jnp.concatenate([imag, real * sine + imag * cosine], axis=1),
    )


def fetch(copies):
    for copy in copies:
        copy.start()
    return copies


def compress_kernel(
    plan, part, form, filter_ref, high_any, low_any, turn_any, raw_ref, *refs
):
    relative = form != "all"
    outs = refs[: {"all": 1, "epochs": plan.epochs, "strips": plan.strips}[form]]
    (
        table_high, table_low, turn_ref, raw, t_high, t_low, y_high, y_low, z_ref, sems, table_sems,
    ) = refs[len(outs) :][:11]
    out_ref = refs[-2] if relative else outs[0]
    base, blocks = plan.base, plan.blocks
    tiles = plan.rows // ROWS
    chunk = blocks * plan.rows
    pieces = sems.shape[0]
    piece = plan.pulses // pieces

    def raw_copy(at):
        rows = pl.ds(at * piece, piece)
        return pltpu.make_async_copy(raw_ref.at[:, rows, :], raw.at[:, rows, :], sems.at[at])

    tables = fetch(
        [
            pltpu.make_async_copy(source, target, table_sems.at[at])
            for at, (source, target) in enumerate(
                ((high_any, table_high), (low_any, table_low), (turn_any, turn_ref))
            )
        ]
    )
    fetch([raw_copy(at) for at in range(pieces)])
    def spread_pulses(at, carry):
        rows = pl.ds(pl.multiple_of(at * 2 * ROWS, 2 * ROWS), 2 * ROWS)
        x = [
            tuple(raw[c, rows, a * base : (a + 1) * base] for c in range(2))
            for a in range(RADIX)
        ]
        for d, value in enumerate(dft8(x, -1.0)):
            for c in range(2):
                high, low = two_parts(value[c])
                y_high[d, rows, c * base : (c + 1) * base] = high
                y_low[d, rows, c * base : (c + 1) * base] = low
        return carry

    steps = piece // (2 * ROWS)
    for at in range(pieces):
        raw_copy(at).wait()
        lax.fori_loop(at * steps, (at + 1) * steps, spread_pulses, 0)

    for copy in tables:
        copy.wait()
    lags = lag_vectors(plan, filter_ref, table_high, table_low, turn_ref)

    for d in range(RADIX):
        spread = [
            pltpu.roll(
                jnp.broadcast_to(lag[d : d + 1, :], (ROWS, 2 * base)),
                0,
                1,
                stride=plan.tile_stride(),
                stride_axis=0,
            )
            for lag in lags
        ]
        for pair in range(blocks * tiles // 2):
            real, imag = [], []
            for at in (2 * pair, 2 * pair + 1):
                shift = plan.tile_shift(part, at // tiles, at % tiles)
                real.append(pltpu.roll(spread[0], shift, 1)[:, :base])
                imag.append(pltpu.roll(spread[1], shift, 1)[:, :base])
            real_high, real_low = two_parts(jnp.concatenate(real, axis=0))
            imag_high, imag_low = two_parts(jnp.concatenate(imag, axis=0))
            top = pl.ds(pair * 2 * ROWS, 2 * ROWS)
            bottom = pl.ds(chunk + pair * 2 * ROWS, 2 * ROWS)
            t_high[d, top, :base] = real_high
            t_high[d, top, base:] = -imag_high
            t_high[d, bottom, :base] = imag_high
            t_high[d, bottom, base:] = real_high
            t_low[d, top, :base] = real_low
            t_low[d, top, base:] = -imag_low
            t_low[d, bottom, :base] = imag_low
            t_low[d, bottom, base:] = real_low
        z_ref[d] = three_products(t_high[d], t_low[d], y_high[d], y_low[d], ((1,), (1,)))

    for block in range(blocks):
        for tile in range(tiles):
            top = (block * tiles + tile) * ROWS
            z = [
                (z_ref[d, top : top + ROWS, :], z_ref[d, chunk + top : chunk + top + ROWS, :])
                for d in range(RADIX)
            ]
            for a, value in enumerate(dft8(z, 1.0)):
                for c in range(2):
                    strip, owner = divmod(a * blocks + block, plan.epochs)
                    rows = slice(tile * ROWS, (tile + 1) * ROWS)
                    if relative:
                        place = owner ^ lax.axis_index("acq"), strip ^ lax.axis_index("strip")
                        place = place if form == "epochs" else place[::-1]
                    else:
                        place = strip, owner
                    out_ref[place[0], place[1], c, rows, :] = value[c]
    if relative:
        copies = fetch(
            [
                pltpu.make_async_copy(out_ref.at[m], out, refs[-1].at[m])
                for m, out in enumerate(outs)
            ]
        )
        for copy in copies:
            copy.wait()


def compress(plan, part, form, range_filter, raw):
    chunk = plan.blocks * plan.rows
    whole = pl.BlockSpec(memory_space=pltpu.VMEM)
    bytes_moved = 4 * (raw.size + raw.size // plan.parts)
    tables = lag_tables(plan)
    slab = (2, plan.rows, plan.pulses)
    scratch, out_specs = [], whole
    shape = jax.ShapeDtypeStruct((plan.strips, plan.epochs) + slab, jnp.float32)
    if form != "all":
        count, inner = plan.epochs, plan.strips
        if form == "strips":
            count, inner = inner, count
        out_specs = [pl.BlockSpec(memory_space=pltpu.HBM)] * count
        scratch = [
            pltpu.VMEM((count, inner) + slab, jnp.float32),
            pltpu.SemaphoreType.DMA((count,)),
        ]
        shape = [jax.ShapeDtypeStruct((inner,) + slab, jnp.float32)] * count
    return pl.pallas_call(
        functools.partial(compress_kernel, plan, part, form),
        out_shape=shape,
        in_specs=[whole] + [pl.BlockSpec(memory_space=pltpu.HBM)] * 4,
        out_specs=out_specs,
        scratch_shapes=[
            *[pltpu.VMEM(table.shape, table.dtype) for table in tables],
            pltpu.VMEM(raw.shape, jnp.float32),
            pltpu.VMEM((RADIX, 2 * chunk, 2 * plan.base), jnp.bfloat16),
            pltpu.VMEM((RADIX, 2 * chunk, 2 * plan.base), jnp.bfloat16),
            pltpu.VMEM((RADIX, plan.pulses, 2 * plan.base), jnp.bfloat16),
            pltpu.VMEM((RADIX, plan.pulses, 2 * plan.base), jnp.bfloat16),
            pltpu.VMEM((RADIX, 2 * chunk, plan.pulses), jnp.float32),
            pltpu.SemaphoreType.DMA((4,)),
            pltpu.SemaphoreType.DMA((3,)),
            *scratch,
        ],
        compiler_params=pltpu.CompilerParams(vmem_limit_bytes=RANGE_VMEM),
        cost_estimate=pl.CostEstimate(
            flops=6 * RADIX * 4 * chunk * plan.base * plan.pulses,
            bytes_accessed=bytes_moved,
            transcendentals=0,
        ),
        name="range_compress",
    )(range_filter, *tables, raw)


def focus_kernel(plan, part, final, field_at, own, *refs):
    filter_any, high_any, low_any, twiddle_any, sum_any = refs[:5]
    if final:
        weight_ref, before_any, halo_any, out_ref = refs[5:9]
    else:
        (out_ref,) = refs[5:6]
    scratch = refs[9 if final else 6 :]
    (
        field_ref, filter_ref, table_high, table_low, twiddle_ref, sum_ref,
        y_high, y_low, z_ref, scene_ref, product_ref, field_sems, table_sems,
    ) = scratch[:13]
    rows, lanes, epochs, looks = plan.rows, plan.lanes, plan.epochs, plan.looks
    step = 2 * ROWS
    group = max(1, step // rows)
    per_block = field_ref.shape[-1] // lanes

    half = epochs // 2
    fields = [
        [
            pltpu.make_async_copy(source, field_ref.at[place], field_sems.at[side, at])
            for at, (source, place) in enumerate(field_at(pl.ds(side * half, half)))
        ]
        for side in range(2)
    ]
    tables = [
        pltpu.make_async_copy(source, target, table_sems.at[at])
        for at, (source, target) in enumerate(
            (
                (twiddle_any, twiddle_ref),
                (high_any, table_high),
                (low_any, table_low),
                (filter_any.at[part], filter_ref),
                (sum_any, sum_ref),
            )
        )
    ]
    fetch(tables[:1])
    for copies in fields:
        fetch(copies)
    fetch(tables[1:])
    if final:
        looked_ref, slope_ref, halo_ref, late_sems = scratch[13:]
        late = [
            pltpu.make_async_copy(
                before, looked_ref.at[:, :, :, pl.ds(at * looks, looks), :], late_sems.at[at]
            )
            for at, before in enumerate(before_any)
        ]
        late = fetch(late + [pltpu.make_async_copy(halo_any, halo_ref, late_sems.at[part])])
    tables[0].wait()

    def rows_of(strip, slot, c, top, start):
        some = [
            field_ref[strip, slot + g, c, top : top + min(rows, step), start : start + lanes]
            for g in range(group)
        ]
        return some[0] if group == 1 else jnp.concatenate(some, axis=0)

    def forward(at, carry):
        slot = at * group
        j = slot ^ own[0]
        for top in range(0, rows, step):
            x = []
            for a in range(RADIX):
                strip, start = a // per_block, a % per_block * lanes
                x.append(tuple(rows_of(strip ^ own[1], slot, c, top, start) for c in range(2)))
            at = pl.ds(pl.multiple_of(j * rows + top, step), step)
            for d, value in enumerate(dft8(x, -1.0)):
                if d > 0:
                    value = times(value, twiddle_ref[0, d : d + 1, :], twiddle_ref[1, d : d + 1, :])
                for c in range(2):
                    high, low = two_parts(value[c])
                    y_high[d, at, c * lanes : (c + 1) * lanes] = high
                    y_low[d, at, c * lanes : (c + 1) * lanes] = low
        return carry

    for side, copies in enumerate(fields):
        for copy in copies:
            copy.wait()
        lax.fori_loop(side * half // group, (side + 1) * half // group, forward, 0)
    for copy in tables[1:]:
        copy.wait()

    for d in range(RADIX):
        spectrum = three_products(
            y_high[d], y_low[d], table_high[...], table_low[...], ((1,), (0,))
        )
        spectrum = spectrum.reshape(epochs, rows, 2 * lanes)
        real, imag = spectrum[:, :, :lanes], spectrum[:, :, lanes:]
        by_real, by_imag = filter_ref[0, d][None], filter_ref[1, d][None]
        spectrum = jnp.concatenate(
            [real * by_real - imag * by_imag, real * by_imag + imag * by_real], axis=2
        )
        high, low = two_parts(spectrum.reshape(epochs * rows, 2 * lanes))
        z_ref[d] = three_products(high, low, table_high[...], table_low[...], ((1,), (1,)))

    scene_ref[0] = jnp.zeros_like(scene_ref[0])
    scene_ref[1] = jnp.zeros_like(scene_ref[1])

    def backward(j, carry):
        for top in range(0, rows, ROWS):
            at = pl.ds(pl.multiple_of(j * rows + top, ROWS), ROWS)
            z = [
                times(
                    tuple(z_ref[d, at, c * lanes : (c + 1) * lanes] for c in range(2)),
                    twiddle_ref[2, d : d + 1, :],
                    twiddle_ref[3, d : d + 1, :],
                )
                for d in range(RADIX)
            ]
            for a, value in enumerate(dft8(z, 1.0)):
                for c in range(2):
                    scene_ref[j + 2, c, top : top + ROWS, a * lanes : (a + 1) * lanes] = value[c]
        return carry

    lax.fori_loop(0, epochs, backward, 0)

    def look(value):
        if plan.planes:
            return sum(value[q * looks : (q + 1) * looks] for q in range(1, LOOK)) + value[:looks]
        return value.reshape(looks, LOOK, value.shape[-1]).sum(axis=1)

    def interfere(j, carry):
        for a in range(RADIX):
            columns = pl.ds(a * lanes, lanes)
            later = (scene_ref[j + 2, 0, :, columns], scene_ref[j + 2, 1, :, columns])
            for lag in (1, 2):
                earlier = (
                    scene_ref[j + 2 - lag, 0, :, columns],
                    scene_ref[j + 2 - lag, 1, :, columns],
                )
                real = earlier[0] * later[0] + earlier[1] * later[1]
                imag = earlier[1] * later[0] - earlier[0] * later[1]
                product_ref[j, lag - 1, 0, :, columns] = look(real)
                product_ref[j, lag - 1, 1, :, columns] = look(imag)
        return carry

    lax.fori_loop(0, epochs, interfere, 0)

    total = epochs * 4 * looks
    products = product_ref[...].reshape(total, plan.azimuth)
    high, low = two_parts(products)
    weights = sum_ref[...]
    looked = []
    for start in range(0, plan.azimuth, weights.shape[0]):
        columns = slice(start, start + weights.shape[0])
        looked.append(
            jnp.dot(high[:, columns], weights, preferred_element_type=jnp.float32)
            + jnp.dot(low[:, columns], weights, preferred_element_type=jnp.float32)
        )
    looked = jnp.concatenate(looked, axis=1)
    looked = looked.reshape(epochs, 2, 2, looks, plan.azimuth_looks)
    if final:
        for copy in late:
            copy.wait()
        looked_ref[:, :, :, part * looks :, :] = looked
        slopes_and_sums(plan, weight_ref, looked_ref, halo_ref, out_ref, slope_ref)
    else:
        out_ref[...] = looked


def slopes_and_sums(plan, weight_ref, looked_ref, halo_ref, out_ref, slope_ref):
    epochs = plan.epochs
    columns = plan.azimuth_looks
    inner = lax.broadcasted_iota(jnp.int32, (plan.looks * plan.parts, columns), 1) < columns - 1

    def slopes(at, carry):
        j, lag = at // 2, at % 2
        real, imag = looked_ref[j, lag, 0], looked_ref[j, lag, 1]
        next_real = pltpu.roll(real, columns - 1, 1)
        next_imag = pltpu.roll(imag, columns - 1, 1)
        slope_ref[at, 0] = jnp.where(inner, next_imag * real - next_real * imag, 0.0)
        next_real = jnp.concatenate([real[1:], halo_ref[j, lag, 0]], axis=0)
        next_imag = jnp.concatenate([imag[1:], halo_ref[j, lag, 1]], axis=0)
        slope_ref[at, 1] = next_imag * real - next_real * imag
        return carry

    lax.fori_loop(0, 2 * epochs, slopes, 0)

    def epoch(e, carry):
        total = weight_ref[e, 0] * slope_ref[0]
        for at in range(1, 2 * epochs):
            total = total + weight_ref[e, at] * slope_ref[at]
        out_ref[e] = total
        return carry

    lax.fori_loop(0, epochs, epoch, 0)


def focus_tables(plan):
    lanes = plan.lanes
    index = np.arange(lanes)
    table = host_parts(real_form(*unit(index[:, None] * index[None, :], lanes, -1.0)))
    cosine, sine = unit(np.arange(RADIX)[:, None] * index[None, :], plan.azimuth, -1.0)
    twiddles = np.stack([cosine, sine, cosine / plan.azimuth, -sine / plan.azimuth])
    sums = np.arange(plan.azimuth // 2)[:, None] // LOOK == np.arange(plan.azimuth_looks // 2)[None, :]
    return table + (twiddles.astype(np.float32), (sums / LOOK).astype(ml_dtypes.bfloat16))


def focus(plan, part, fields, spectrum, finish=None):
    lanes = plan.lanes
    total = plan.epochs * plan.rows
    tables = focus_tables(plan)
    whole = pl.BlockSpec(memory_space=pltpu.VMEM)
    looked = (plan.epochs, 2, 2, plan.looks, plan.azimuth_looks)
    gradients = (plan.epochs, 2, plan.looks * plan.parts, plan.azimuth_looks)
    operands = [*fields, spectrum, *tables]
    in_specs = [pl.BlockSpec(memory_space=pltpu.HBM)] * len(operands)
    assert plan.strips != plan.epochs or len(fields) == 1
    blocks = plan.azimuth // fields[0].shape[-1]
    before = ()
    scratch = [
        pltpu.VMEM((blocks, plan.epochs) + fields[0].shape[-3:], jnp.float32),
        pltpu.VMEM(spectrum.shape[1:], jnp.float32),
        *[pltpu.VMEM(table.shape, table.dtype) for table in tables],
        pltpu.VMEM((RADIX, total, 2 * lanes), jnp.bfloat16),
        pltpu.VMEM((RADIX, total, 2 * lanes), jnp.bfloat16),
        pltpu.VMEM((RADIX, total, 2 * lanes), jnp.float32),
        pltpu.VMEM((plan.epochs + 2, 2, plan.rows, plan.azimuth), jnp.float32),
        pltpu.VMEM((plan.epochs, 2, 2, plan.looks, plan.azimuth), jnp.float32),
        pltpu.SemaphoreType.DMA((2, max(blocks, plan.epochs // 2))),
        pltpu.SemaphoreType.DMA((5,)),
    ]
    shape = looked
    if finish is not None:
        weights, before, halo = finish
        shape = gradients
        operands += [weights, *before, halo]
        in_specs += [pl.BlockSpec(memory_space=pltpu.SMEM)]
        in_specs += [pl.BlockSpec(memory_space=pltpu.HBM)] * (len(before) + 1)
        scratch += [
            pltpu.VMEM((plan.epochs, 2, 2, plan.looks * plan.parts, plan.azimuth_looks), jnp.float32),
            pltpu.VMEM((2 * plan.epochs,) + gradients[1:], jnp.float32),
            pltpu.VMEM(halo.shape, jnp.float32),
            pltpu.SemaphoreType.DMA((plan.parts,)),
        ]

    def kernel(*refs):
        some, refs = refs[: len(fields)], refs[len(fields) :]

        relative = len(some) > 1
        own = (lax.axis_index("acq"), lax.axis_index("strip")) if relative else (0, 0)

        def field_at(some_epochs):
            if not relative:
                return [(some[0].at[at, some_epochs], (at, some_epochs)) for at in range(blocks)]
            if len(some) == plan.strips:
                return [(block.at[some_epochs], (at, some_epochs)) for at, block in enumerate(some)]
            inside = range(some_epochs.start, some_epochs.start + some_epochs.size)
            return [(some[m], (slice(None), m)) for m in inside]

        if finish is None:
            focus_kernel(plan, part, False, field_at, own, *refs)
        else:
            count = len(before)
            focus_kernel(
                plan, part, True, field_at, own, *refs[:6], refs[6 : 6 + count], *refs[6 + count :]
            )

    return pl.pallas_call(
        kernel,
        out_shape=jax.ShapeDtypeStruct(shape, jnp.float32),
        in_specs=in_specs,
        out_specs=whole,
        scratch_shapes=scratch,
        compiler_params=pltpu.CompilerParams(vmem_limit_bytes=FOCUS_VMEM),
        cost_estimate=pl.CostEstimate(
            flops=2 * 6 * RADIX * total * 4 * lanes * lanes,
            bytes_accessed=4 * total * 2 * plan.azimuth + 4 * 1024 * 1024,
            transcendentals=0,
        ),
        name="azimuth_focus",
    )(*operands)


def slope_kernel(plan, weight_ref, looked_ref, halo_ref, out_ref, slope_ref):
    slopes_and_sums(plan, weight_ref, looked_ref, halo_ref, out_ref, slope_ref)


def slopes_to_epochs(plan, weights, looked, halo):
    whole = pl.BlockSpec(memory_space=pltpu.VMEM)
    looks = plan.looks * plan.parts
    return pl.pallas_call(
        functools.partial(slope_kernel, plan),
        out_shape=jax.ShapeDtypeStruct(
            (plan.epochs, 2, looks, plan.azimuth_looks), jnp.float32
        ),
        in_specs=[pl.BlockSpec(memory_space=pltpu.SMEM), whole, whole],
        out_specs=whole,
        scratch_shapes=[
            pltpu.VMEM((2 * plan.epochs, 2, looks, plan.azimuth_looks), jnp.float32)
        ],
        compiler_params=pltpu.CompilerParams(vmem_limit_bytes=FOCUS_VMEM),
        cost_estimate=pl.CostEstimate(
            flops=8 * looked.size * plan.epochs, bytes_accessed=5 * looked.size, transcendentals=0
        ),
        name="slopes_to_epochs",
    )(weights, looked, halo)


def own_filter(plan, azimuth_filter):
    start = lax.axis_index("acq") * plan.owned
    own = lax.dynamic_slice_in_dim(azimuth_filter, start, plan.owned, axis=2)
    own = own.reshape(2, plan.lanes, RADIX, plan.parts, plan.looks, LOOK)
    order = (3, 0, 2, 5, 4, 1) if plan.planes else (3, 0, 2, 4, 5, 1)
    return own.transpose(order).reshape(plan.parts, 2, RADIX, plan.rows, plan.lanes)


def own_filter_kernel(plan, filter_any, out_ref, block_ref, turned_ref, sem):
    width = block_ref.shape[-1]
    acq = lax.axis_index("acq")
    start = acq * plan.owned // width * width
    inside = acq * plan.owned % width
    copy = pltpu.make_async_copy(
        filter_any.at[:, :, pl.ds(pl.multiple_of(start, width), width)], block_ref, sem
    )
    copy.start()
    copy.wait()
    for c in range(2):
        for d in range(RADIX):
            turned_ref[...] = block_ref[c, pl.ds(d, plan.lanes, stride=RADIX), :].T
            for part in range(plan.parts):
                for tile in range(plan.rows // ROWS):
                    row = plan.tile_shift(part, 0, tile)
                    rows = pl.ds(inside + row, ROWS, stride=plan.tile_stride())
                    out_ref[part, c, d, tile * ROWS : (tile + 1) * ROWS, :] = turned_ref[rows, :]


def own_filter_by_kernel(plan, azimuth_filter):
    width = 128
    return pl.pallas_call(
        functools.partial(own_filter_kernel, plan),
        out_shape=jax.ShapeDtypeStruct(
            (plan.parts, 2, RADIX, plan.rows, plan.lanes), jnp.float32
        ),
        in_specs=[pl.BlockSpec(memory_space=pltpu.HBM)],
        out_specs=pl.BlockSpec(memory_space=pltpu.VMEM),
        scratch_shapes=[
            pltpu.VMEM((2, plan.azimuth, width), jnp.float32),
            pltpu.VMEM((width, plan.lanes), jnp.float32),
            pltpu.SemaphoreType.DMA,
        ],
        compiler_params=pltpu.CompilerParams(vmem_limit_bytes=LAYOUT_VMEM),
        cost_estimate=pl.CostEstimate(flops=0, bytes_accessed=1024, transcendentals=0),
        name="own_filter",
    )(azimuth_filter)


def exchange_all(plan, block):
    shape = block.shape
    block = block.reshape((plan.strips * plan.epochs,) + shape[2:])
    received = lax.all_to_all(block, OWNERS, split_axis=0, concat_axis=0, tiled=True)
    join = max(1, plan.lanes // plan.pulses)
    received = received.reshape((plan.strips // join, join) + shape[1:])
    if join > 1:
        received = received.transpose(0, 2, 3, 4, 1, 5)
    return received.reshape(plan.strips // join, plan.epochs, 2, plan.rows, join * plan.pulses)


def partners(slots, axis):
    size = lax.axis_size(axis)
    moved = []
    for k, slot in enumerate(slots):
        moved.append(slot if k == 0 else lax.ppermute(slot, axis, [(i, i ^ k) for i in range(size)]))
    return moved


def regroup(blocks):
    count, inner = len(blocks), blocks[0].shape[0]

    def kernel(*refs):
        ins, outs = refs[:count], refs[count : count + inner]
        stage, in_sems, out_sems = refs[count + inner :]
        inward = [
            fetch(
                [
                    pltpu.make_async_copy(ins[m].at[k], stage.at[k, m], in_sems.at[k, m])
                    for m in range(count)
                ]
            )
            for k in range(inner)
        ]
        outward = []
        for k in range(inner):
            for copy in inward[k]:
                copy.wait()
            outward += fetch([pltpu.make_async_copy(stage.at[k], outs[k], out_sems.at[k])])
        for copy in outward:
            copy.wait()

    slab = (count,) + blocks[0].shape[1:]
    place = pl.BlockSpec(memory_space=pltpu.HBM)
    return pl.pallas_call(
        kernel,
        out_shape=[jax.ShapeDtypeStruct(slab, jnp.float32)] * inner,
        in_specs=[place] * count,
        out_specs=[place] * inner,
        scratch_shapes=[
            pltpu.VMEM((inner,) + slab, jnp.float32),
            pltpu.SemaphoreType.DMA((inner, count)),
            pltpu.SemaphoreType.DMA((inner,)),
        ],
        compiler_params=pltpu.CompilerParams(vmem_limit_bytes=LAYOUT_VMEM),
        cost_estimate=pl.CostEstimate(flops=0, bytes_accessed=1024, transcendentals=0),
        name="regroup",
    )(*blocks)


def all_weights(pair_mask, inversion):
    lags = jnp.array([1, 2], dtype=jnp.int32)
    usable = pair_mask[0].astype(jnp.float32) * (lax.axis_index("acq") >= lags).astype(jnp.float32)
    weights = lax.all_gather(inversion[:, 0, :] * usable[None, :], "acq", axis=1, tiled=False)
    return weights.reshape(weights.shape[0], -1)


def per_device(raw_echoes, range_filter, azimuth_filter, pair_mask, inversion):
    strips, epochs = lax.axis_size("strip"), lax.axis_size("acq")
    plan = Plan(strips, epochs, raw_echoes.shape[2], raw_echoes.shape[3])

    raw = raw_echoes[0]
    block = compress(plan, 0, "all", range_filter, raw)
    if plan.parts > 1:
        range_filter, block = lax.optimization_barrier((range_filter, block))
        other = compress(plan, 1, "all", range_filter, raw)
        other, azimuth_filter = lax.optimization_barrier((other, azimuth_filter))
        spectrum = own_filter_by_kernel(plan, azimuth_filter)
        field, other = exchange_all(plan, block), exchange_all(plan, other)
    else:
        spectrum = own_filter(plan, azimuth_filter)
        field = exchange_all(plan, block)
    before = [focus(plan, 0, [field], spectrum)]
    before[0], pair_mask, inversion = lax.optimization_barrier((before[0], pair_mask, inversion))
    weights = all_weights(pair_mask, inversion)

    owners = strips * epochs
    device = [i % epochs * strips + i // epochs for i in range(owners)]
    halo = lax.ppermute(
        before[0][:, :, :, :1, :],
        ("acq", "strip"),
        [(device[i], device[i - 1]) for i in range(1, owners)],
    )
    if plan.parts > 1:
        gradients = focus(plan, 1, [other], spectrum, (weights, before, halo))
    else:
        gradients = slopes_to_epochs(plan, weights, before[0], halo)
    gathered = lax.all_to_all(gradients, "acq", split_axis=0, concat_axis=0, tiled=True)
    gathered = gathered.reshape(epochs, 2, plan.looks * plan.parts, plan.azimuth_looks)
    return gathered.swapaxes(0, 1).reshape(1, 2, -1, plan.azimuth_looks)


def solution(mesh):
    return jax.shard_map(
        per_device,
        mesh=mesh,
        in_specs=(
            P("acq", None, "strip", None),
            P(),
            P(None, None, "strip"),
            P("acq", None),
            P(None, "acq", None),
        ),
        out_specs=P("acq", None, "strip", None),
        check_vma=False,
    )
```

```python
import copy
import functools
import math

import jax
import jax.numpy as jnp
import ml_dtypes
import numpy as np
from jax import lax
from jax.experimental import pallas as pl
from jax.experimental.pallas import tpu as pltpu
from jax.sharding import PartitionSpec as P

LOOK = 4
RADIX = 8
ROWS = 8
RANGE_VMEM = 63 * 1024 * 1024
LAYOUT_VMEM = 8 * 1024 * 1024
FOCUS_VMEM = 32 * 1024 * 1024
OWNERS = ("strip", "acq")


def add(left, right):
    return (left[0] + right[0], left[1] + right[1])


def sub(left, right):
    return (left[0] - right[0], left[1] - right[1])


def times(value, cosine, sine):
    return (value[0] * cosine - value[1] * sine, value[0] * sine + value[1] * cosine)


def turn(value, sign):
    if sign > 0:
        return (-value[1], value[0])
    return (value[1], -value[0])


def dft4(x0, x1, x2, x3, sign):
    a, b = add(x0, x2), sub(x0, x2)
    c, d = add(x1, x3), turn(sub(x1, x3), sign)
    return [add(a, c), add(b, d), sub(a, c), sub(b, d)]


def dft8(x, sign):
    even = dft4(x[0], x[2], x[4], x[6], sign)
    odd = dft4(x[1], x[3], x[5], x[7], sign)
    half = math.sqrt(0.5)
    o1, o3 = odd[1], odd[3]
    t1 = add(o1, turn(o1, sign))
    t3 = sub(turn(o3, sign), o3)
    odd = [
        odd[0],
        (t1[0] * half, t1[1] * half),
        turn(odd[2], sign),
        (t3[0] * half, t3[1] * half),
    ]
    return [add(e, o) for e, o in zip(even, odd)] + [sub(e, o) for e, o in zip(even, odd)]


def two_parts(value):
    high = value.astype(jnp.bfloat16)
    low = (value - high.astype(jnp.float32)).astype(jnp.bfloat16)
    return high, low


def three_products(left_high, left_low, right_high, right_low, contract):
    def product(left, right):
        return lax.dot_general(
            left, right, (contract, ((), ())), preferred_element_type=jnp.float32
        )

    return (
        product(left_high, right_high)
        + product(left_high, right_low)
        + product(left_low, right_high)
    )


def host_parts(table):
    table = np.asarray(table, np.float64)
    high = table.astype(np.float32).astype(ml_dtypes.bfloat16)
    low = (table - high.astype(np.float64)).astype(np.float32).astype(ml_dtypes.bfloat16)
    return high, low


def unit(exponent, size, sign):
    angle = sign * 2.0 * np.pi / size * (exponent % size)
    return np.cos(angle), np.sin(angle)


def real_form(cosine, sine):
    top = np.concatenate([cosine, sine], axis=-1)
    bottom = np.concatenate([-sine, cosine], axis=-1)
    return np.concatenate([top, bottom], axis=-2)


class Plan:
    def __init__(self, strips, epochs, pulses, samples):
        self.strips, self.epochs = strips, epochs
        self.pulses, self.samples = pulses, samples
        self.azimuth = pulses * strips
        self.base = samples // RADIX
        self.owned = samples // (strips * epochs)
        even = all(size & (size - 1) == 0 for size in (strips, epochs))
        self.parts = 2 if even and self.owned in (64, 128) else 1
        self.start, self.rows = 0, self.owned
        self.looks = self.rows // LOOK
        self.all_looks = self.looks
        self.blocks = self.base // self.owned
        self.lanes = self.azimuth // RADIX
        self.azimuth_looks = self.azimuth // LOOK

    def part(self, number):
        if self.parts == 1:
            return self
        own = copy.copy(self)
        size = self.owned // 4
        own.start, own.rows = (0, 3 * size) if number == 0 else (3 * size, size)
        own.looks = own.rows // LOOK
        return own

    def tile_shift(self, block, tile):
        return block * self.owned + self.start + tile * ROWS


def lag_tables(plan):
    base, samples = plan.base, plan.samples
    index = np.arange(base)
    table = host_parts(
        np.concatenate(unit(index[:, None] * index[None, :], samples, -1.0), axis=1) / samples
    )
    block = np.arange(RADIX)[:, None]
    turns = np.stack(
        unit(block * index[None, :], RADIX, -1.0)
        + tuple(np.broadcast_to(part, (RADIX, base)) for part in unit(block, RADIX, 1.0))
    )
    return table + (turns.astype(np.float32),)


def lag_vectors(plan, filter_ref, table_high, table_low, turn_ref):
    base = plan.base
    lane = lax.broadcasted_iota(jnp.int32, (RADIX, base), 1)
    chosen = lane % RADIX == lax.broadcasted_iota(jnp.int32, (RADIX, base), 0)
    rows = []
    for c in range(2):
        for e in range(RADIX):
            block = jnp.broadcast_to(filter_ref[c : c + 1, e * base : (e + 1) * base], (RADIX, base))
            rows.append(jnp.where(chosen, block, 0.0))
    high, low = two_parts(jnp.concatenate(rows, axis=0))
    sums = three_products(high, low, table_high[...], table_low[...], ((1,), (0,)))
    real, imag = 0.0, 0.0
    for e in range(RADIX):
        by_real = sums[e * RADIX : (e + 1) * RADIX]
        by_imag = sums[(RADIX + e) * RADIX : (RADIX + e + 1) * RADIX]
        part_real = by_real[:, :base] - by_imag[:, base:]
        part_imag = by_real[:, base:] + by_imag[:, :base]
        cosine, sine = turn_ref[0, e : e + 1, :], turn_ref[1, e : e + 1, :]
        real = real + part_real * cosine - part_imag * sine
        imag = imag + part_real * sine + part_imag * cosine
    cosine, sine = turn_ref[2], turn_ref[3]
    return (
        jnp.concatenate([real, real * cosine - imag * sine], axis=1),
        jnp.concatenate([imag, real * sine + imag * cosine], axis=1),
    )


def fetch(copies):
    for move in copies:
        move.start()
    return copies


def compress_kernel(
    plan, relative, filter_ref, high_any, low_any, turn_any, raw_ref, *refs
):
    outs = refs[: plan.epochs if relative else 1]
    (
        table_high, table_low, turn_ref, raw, t_high, t_low, y_high, y_low, z_ref, sems, table_sems,
    ) = refs[len(outs) :][:11]
    out_ref = refs[-2] if relative else outs[0]
    base, blocks = plan.base, plan.blocks
    tiles = plan.rows // ROWS
    chunk = blocks * plan.rows
    pieces = sems.shape[0]
    piece = plan.pulses // pieces

    def raw_copy(at):
        rows = pl.ds(at * piece, piece)
        return pltpu.make_async_copy(raw_ref.at[:, rows, :], raw.at[:, rows, :], sems.at[at])

    tables = fetch(
        [
            pltpu.make_async_copy(source, target, table_sems.at[at])
            for at, (source, target) in enumerate(
                ((high_any, table_high), (low_any, table_low), (turn_any, turn_ref))
            )
        ]
    )
    fetch([raw_copy(at) for at in range(pieces)])
    def spread_pulses(at, carry):
        rows = pl.ds(pl.multiple_of(at * 2 * ROWS, 2 * ROWS), 2 * ROWS)
        x = [
            tuple(raw[c, rows, a * base : (a + 1) * base] for c in range(2))
            for a in range(RADIX)
        ]
        for d, value in enumerate(dft8(x, -1.0)):
            for c in range(2):
                high, low = two_parts(value[c])
                y_high[d, rows, c * base : (c + 1) * base] = high
                y_low[d, rows, c * base : (c + 1) * base] = low
        return carry

    steps = piece // (2 * ROWS)
    for at in range(pieces):
        raw_copy(at).wait()
        lax.fori_loop(at * steps, (at + 1) * steps, spread_pulses, 0)

    for move in tables:
        move.wait()
    lags = lag_vectors(plan, filter_ref, table_high, table_low, turn_ref)

    for d in range(RADIX):
        spread = [
            pltpu.roll(
                jnp.broadcast_to(lag[d : d + 1, :], (ROWS, 2 * base)),
                0,
                1,
                stride=1,
                stride_axis=0,
            )
            for lag in lags
        ]
        for pair in range(blocks * tiles // 2):
            real, imag = [], []
            for at in (2 * pair, 2 * pair + 1):
                shift = plan.tile_shift(at // tiles, at % tiles)
                real.append(pltpu.roll(spread[0], shift, 1)[:, :base])
                imag.append(pltpu.roll(spread[1], shift, 1)[:, :base])
            real_high, real_low = two_parts(jnp.concatenate(real, axis=0))
            imag_high, imag_low = two_parts(jnp.concatenate(imag, axis=0))
            top = pl.ds(pair * 2 * ROWS, 2 * ROWS)
            bottom = pl.ds(chunk + pair * 2 * ROWS, 2 * ROWS)
            t_high[d, top, :base] = real_high
            t_high[d, top, base:] = -imag_high
            t_high[d, bottom, :base] = imag_high
            t_high[d, bottom, base:] = real_high
            t_low[d, top, :base] = real_low
            t_low[d, top, base:] = -imag_low
            t_low[d, bottom, :base] = imag_low
            t_low[d, bottom, base:] = real_low
        z_ref[d] = three_products(t_high[d], t_low[d], y_high[d], y_low[d], ((1,), (1,)))

    for block in range(blocks):
        for tile in range(tiles):
            top = (block * tiles + tile) * ROWS
            z = [
                (z_ref[d, top : top + ROWS, :], z_ref[d, chunk + top : chunk + top + ROWS, :])
                for d in range(RADIX)
            ]
            for a, value in enumerate(dft8(z, 1.0)):
                for c in range(2):
                    strip, owner = divmod(a * blocks + block, plan.epochs)
                    rows = slice(tile * ROWS, (tile + 1) * ROWS)
                    if relative:
                        place = owner ^ lax.axis_index("acq"), strip ^ lax.axis_index("strip")
                    else:
                        place = strip, owner
                    out_ref[place[0], place[1], c, rows, :] = value[c]
    if relative:
        copies = fetch(
            [
                pltpu.make_async_copy(out_ref.at[m], out, refs[-1].at[m])
                for m, out in enumerate(outs)
            ]
        )
        for move in copies:
            move.wait()


def compress(plan, relative, range_filter, raw):
    chunk = plan.blocks * plan.rows
    whole = pl.BlockSpec(memory_space=pltpu.VMEM)
    bytes_moved = 8 * raw.size
    tables = lag_tables(plan)
    slab = (2, plan.rows, plan.pulses)
    shape = (plan.strips,) + (slab if relative else (plan.epochs,) + slab)
    scratch, out_specs = [], whole
    if relative:
        out_specs = [pl.BlockSpec(memory_space=pltpu.HBM)] * plan.epochs
        scratch = [
            pltpu.VMEM((plan.epochs,) + shape, jnp.float32),
            pltpu.SemaphoreType.DMA((plan.epochs,)),
        ]
    shape = jax.ShapeDtypeStruct(shape, jnp.float32)
    return pl.pallas_call(
        functools.partial(compress_kernel, plan, relative),
        out_shape=[shape] * plan.epochs if relative else shape,
        in_specs=[whole] + [pl.BlockSpec(memory_space=pltpu.HBM)] * 4,
        out_specs=out_specs,
        scratch_shapes=[
            *[pltpu.VMEM(table.shape, table.dtype) for table in tables],
            pltpu.VMEM(raw.shape, jnp.float32),
            pltpu.VMEM((RADIX, 2 * chunk, 2 * plan.base), jnp.bfloat16),
            pltpu.VMEM((RADIX, 2 * chunk, 2 * plan.base), jnp.bfloat16),
            pltpu.VMEM((RADIX, plan.pulses, 2 * plan.base), jnp.bfloat16),
            pltpu.VMEM((RADIX, plan.pulses, 2 * plan.base), jnp.bfloat16),
            pltpu.VMEM((RADIX, 2 * chunk, plan.pulses), jnp.float32),
            pltpu.SemaphoreType.DMA((4,)),
            pltpu.SemaphoreType.DMA((3,)),
            *scratch,
        ],
        compiler_params=pltpu.CompilerParams(vmem_limit_bytes=RANGE_VMEM),
        cost_estimate=pl.CostEstimate(
            flops=6 * RADIX * 4 * chunk * plan.base * plan.pulses,
            bytes_accessed=bytes_moved,
            transcendentals=0,
        ),
        name="range_compress",
    )(range_filter, *tables, raw)


def focus_kernel(plan, final, field_at, own, *refs):
    filter_any, high_any, low_any, twiddle_any, sum_any = refs[:5]
    if final:
        weight_ref, before_any, halo_any, out_ref = refs[5:9]
    else:
        (out_ref,) = refs[5:6]
    scratch = refs[9 if final else 6 :]
    (
        field_ref, filter_ref, table_high, table_low, twiddle_ref, sum_ref,
        y_high, y_low, z_ref, scene_ref, product_ref, field_sems, table_sems,
    ) = scratch[:13]
    rows, lanes, epochs, looks = plan.rows, plan.lanes, plan.epochs, plan.looks
    step = 2 * ROWS
    group = max(1, step // rows)
    per_block = field_ref.shape[-1] // lanes

    half = epochs // 2
    fields = [
        [
            pltpu.make_async_copy(
                field_at(at).at[pl.ds(side * half, half)],
                field_ref.at[at, pl.ds(side * half, half)],
                field_sems.at[at, side],
            )
            for at in range(field_ref.shape[0])
        ]
        for side in range(2)
    ]
    tables = [
        pltpu.make_async_copy(source, target, table_sems.at[at])
        for at, (source, target) in enumerate(
            (
                (twiddle_any, twiddle_ref),
                (high_any, table_high),
                (low_any, table_low),
                (filter_any, filter_ref),
                (sum_any, sum_ref),
            )
        )
    ]
    fetch(tables[:1])
    for copies in fields:
        fetch(copies)
    fetch(tables[1:])
    if final:
        looked_ref, slope_ref, halo_ref, late_sems = scratch[13:]
        late = fetch(
            [
                pltpu.make_async_copy(before_any, looked_ref, late_sems.at[0]),
                pltpu.make_async_copy(halo_any, halo_ref, late_sems.at[1]),
            ]
        )
    tables[0].wait()

    def rows_of(strip, slot, c, top, start):
        some = [
            field_ref[strip, slot + g, c, top : top + min(rows, step), start : start + lanes]
            for g in range(group)
        ]
        return some[0] if group == 1 else jnp.concatenate(some, axis=0)

    def forward(at, carry):
        slot = at * group
        j = slot ^ own[0]
        for top in range(0, rows, step):
            x = []
            for a in range(RADIX):
                strip, start = a // per_block, a % per_block * lanes
                x.append(tuple(rows_of(strip ^ own[1], slot, c, top, start) for c in range(2)))
            at = pl.ds(pl.multiple_of(j * rows + top, step), step)
            for d, value in enumerate(dft8(x, -1.0)):
                if d > 0:
                    value = times(value, twiddle_ref[0, d : d + 1, :], twiddle_ref[1, d : d + 1, :])
                for c in range(2):
                    high, low = two_parts(value[c])
                    y_high[d, at, c * lanes : (c + 1) * lanes] = high
                    y_low[d, at, c * lanes : (c + 1) * lanes] = low
        return carry

    for side, copies in enumerate(fields):
        for move in copies:
            move.wait()
        lax.fori_loop(side * half // group, (side + 1) * half // group, forward, 0)
    for move in tables[1:]:
        move.wait()

    for d in range(RADIX):
        spectrum = three_products(
            y_high[d], y_low[d], table_high[...], table_low[...], ((1,), (0,))
        )
        spectrum = spectrum.reshape(epochs, rows, 2 * lanes)
        real, imag = spectrum[:, :, :lanes], spectrum[:, :, lanes:]
        by_real, by_imag = filter_ref[0, d][None], filter_ref[1, d][None]
        spectrum = jnp.concatenate(
            [real * by_real - imag * by_imag, real * by_imag + imag * by_real], axis=2
        )
        high, low = two_parts(spectrum.reshape(epochs * rows, 2 * lanes))
        z_ref[d] = three_products(high, low, table_high[...], table_low[...], ((1,), (1,)))

    scene_ref[0] = jnp.zeros_like(scene_ref[0])
    scene_ref[1] = jnp.zeros_like(scene_ref[1])

    def backward(j, carry):
        for top in range(0, rows, ROWS):
            at = pl.ds(pl.multiple_of(j * rows + top, ROWS), ROWS)
            z = [
                times(
                    tuple(z_ref[d, at, c * lanes : (c + 1) * lanes] for c in range(2)),
                    twiddle_ref[2, d : d + 1, :],
                    twiddle_ref[3, d : d + 1, :],
                )
                for d in range(RADIX)
            ]
            for a, value in enumerate(dft8(z, 1.0)):
                for c in range(2):
                    scene_ref[j + 2, c, a, top : top + ROWS, :] = value[c]
        return carry

    lax.fori_loop(0, epochs, backward, 0)

    def interfere(j, carry):
        for a in range(RADIX):
            columns = pl.ds(a * lanes, lanes)
            sums = [0.0] * 4
            for q in range(LOOK):
                rows_at = pl.ds(q, looks, stride=LOOK)
                later, *earlier = [
                    tuple(scene_ref[j + 2 - lag, c, a, rows_at, :] for c in range(2))
                    for lag in range(3)
                ]
                for at, value in enumerate(earlier):
                    sums[2 * at] += value[0] * later[0] + value[1] * later[1]
                    sums[2 * at + 1] += value[1] * later[0] - value[0] * later[1]
            place = pl.ds(pl.multiple_of(j * 4 * looks, ROWS), 4 * looks)
            product_ref[place, columns] = jnp.concatenate(sums, axis=0)
        return carry

    lax.fori_loop(0, epochs, interfere, 0)

    products = product_ref[...]
    high, low = two_parts(products)
    weights = sum_ref[...]
    looked = []
    for start in range(0, plan.azimuth, weights.shape[0]):
        columns = slice(start, start + weights.shape[0])
        looked.append(
            jnp.dot(high[:, columns], weights, preferred_element_type=jnp.float32)
            + jnp.dot(low[:, columns], weights, preferred_element_type=jnp.float32)
        )
    looked = jnp.concatenate(looked, axis=1)
    looked = looked.reshape(epochs, 2, 2, looks, plan.azimuth_looks)
    if final:
        for move in late:
            move.wait()
        looked_ref[:, :, :, plan.all_looks - looks :, :] = looked
        slopes_and_sums(plan, weight_ref, looked_ref, halo_ref, out_ref, slope_ref)
    else:
        out_ref[:, :, :, :looks, :] = looked
        if looks < plan.all_looks:
            rest = (epochs, 2, 2, plan.all_looks - looks, plan.azimuth_looks)
            out_ref[:, :, :, looks:, :] = jnp.zeros(rest, jnp.float32)


def slopes_and_sums(plan, weight_ref, looked_ref, halo_ref, out_ref, slope_ref):
    epochs = plan.epochs
    columns = plan.azimuth_looks
    inner = lax.broadcasted_iota(jnp.int32, (plan.all_looks, columns), 1) < columns - 1

    def slopes(at, carry):
        j, lag = at // 2, at % 2
        real, imag = looked_ref[j, lag, 0], looked_ref[j, lag, 1]
        next_real = pltpu.roll(real, columns - 1, 1)
        next_imag = pltpu.roll(imag, columns - 1, 1)
        slope_ref[at, 0] = jnp.where(inner, next_imag * real - next_real * imag, 0.0)
        next_real = jnp.concatenate([real[1:], halo_ref[j, lag, 0]], axis=0)
        next_imag = jnp.concatenate([imag[1:], halo_ref[j, lag, 1]], axis=0)
        slope_ref[at, 1] = next_imag * real - next_real * imag
        return carry

    lax.fori_loop(0, 2 * epochs, slopes, 0)

    def epoch(e, carry):
        total = weight_ref[e, 0] * slope_ref[0]
        for at in range(1, 2 * epochs):
            total = total + weight_ref[e, at] * slope_ref[at]
        out_ref[e] = total
        return carry

    lax.fori_loop(0, epochs, epoch, 0)


def focus_tables(plan):
    lanes = plan.lanes
    index = np.arange(lanes)
    table = host_parts(real_form(*unit(index[:, None] * index[None, :], lanes, -1.0)))
    cosine, sine = unit(np.arange(RADIX)[:, None] * index[None, :], plan.azimuth, -1.0)
    twiddles = np.stack([cosine, sine, cosine / plan.azimuth, -sine / plan.azimuth])
    sums = np.arange(plan.azimuth // 2)[:, None] // LOOK == np.arange(plan.azimuth_looks // 2)[None, :]
    return table + (twiddles.astype(np.float32), (sums / LOOK).astype(ml_dtypes.bfloat16))


def focus(plan, fields, spectrum, finish=None):
    lanes = plan.lanes
    total = plan.epochs * plan.rows
    tables = focus_tables(plan)
    whole = pl.BlockSpec(memory_space=pltpu.VMEM)
    looked = (plan.epochs, 2, 2, plan.all_looks, plan.azimuth_looks)
    gradients = (plan.epochs, 2, plan.all_looks, plan.azimuth_looks)
    operands = [*fields, spectrum, *tables]
    in_specs = [pl.BlockSpec(memory_space=pltpu.HBM)] * len(operands)
    blocks = plan.azimuth // fields[0].shape[-1]
    scratch = [
        pltpu.VMEM((blocks, plan.epochs) + fields[0].shape[-3:], jnp.float32),
        pltpu.VMEM(spectrum.shape, jnp.float32),
        *[pltpu.VMEM(table.shape, table.dtype) for table in tables],
        pltpu.VMEM((RADIX, total, 2 * lanes), jnp.bfloat16),
        pltpu.VMEM((RADIX, total, 2 * lanes), jnp.bfloat16),
        pltpu.VMEM((RADIX, total, 2 * lanes), jnp.float32),
        pltpu.VMEM((plan.epochs + 2, 2, RADIX, plan.rows, lanes), jnp.float32),
        pltpu.VMEM((plan.epochs * 4 * plan.looks, plan.azimuth), jnp.float32),
        pltpu.SemaphoreType.DMA((blocks, 2)),
        pltpu.SemaphoreType.DMA((5,)),
    ]
    shape = looked
    if finish is not None:
        weights, before, halo = finish
        shape = gradients
        operands += [weights, before, halo]
        in_specs += [pl.BlockSpec(memory_space=pltpu.SMEM)]
        in_specs += [pl.BlockSpec(memory_space=pltpu.HBM)] * 2
        scratch += [
            pltpu.VMEM(looked, jnp.float32),
            pltpu.VMEM((2 * plan.epochs,) + gradients[1:], jnp.float32),
            pltpu.VMEM(halo.shape, jnp.float32),
            pltpu.SemaphoreType.DMA((2,)),
        ]

    def kernel(*refs):
        some, refs = refs[: len(fields)], refs[len(fields) :]

        relative = len(some) > 1
        own = (lax.axis_index("acq"), lax.axis_index("strip")) if relative else (0, 0)

        def field_at(at):
            return some[at] if relative else some[0].at[at]

        focus_kernel(plan, finish is not None, field_at, own, *refs)

    return pl.pallas_call(
        kernel,
        out_shape=jax.ShapeDtypeStruct(shape, jnp.float32),
        in_specs=in_specs,
        out_specs=whole,
        scratch_shapes=scratch,
        compiler_params=pltpu.CompilerParams(vmem_limit_bytes=FOCUS_VMEM),
        cost_estimate=pl.CostEstimate(
            flops=2 * 6 * RADIX * total * 4 * lanes * lanes,
            bytes_accessed=4 * total * 2 * plan.azimuth + 4 * 1024 * 1024,
            transcendentals=0,
        ),
        name="azimuth_focus",
    )(*operands)


def slope_kernel(plan, weight_ref, looked_ref, halo_ref, out_ref, slope_ref):
    slopes_and_sums(plan, weight_ref, looked_ref, halo_ref, out_ref, slope_ref)


def slopes_to_epochs(plan, weights, looked, halo):
    whole = pl.BlockSpec(memory_space=pltpu.VMEM)
    looks = plan.all_looks
    return pl.pallas_call(
        functools.partial(slope_kernel, plan),
        out_shape=jax.ShapeDtypeStruct(
            (plan.epochs, 2, looks, plan.azimuth_looks), jnp.float32
        ),
        in_specs=[pl.BlockSpec(memory_space=pltpu.SMEM), whole, whole],
        out_specs=whole,
        scratch_shapes=[
            pltpu.VMEM((2 * plan.epochs, 2, looks, plan.azimuth_looks), jnp.float32)
        ],
        compiler_params=pltpu.CompilerParams(vmem_limit_bytes=FOCUS_VMEM),
        cost_estimate=pl.CostEstimate(
            flops=8 * looked.size * plan.epochs, bytes_accessed=5 * looked.size, transcendentals=0
        ),
        name="slopes_to_epochs",
    )(weights, looked, halo)


def own_filter(plan, azimuth_filter):
    start = lax.axis_index("acq") * plan.owned
    own = lax.dynamic_slice_in_dim(azimuth_filter, start, plan.owned, axis=2)
    return own.reshape(2, plan.lanes, RADIX, plan.owned).transpose(0, 2, 3, 1)


def own_filter_kernel(plan, filter_any, *refs):
    *outs, block_ref, turned_ref, sem = refs
    width = block_ref.shape[-1]
    acq = lax.axis_index("acq")
    start = acq * plan.owned // width * width
    inside = acq * plan.owned % width
    move = pltpu.make_async_copy(
        filter_any.at[:, :, pl.ds(pl.multiple_of(start, width), width)], block_ref, sem
    )
    move.start()
    move.wait()
    for c in range(2):
        for d in range(RADIX):
            turned_ref[...] = block_ref[c, pl.ds(d, plan.lanes, stride=RADIX), :].T
            for number, out_ref in enumerate(outs):
                part = plan.part(number)
                start = pl.multiple_of(inside + part.start, ROWS)
                out_ref[c, d] = turned_ref[pl.ds(start, part.rows), :]


def own_filter_by_kernel(plan, azimuth_filter):
    width = 128
    return pl.pallas_call(
        functools.partial(own_filter_kernel, plan),
        out_shape=[
            jax.ShapeDtypeStruct((2, RADIX, plan.part(number).rows, plan.lanes), jnp.float32)
            for number in range(plan.parts)
        ],
        in_specs=[pl.BlockSpec(memory_space=pltpu.HBM)],
        out_specs=[pl.BlockSpec(memory_space=pltpu.VMEM)] * plan.parts,
        scratch_shapes=[
            pltpu.VMEM((2, plan.azimuth, width), jnp.float32),
            pltpu.VMEM((width, plan.lanes), jnp.float32),
            pltpu.SemaphoreType.DMA,
        ],
        compiler_params=pltpu.CompilerParams(vmem_limit_bytes=LAYOUT_VMEM),
        cost_estimate=pl.CostEstimate(flops=0, bytes_accessed=1024, transcendentals=0),
        name="own_filter",
    )(azimuth_filter)


def exchange_all(plan, block):
    shape = block.shape
    block = block.reshape((plan.strips * plan.epochs,) + shape[2:])
    received = lax.all_to_all(block, OWNERS, split_axis=0, concat_axis=0, tiled=True)
    join = max(1, plan.lanes // plan.pulses)
    received = received.reshape((plan.strips // join, join) + shape[1:])
    if join > 1:
        received = received.transpose(0, 2, 3, 4, 1, 5)
    return received.reshape(plan.strips // join, plan.epochs, 2, plan.rows, join * plan.pulses)


def partners(slots, axis):
    size = lax.axis_size(axis)
    moved = []
    for k, slot in enumerate(slots):
        moved.append(slot if k == 0 else lax.ppermute(slot, axis, [(i, i ^ k) for i in range(size)]))
    return moved


def regroup(blocks):
    count, inner = len(blocks), blocks[0].shape[0]

    def kernel(*refs):
        ins, outs = refs[:count], refs[count : count + inner]
        stage, in_sems, out_sems = refs[count + inner :]
        inward = [
            fetch(
                [
                    pltpu.make_async_copy(ins[m].at[k], stage.at[k, m], in_sems.at[k, m])
                    for m in range(count)
                ]
            )
            for k in range(inner)
        ]
        outward = []
        for k in range(inner):
            for move in inward[k]:
                move.wait()
            outward += fetch([pltpu.make_async_copy(stage.at[k], outs[k], out_sems.at[k])])
        for move in outward:
            move.wait()

    slab = (count,) + blocks[0].shape[1:]
    place = pl.BlockSpec(memory_space=pltpu.HBM)
    return pl.pallas_call(
        kernel,
        out_shape=[jax.ShapeDtypeStruct(slab, jnp.float32)] * inner,
        in_specs=[place] * count,
        out_specs=[place] * inner,
        scratch_shapes=[
            pltpu.VMEM((inner,) + slab, jnp.float32),
            pltpu.SemaphoreType.DMA((inner, count)),
            pltpu.SemaphoreType.DMA((inner,)),
        ],
        compiler_params=pltpu.CompilerParams(vmem_limit_bytes=LAYOUT_VMEM),
        cost_estimate=pl.CostEstimate(flops=0, bytes_accessed=1024, transcendentals=0),
        name="regroup",
    )(*blocks)


def all_weights(pair_mask, inversion):
    lags = jnp.array([1, 2], dtype=jnp.int32)
    usable = pair_mask[0].astype(jnp.float32) * (lax.axis_index("acq") >= lags).astype(jnp.float32)
    weights = lax.all_gather(inversion[:, 0, :] * usable[None, :], "acq", axis=1, tiled=False)
    return weights.reshape(weights.shape[0], -1)


def per_device(raw_echoes, range_filter, azimuth_filter, pair_mask, inversion):
    strips, epochs = lax.axis_size("strip"), lax.axis_size("acq")
    plan = Plan(strips, epochs, raw_echoes.shape[2], raw_echoes.shape[3])

    raw = raw_echoes[0]
    big, small = plan.part(0), plan.part(1)
    block = compress(big, False, range_filter, raw)
    if plan.parts > 1:
        range_filter, block = lax.optimization_barrier((range_filter, block))
        other = compress(small, True, range_filter, raw)
        *other, azimuth_filter, pair_mask, inversion = lax.optimization_barrier(
            (*other, azimuth_filter, pair_mask, inversion)
        )
        weights = all_weights(pair_mask, inversion)
        spectrum, other_spectrum = own_filter_by_kernel(plan, azimuth_filter)
        field = exchange_all(big, block)
        other = partners(other, "acq")
        *other, spectrum, weights = lax.optimization_barrier((*other, spectrum, weights))
        other = partners(regroup(other), "strip")
    else:
        weights = all_weights(pair_mask, inversion)
        spectrum = own_filter(plan, azimuth_filter)
        field = exchange_all(plan, block)
    before = focus(big, [field], spectrum)

    owners = strips * epochs
    device = [i % epochs * strips + i // epochs for i in range(owners)]
    halo = lax.ppermute(
        before[:, :, :, :1, :],
        ("acq", "strip"),
        [(device[i], device[i - 1]) for i in range(1, owners)],
    )
    if plan.parts > 1:
        gradients = focus(small, other, other_spectrum, (weights, before, halo))
    else:
        gradients = slopes_to_epochs(plan, weights, before, halo)
    gathered = lax.all_to_all(gradients, "acq", split_axis=0, concat_axis=0, tiled=True)
    gathered = gathered.reshape(epochs, 2, plan.all_looks, plan.azimuth_looks)
    return gathered.swapaxes(0, 1).reshape(1, 2, -1, plan.azimuth_looks)


def solution(mesh):
    return jax.shard_map(
        per_device,
        mesh=mesh,
        in_specs=(
            P("acq", None, "strip", None),
            P(),
            P(None, None, "strip"),
            P("acq", None),
            P(None, "acq", None),
        ),
        out_specs=P("acq", None, "strip", None),
        check_vma=False,
    )
```

```python
import copy
import functools
import math

import jax
import jax.numpy as jnp
import ml_dtypes
import numpy as np
from jax import lax
from jax.experimental import pallas as pl
from jax.experimental.pallas import tpu as pltpu
from jax.sharding import PartitionSpec as P

LOOK = 4
RADIX = 8
ROWS = 8
RANGE_VMEM = 63 * 1024 * 1024
LAYOUT_VMEM = 8 * 1024 * 1024
FOCUS_VMEM = 32 * 1024 * 1024
OWNERS = ("strip", "acq")


def add(left, right):
    return (left[0] + right[0], left[1] + right[1])


def sub(left, right):
    return (left[0] - right[0], left[1] - right[1])


def times(value, cosine, sine):
    return (value[0] * cosine - value[1] * sine, value[0] * sine + value[1] * cosine)


def turn(value, sign):
    if sign > 0:
        return (-value[1], value[0])
    return (value[1], -value[0])


def dft4(x0, x1, x2, x3, sign):
    a, b = add(x0, x2), sub(x0, x2)
    c, d = add(x1, x3), turn(sub(x1, x3), sign)
    return [add(a, c), add(b, d), sub(a, c), sub(b, d)]


def dft8(x, sign):
    even = dft4(x[0], x[2], x[4], x[6], sign)
    odd = dft4(x[1], x[3], x[5], x[7], sign)
    half = math.sqrt(0.5)
    o1, o3 = odd[1], odd[3]
    t1 = add(o1, turn(o1, sign))
    t3 = sub(turn(o3, sign), o3)
    odd = [
        odd[0],
        (t1[0] * half, t1[1] * half),
        turn(odd[2], sign),
        (t3[0] * half, t3[1] * half),
    ]
    return [add(e, o) for e, o in zip(even, odd)] + [sub(e, o) for e, o in zip(even, odd)]


def two_parts(value):
    high = value.astype(jnp.bfloat16)
    low = (value - high.astype(jnp.float32)).astype(jnp.bfloat16)
    return high, low


def three_products(left_high, left_low, right_high, right_low, contract):
    def product(left, right):
        return lax.dot_general(
            left, right, (contract, ((), ())), preferred_element_type=jnp.float32
        )

    return (
        product(left_high, right_high)
        + product(left_high, right_low)
        + product(left_low, right_high)
    )


def host_parts(table):
    table = np.asarray(table, np.float64)
    high = table.astype(np.float32).astype(ml_dtypes.bfloat16)
    low = (table - high.astype(np.float64)).astype(np.float32).astype(ml_dtypes.bfloat16)
    return high, low


def unit(exponent, size, sign):
    angle = sign * 2.0 * np.pi / size * (exponent % size)
    return np.cos(angle), np.sin(angle)


def real_form(cosine, sine):
    top = np.concatenate([cosine, sine], axis=-1)
    bottom = np.concatenate([-sine, cosine], axis=-1)
    return np.concatenate([top, bottom], axis=-2)


class Plan:
    def __init__(self, strips, epochs, pulses, samples):
        self.strips, self.epochs = strips, epochs
        self.pulses, self.samples = pulses, samples
        self.azimuth = pulses * strips
        self.base = samples // RADIX
        self.owned = samples // (strips * epochs)
        even = all(size & (size - 1) == 0 for size in (strips, epochs))
        self.parts = 2 if even and self.owned in (64, 128) else 1
        self.start, self.rows = 0, self.owned
        self.looks = self.rows // LOOK
        self.all_looks = self.looks
        self.blocks = self.base // self.owned
        self.lanes = self.azimuth // RADIX
        self.azimuth_looks = self.azimuth // LOOK

    def part(self, number):
        if self.parts == 1:
            return self
        own = copy.copy(self)
        size = self.owned // 4
        own.start, own.rows = (0, size) if number == 0 else (size, 3 * size)
        own.looks = own.rows // LOOK
        return own

    def tile_shift(self, block, tile):
        return block * self.owned + self.start + tile * ROWS


def lag_tables(plan):
    base, samples = plan.base, plan.samples
    index = np.arange(base)
    table = host_parts(
        np.concatenate(unit(index[:, None] * index[None, :], samples, -1.0), axis=1) / samples
    )
    block = np.arange(RADIX)[:, None]
    turns = np.stack(
        unit(block * index[None, :], RADIX, -1.0)
        + tuple(np.broadcast_to(part, (RADIX, base)) for part in unit(block, RADIX, 1.0))
    )
    return table + (turns.astype(np.float32),)


def lag_vectors(plan, filter_ref, table_high, table_low, turn_ref):
    base = plan.base
    lane = lax.broadcasted_iota(jnp.int32, (RADIX, base), 1)
    chosen = lane % RADIX == lax.broadcasted_iota(jnp.int32, (RADIX, base), 0)
    rows = []
    for c in range(2):
        for e in range(RADIX):
            block = jnp.broadcast_to(filter_ref[c : c + 1, e * base : (e + 1) * base], (RADIX, base))
            rows.append(jnp.where(chosen, block, 0.0))
    high, low = two_parts(jnp.concatenate(rows, axis=0))
    sums = three_products(high, low, table_high[...], table_low[...], ((1,), (0,)))
    real, imag = 0.0, 0.0
    for e in range(RADIX):
        by_real = sums[e * RADIX : (e + 1) * RADIX]
        by_imag = sums[(RADIX + e) * RADIX : (RADIX + e + 1) * RADIX]
        part_real = by_real[:, :base] - by_imag[:, base:]
        part_imag = by_real[:, base:] + by_imag[:, :base]
        cosine, sine = turn_ref[0, e : e + 1, :], turn_ref[1, e : e + 1, :]
        real = real + part_real * cosine - part_imag * sine
        imag = imag + part_real * sine + part_imag * cosine
    cosine, sine = turn_ref[2], turn_ref[3]
    return (
        jnp.concatenate([real, real * cosine - imag * sine], axis=1),
        jnp.concatenate([imag, real * sine + imag * cosine], axis=1),
    )


def fetch(copies):
    for move in copies:
        move.start()
    return copies


def compress_kernel(
    plan, relative, filter_ref, high_any, low_any, turn_any, raw_ref, *refs
):
    outs = refs[: plan.epochs if relative else 1]
    (
        table_high, table_low, turn_ref, raw, t_high, t_low, y_high, y_low, z_ref, sems, table_sems,
    ) = refs[len(outs) :][:11]
    out_ref = refs[-2] if relative else outs[0]
    base, blocks = plan.base, plan.blocks
    tiles = plan.rows // ROWS
    chunk = blocks * plan.rows
    pieces = sems.shape[0]
    piece = plan.pulses // pieces

    def raw_copy(at):
        rows = pl.ds(at * piece, piece)
        return pltpu.make_async_copy(raw_ref.at[:, rows, :], raw.at[:, rows, :], sems.at[at])

    tables = fetch(
        [
            pltpu.make_async_copy(source, target, table_sems.at[at])
            for at, (source, target) in enumerate(
                ((high_any, table_high), (low_any, table_low), (turn_any, turn_ref))
            )
        ]
    )
    fetch([raw_copy(at) for at in range(pieces)])
    def spread_pulses(at, carry):
        rows = pl.ds(pl.multiple_of(at * 2 * ROWS, 2 * ROWS), 2 * ROWS)
        x = [
            tuple(raw[c, rows, a * base : (a + 1) * base] for c in range(2))
            for a in range(RADIX)
        ]
        for d, value in enumerate(dft8(x, -1.0)):
            for c in range(2):
                high, low = two_parts(value[c])
                y_high[d, rows, c * base : (c + 1) * base] = high
                y_low[d, rows, c * base : (c + 1) * base] = low
        return carry

    steps = piece // (2 * ROWS)
    for at in range(pieces):
        raw_copy(at).wait()
        lax.fori_loop(at * steps, (at + 1) * steps, spread_pulses, 0)

    for move in tables:
        move.wait()
    lags = lag_vectors(plan, filter_ref, table_high, table_low, turn_ref)

    for d in range(RADIX):
        spread = [
            pltpu.roll(
                jnp.broadcast_to(lag[d : d + 1, :], (ROWS, 2 * base)),
                0,
                1,
                stride=1,
                stride_axis=0,
            )
            for lag in lags
        ]
        for pair in range(blocks * tiles // 2):
            real, imag = [], []
            for at in (2 * pair, 2 * pair + 1):
                shift = plan.tile_shift(at // tiles, at % tiles)
                real.append(pltpu.roll(spread[0], shift, 1)[:, :base])
                imag.append(pltpu.roll(spread[1], shift, 1)[:, :base])
            real_high, real_low = two_parts(jnp.concatenate(real, axis=0))
            imag_high, imag_low = two_parts(jnp.concatenate(imag, axis=0))
            top = pl.ds(pair * 2 * ROWS, 2 * ROWS)
            bottom = pl.ds(chunk + pair * 2 * ROWS, 2 * ROWS)
            t_high[d, top, :base] = real_high
            t_high[d, top, base:] = -imag_high
            t_high[d, bottom, :base] = imag_high
            t_high[d, bottom, base:] = real_high
            t_low[d, top, :base] = real_low
            t_low[d, top, base:] = -imag_low
            t_low[d, bottom, :base] = imag_low
            t_low[d, bottom, base:] = real_low
        z_ref[d] = three_products(t_high[d], t_low[d], y_high[d], y_low[d], ((1,), (1,)))

    for block in range(blocks):
        for tile in range(tiles):
            top = (block * tiles + tile) * ROWS
            z = [
                (z_ref[d, top : top + ROWS, :], z_ref[d, chunk + top : chunk + top + ROWS, :])
                for d in range(RADIX)
            ]
            for a, value in enumerate(dft8(z, 1.0)):
                for c in range(2):
                    strip, owner = divmod(a * blocks + block, plan.epochs)
                    rows = slice(tile * ROWS, (tile + 1) * ROWS)
                    if relative:
                        place = owner ^ lax.axis_index("acq"), strip ^ lax.axis_index("strip")
                    else:
                        place = strip, owner
                    out_ref[place[0], place[1], c, rows, :] = value[c]
    if relative:
        copies = fetch(
            [
                pltpu.make_async_copy(out_ref.at[m], out, refs[-1].at[m])
                for m, out in enumerate(outs)
            ]
        )
        for move in copies:
            move.wait()


def compress(plan, relative, range_filter, raw):
    chunk = plan.blocks * plan.rows
    whole = pl.BlockSpec(memory_space=pltpu.VMEM)
    bytes_moved = 8 * raw.size
    tables = lag_tables(plan)
    slab = (2, plan.rows, plan.pulses)
    shape = (plan.strips,) + (slab if relative else (plan.epochs,) + slab)
    scratch, out_specs = [], whole
    if relative:
        out_specs = [pl.BlockSpec(memory_space=pltpu.HBM)] * plan.epochs
        scratch = [
            pltpu.VMEM((plan.epochs,) + shape, jnp.float32),
            pltpu.SemaphoreType.DMA((plan.epochs,)),
        ]
    shape = jax.ShapeDtypeStruct(shape, jnp.float32)
    return pl.pallas_call(
        functools.partial(compress_kernel, plan, relative),
        out_shape=[shape] * plan.epochs if relative else shape,
        in_specs=[whole] + [pl.BlockSpec(memory_space=pltpu.HBM)] * 4,
        out_specs=out_specs,
        scratch_shapes=[
            *[pltpu.VMEM(table.shape, table.dtype) for table in tables],
            pltpu.VMEM(raw.shape, jnp.float32),
            pltpu.VMEM((RADIX, 2 * chunk, 2 * plan.base), jnp.bfloat16),
            pltpu.VMEM((RADIX, 2 * chunk, 2 * plan.base), jnp.bfloat16),
            pltpu.VMEM((RADIX, plan.pulses, 2 * plan.base), jnp.bfloat16),
            pltpu.VMEM((RADIX, plan.pulses, 2 * plan.base), jnp.bfloat16),
            pltpu.VMEM((RADIX, 2 * chunk, plan.pulses), jnp.float32),
            pltpu.SemaphoreType.DMA((4,)),
            pltpu.SemaphoreType.DMA((3,)),
            *scratch,
        ],
        compiler_params=pltpu.CompilerParams(vmem_limit_bytes=RANGE_VMEM),
        cost_estimate=pl.CostEstimate(
            flops=6 * RADIX * 4 * chunk * plan.base * plan.pulses,
            bytes_accessed=bytes_moved,
            transcendentals=0,
        ),
        name="range_compress",
    )(range_filter, *tables, raw)


def focus_kernel(plan, final, field_at, own, *refs):
    filter_any, high_any, low_any, twiddle_any, sum_any = refs[:5]
    if final:
        weight_ref, before_any, halo_any, out_ref = refs[5:9]
    else:
        (out_ref,) = refs[5:6]
    scratch = refs[9 if final else 6 :]
    (
        field_ref, filter_ref, table_high, table_low, twiddle_ref, sum_ref,
        y_high, y_low, z_ref, scene_ref, product_ref, field_sems, table_sems,
    ) = scratch[:13]
    rows, lanes, epochs, looks = plan.rows, plan.lanes, plan.epochs, plan.looks
    step = 2 * ROWS
    group = max(1, step // rows)
    per_block = field_ref.shape[-1] // lanes

    half = epochs // 2
    fields = [
        [
            pltpu.make_async_copy(
                field_at(at).at[pl.ds(side * half, half)],
                field_ref.at[at, pl.ds(side * half, half)],
                field_sems.at[at, side],
            )
            for at in range(field_ref.shape[0])
        ]
        for side in range(2)
    ]
    tables = [
        pltpu.make_async_copy(source, target, table_sems.at[at])
        for at, (source, target) in enumerate(
            (
                (twiddle_any, twiddle_ref),
                (high_any, table_high),
                (low_any, table_low),
                (filter_any, filter_ref),
                (sum_any, sum_ref),
            )
        )
    ]
    fetch(tables[:1])
    for copies in fields:
        fetch(copies)
    fetch(tables[1:])
    if final:
        looked_ref, slope_ref, halo_ref, late_sems = scratch[13:]
        late = fetch(
            [
                pltpu.make_async_copy(before_any, looked_ref, late_sems.at[0]),
                pltpu.make_async_copy(halo_any, halo_ref, late_sems.at[1]),
            ]
        )
    tables[0].wait()

    def rows_of(strip, slot, c, top, start):
        some = [
            field_ref[strip, slot + g, c, top : top + min(rows, step), start : start + lanes]
            for g in range(group)
        ]
        return some[0] if group == 1 else jnp.concatenate(some, axis=0)

    def forward(at, carry):
        slot = at * group
        j = slot ^ own[0]
        for top in range(0, rows, step):
            x = []
            for a in range(RADIX):
                strip, start = a // per_block, a % per_block * lanes
                x.append(tuple(rows_of(strip ^ own[1], slot, c, top, start) for c in range(2)))
            at = pl.ds(pl.multiple_of(j * rows + top, step), step)
            for d, value in enumerate(dft8(x, -1.0)):
                if d > 0:
                    value = times(value, twiddle_ref[0, d : d + 1, :], twiddle_ref[1, d : d + 1, :])
                for c in range(2):
                    high, low = two_parts(value[c])
                    y_high[d, at, c * lanes : (c + 1) * lanes] = high
                    y_low[d, at, c * lanes : (c + 1) * lanes] = low
        return carry

    for side, copies in enumerate(fields):
        for move in copies:
            move.wait()
        lax.fori_loop(side * half // group, (side + 1) * half // group, forward, 0)
    for move in tables[1:]:
        move.wait()

    for d in range(RADIX):
        spectrum = three_products(
            y_high[d], y_low[d], table_high[...], table_low[...], ((1,), (0,))
        )
        spectrum = spectrum.reshape(epochs, rows, 2 * lanes)
        real, imag = spectrum[:, :, :lanes], spectrum[:, :, lanes:]
        by_real, by_imag = filter_ref[0, d][None], filter_ref[1, d][None]
        spectrum = jnp.concatenate(
            [real * by_real - imag * by_imag, real * by_imag + imag * by_real], axis=2
        )
        high, low = two_parts(spectrum.reshape(epochs * rows, 2 * lanes))
        z_ref[d] = three_products(high, low, table_high[...], table_low[...], ((1,), (1,)))

    scene_ref[0] = jnp.zeros_like(scene_ref[0])
    scene_ref[1] = jnp.zeros_like(scene_ref[1])

    def backward(j, carry):
        for top in range(0, rows, ROWS):
            at = pl.ds(pl.multiple_of(j * rows + top, ROWS), ROWS)
            z = [
                times(
                    tuple(z_ref[d, at, c * lanes : (c + 1) * lanes] for c in range(2)),
                    twiddle_ref[2, d : d + 1, :],
                    twiddle_ref[3, d : d + 1, :],
                )
                for d in range(RADIX)
            ]
            for a, value in enumerate(dft8(z, 1.0)):
                for c in range(2):
                    scene_ref[j + 2, c, a, top : top + ROWS, :] = value[c]
        return carry

    lax.fori_loop(0, epochs, backward, 0)

    def interfere(j, carry):
        for a in range(RADIX):
            columns = pl.ds(a * lanes, lanes)
            sums = [0.0] * 4
            for q in range(LOOK):
                rows_at = pl.ds(q, looks, stride=LOOK)
                later, *earlier = [
                    tuple(scene_ref[j + 2 - lag, c, a, rows_at, :] for c in range(2))
                    for lag in range(3)
                ]
                for at, value in enumerate(earlier):
                    sums[2 * at] += value[0] * later[0] + value[1] * later[1]
                    sums[2 * at + 1] += value[1] * later[0] - value[0] * later[1]
            place = pl.ds(pl.multiple_of(j * 4 * looks, ROWS), 4 * looks)
            product_ref[place, columns] = jnp.concatenate(sums, axis=0)
        return carry

    lax.fori_loop(0, epochs, interfere, 0)

    products = product_ref[...]
    high, low = two_parts(products)
    weights = sum_ref[...]
    looked = []
    for start in range(0, plan.azimuth, weights.shape[0]):
        columns = slice(start, start + weights.shape[0])
        looked.append(
            jnp.dot(high[:, columns], weights, preferred_element_type=jnp.float32)
            + jnp.dot(low[:, columns], weights, preferred_element_type=jnp.float32)
        )
    looked = jnp.concatenate(looked, axis=1)
    looked = looked.reshape(epochs, 2, 2, looks, plan.azimuth_looks)
    if final:
        for move in late:
            move.wait()
        looked_ref[:, :, :, plan.all_looks - looks :, :] = looked
        slopes_and_sums(plan, weight_ref, looked_ref, halo_ref, out_ref, slope_ref)
    else:
        out_ref[:, :, :, :looks, :] = looked
        if looks < plan.all_looks:
            rest = (epochs, 2, 2, plan.all_looks - looks, plan.azimuth_looks)
            out_ref[:, :, :, looks:, :] = jnp.zeros(rest, jnp.float32)


def slopes_and_sums(plan, weight_ref, looked_ref, halo_ref, out_ref, slope_ref):
    epochs = plan.epochs
    columns = plan.azimuth_looks
    inner = lax.broadcasted_iota(jnp.int32, (plan.all_looks, columns), 1) < columns - 1

    def slopes(at, carry):
        j, lag = at // 2, at % 2
        real, imag = looked_ref[j, lag, 0], looked_ref[j, lag, 1]
        next_real = pltpu.roll(real, columns - 1, 1)
        next_imag = pltpu.roll(imag, columns - 1, 1)
        slope_ref[at, 0] = jnp.where(inner, next_imag * real - next_real * imag, 0.0)
        next_real = jnp.concatenate([real[1:], halo_ref[j, lag, 0]], axis=0)
        next_imag = jnp.concatenate([imag[1:], halo_ref[j, lag, 1]], axis=0)
        slope_ref[at, 1] = next_imag * real - next_real * imag
        return carry

    lax.fori_loop(0, 2 * epochs, slopes, 0)

    def epoch(e, carry):
        total = weight_ref[e, 0] * slope_ref[0]
        for at in range(1, 2 * epochs):
            total = total + weight_ref[e, at] * slope_ref[at]
        out_ref[e] = total
        return carry

    lax.fori_loop(0, epochs, epoch, 0)


def focus_tables(plan):
    lanes = plan.lanes
    index = np.arange(lanes)
    table = host_parts(real_form(*unit(index[:, None] * index[None, :], lanes, -1.0)))
    cosine, sine = unit(np.arange(RADIX)[:, None] * index[None, :], plan.azimuth, -1.0)
    twiddles = np.stack([cosine, sine, cosine / plan.azimuth, -sine / plan.azimuth])
    sums = np.arange(plan.azimuth // 2)[:, None] // LOOK == np.arange(plan.azimuth_looks // 2)[None, :]
    return table + (twiddles.astype(np.float32), (sums / LOOK).astype(ml_dtypes.bfloat16))


def focus(plan, fields, spectrum, finish=None):
    lanes = plan.lanes
    total = plan.epochs * plan.rows
    tables = focus_tables(plan)
    whole = pl.BlockSpec(memory_space=pltpu.VMEM)
    looked = (plan.epochs, 2, 2, plan.all_looks, plan.azimuth_looks)
    gradients = (plan.epochs, 2, plan.all_looks, plan.azimuth_looks)
    operands = [*fields, spectrum, *tables]
    in_specs = [pl.BlockSpec(memory_space=pltpu.HBM)] * len(operands)
    blocks = plan.azimuth // fields[0].shape[-1]
    scratch = [
        pltpu.VMEM((blocks, plan.epochs) + fields[0].shape[-3:], jnp.float32),
        pltpu.VMEM(spectrum.shape, jnp.float32),
        *[pltpu.VMEM(table.shape, table.dtype) for table in tables],
        pltpu.VMEM((RADIX, total, 2 * lanes), jnp.bfloat16),
        pltpu.VMEM((RADIX, total, 2 * lanes), jnp.bfloat16),
        pltpu.VMEM((RADIX, total, 2 * lanes), jnp.float32),
        pltpu.VMEM((plan.epochs + 2, 2, RADIX, plan.rows, lanes), jnp.float32),
        pltpu.VMEM((plan.epochs * 4 * plan.looks, plan.azimuth), jnp.float32),
        pltpu.SemaphoreType.DMA((blocks, 2)),
        pltpu.SemaphoreType.DMA((5,)),
    ]
    shape = looked
    if finish is not None:
        weights, before, halo = finish
        shape = gradients
        operands += [weights, before, halo]
        in_specs += [pl.BlockSpec(memory_space=pltpu.SMEM)]
        in_specs += [pl.BlockSpec(memory_space=pltpu.HBM)] * 2
        scratch += [
            pltpu.VMEM(looked, jnp.float32),
            pltpu.VMEM((2 * plan.epochs,) + gradients[1:], jnp.float32),
            pltpu.VMEM(halo.shape, jnp.float32),
            pltpu.SemaphoreType.DMA((2,)),
        ]

    def kernel(*refs):
        some, refs = refs[: len(fields)], refs[len(fields) :]

        relative = len(some) > 1
        own = (lax.axis_index("acq"), lax.axis_index("strip")) if relative else (0, 0)

        def field_at(at):
            return some[at] if relative else some[0].at[at]

        focus_kernel(plan, finish is not None, field_at, own, *refs)

    return pl.pallas_call(
        kernel,
        out_shape=jax.ShapeDtypeStruct(shape, jnp.float32),
        in_specs=in_specs,
        out_specs=whole,
        scratch_shapes=scratch,
        compiler_params=pltpu.CompilerParams(vmem_limit_bytes=FOCUS_VMEM),
        cost_estimate=pl.CostEstimate(
            flops=2 * 6 * RADIX * total * 4 * lanes * lanes,
            bytes_accessed=4 * total * 2 * plan.azimuth + 4 * 1024 * 1024,
            transcendentals=0,
        ),
        name="azimuth_focus",
    )(*operands)


def slope_kernel(plan, weight_ref, looked_ref, halo_ref, out_ref, slope_ref):
    slopes_and_sums(plan, weight_ref, looked_ref, halo_ref, out_ref, slope_ref)


def slopes_to_epochs(plan, weights, looked, halo):
    whole = pl.BlockSpec(memory_space=pltpu.VMEM)
    looks = plan.all_looks
    return pl.pallas_call(
        functools.partial(slope_kernel, plan),
        out_shape=jax.ShapeDtypeStruct(
            (plan.epochs, 2, looks, plan.azimuth_looks), jnp.float32
        ),
        in_specs=[pl.BlockSpec(memory_space=pltpu.SMEM), whole, whole],
        out_specs=whole,
        scratch_shapes=[
            pltpu.VMEM((2 * plan.epochs, 2, looks, plan.azimuth_looks), jnp.float32)
        ],
        compiler_params=pltpu.CompilerParams(vmem_limit_bytes=FOCUS_VMEM),
        cost_estimate=pl.CostEstimate(
            flops=8 * looked.size * plan.epochs, bytes_accessed=5 * looked.size, transcendentals=0
        ),
        name="slopes_to_epochs",
    )(weights, looked, halo)


def own_filter(plan, azimuth_filter):
    start = lax.axis_index("acq") * plan.owned
    own = lax.dynamic_slice_in_dim(azimuth_filter, start, plan.owned, axis=2)
    return own.reshape(2, plan.lanes, RADIX, plan.owned).transpose(0, 2, 3, 1)


def own_filter_kernel(plan, filter_any, *refs):
    *outs, block_ref, turned_ref, sem = refs
    width = block_ref.shape[-1]
    acq = lax.axis_index("acq")
    start = acq * plan.owned // width * width
    inside = acq * plan.owned % width
    move = pltpu.make_async_copy(
        filter_any.at[:, :, pl.ds(pl.multiple_of(start, width), width)], block_ref, sem
    )
    move.start()
    move.wait()
    for c in range(2):
        for d in range(RADIX):
            turned_ref[...] = block_ref[c, pl.ds(d, plan.lanes, stride=RADIX), :].T
            for number, out_ref in enumerate(outs):
                part = plan.part(number)
                start = pl.multiple_of(inside + part.start, ROWS)
                out_ref[c, d] = turned_ref[pl.ds(start, part.rows), :]


def own_filter_by_kernel(plan, azimuth_filter):
    width = 128
    return pl.pallas_call(
        functools.partial(own_filter_kernel, plan),
        out_shape=[
            jax.ShapeDtypeStruct((2, RADIX, plan.part(number).rows, plan.lanes), jnp.float32)
            for number in range(plan.parts)
        ],
        in_specs=[pl.BlockSpec(memory_space=pltpu.HBM)],
        out_specs=[pl.BlockSpec(memory_space=pltpu.VMEM)] * plan.parts,
        scratch_shapes=[
            pltpu.VMEM((2, plan.azimuth, width), jnp.float32),
            pltpu.VMEM((width, plan.lanes), jnp.float32),
            pltpu.SemaphoreType.DMA,
        ],
        compiler_params=pltpu.CompilerParams(vmem_limit_bytes=LAYOUT_VMEM),
        cost_estimate=pl.CostEstimate(flops=0, bytes_accessed=1024, transcendentals=0),
        name="own_filter",
    )(azimuth_filter)


def exchange_all(plan, block):
    shape = block.shape
    block = block.reshape((plan.strips * plan.epochs,) + shape[2:])
    received = lax.all_to_all(block, OWNERS, split_axis=0, concat_axis=0, tiled=True)
    join = max(1, plan.lanes // plan.pulses)
    received = received.reshape((plan.strips // join, join) + shape[1:])
    if join > 1:
        received = received.transpose(0, 2, 3, 4, 1, 5)
    return received.reshape(plan.strips // join, plan.epochs, 2, plan.rows, join * plan.pulses)


def partners(slots, axis):
    size = lax.axis_size(axis)
    moved = []
    for k, slot in enumerate(slots):
        moved.append(slot if k == 0 else lax.ppermute(slot, axis, [(i, i ^ k) for i in range(size)]))
    return moved


def regroup(blocks):
    count, inner = len(blocks), blocks[0].shape[0]

    def kernel(*refs):
        ins, outs = refs[:count], refs[count : count + inner]
        stage, in_sems, out_sems = refs[count + inner :]
        inward = [
            fetch(
                [
                    pltpu.make_async_copy(ins[m].at[k], stage.at[k, m], in_sems.at[k, m])
                    for m in range(count)
                ]
            )
            for k in range(inner)
        ]
        outward = []
        for k in range(inner):
            for move in inward[k]:
                move.wait()
            outward += fetch([pltpu.make_async_copy(stage.at[k], outs[k], out_sems.at[k])])
        for move in outward:
            move.wait()

    slab = (count,) + blocks[0].shape[1:]
    place = pl.BlockSpec(memory_space=pltpu.HBM)
    return pl.pallas_call(
        kernel,
        out_shape=[jax.ShapeDtypeStruct(slab, jnp.float32)] * inner,
        in_specs=[place] * count,
        out_specs=[place] * inner,
        scratch_shapes=[
            pltpu.VMEM((inner,) + slab, jnp.float32),
            pltpu.SemaphoreType.DMA((inner, count)),
            pltpu.SemaphoreType.DMA((inner,)),
        ],
        compiler_params=pltpu.CompilerParams(vmem_limit_bytes=LAYOUT_VMEM),
        cost_estimate=pl.CostEstimate(flops=0, bytes_accessed=1024, transcendentals=0),
        name="regroup",
    )(*blocks)


def all_weights(pair_mask, inversion):
    lags = jnp.array([1, 2], dtype=jnp.int32)
    usable = pair_mask[0].astype(jnp.float32) * (lax.axis_index("acq") >= lags).astype(jnp.float32)
    weights = lax.all_gather(inversion[:, 0, :] * usable[None, :], "acq", axis=1, tiled=False)
    return weights.reshape(weights.shape[0], -1)


def per_device(raw_echoes, range_filter, azimuth_filter, pair_mask, inversion):
    strips, epochs = lax.axis_size("strip"), lax.axis_size("acq")
    plan = Plan(strips, epochs, raw_echoes.shape[2], raw_echoes.shape[3])

    raw = raw_echoes[0]
    small, big = plan.part(0), plan.part(1)
    block = compress(big, False, range_filter, raw)
    if plan.parts > 1:
        range_filter, block = lax.optimization_barrier((range_filter, block))
        other = compress(small, True, range_filter, raw)
        *other, azimuth_filter = lax.optimization_barrier((*other, azimuth_filter))
        other_spectrum, spectrum = own_filter_by_kernel(plan, azimuth_filter)
        field = exchange_all(big, block)
        other = partners(other, "acq")
        *other, other_spectrum = lax.optimization_barrier((*other, other_spectrum))
        other = partners(regroup(other), "strip")
        before = focus(small, other, other_spectrum)
        before, pair_mask, inversion = lax.optimization_barrier((before, pair_mask, inversion))
    else:
        before = focus(plan, [exchange_all(plan, block)], own_filter(plan, azimuth_filter))
    weights = all_weights(pair_mask, inversion)

    owners = strips * epochs
    device = [i % epochs * strips + i // epochs for i in range(owners)]
    halo = lax.ppermute(
        before[:, :, :, :1, :],
        ("acq", "strip"),
        [(device[i], device[i - 1]) for i in range(1, owners)],
    )
    if plan.parts > 1:
        gradients = focus(big, [field], spectrum, (weights, before, halo))
    else:
        gradients = slopes_to_epochs(plan, weights, before, halo)
    gathered = lax.all_to_all(gradients, "acq", split_axis=0, concat_axis=0, tiled=True)
    gathered = gathered.reshape(epochs, 2, plan.all_looks, plan.azimuth_looks)
    return gathered.swapaxes(0, 1).reshape(1, 2, -1, plan.azimuth_looks)


def solution(mesh):
    return jax.shard_map(
        per_device,
        mesh=mesh,
        in_specs=(
            P("acq", None, "strip", None),
            P(),
            P(None, None, "strip"),
            P("acq", None),
            P(None, "acq", None),
        ),
        out_specs=P("acq", None, "strip", None),
        check_vma=False,
    )
```

```python
import copy
import functools
import math

import jax
import jax.numpy as jnp
import ml_dtypes
import numpy as np
from jax import lax
from jax.experimental import pallas as pl
from jax.experimental.pallas import tpu as pltpu
from jax.sharding import PartitionSpec as P

LOOK = 4
RADIX = 8
ROWS = 8
RANGE_VMEM = 63 * 1024 * 1024
LAYOUT_VMEM = 8 * 1024 * 1024
FOCUS_VMEM = 32 * 1024 * 1024
OWNERS = ("strip", "acq")


def add(left, right):
    return (left[0] + right[0], left[1] + right[1])


def sub(left, right):
    return (left[0] - right[0], left[1] - right[1])


def times(value, cosine, sine):
    return (value[0] * cosine - value[1] * sine, value[0] * sine + value[1] * cosine)


def turn(value, sign):
    if sign > 0:
        return (-value[1], value[0])
    return (value[1], -value[0])


def dft4(x0, x1, x2, x3, sign):
    a, b = add(x0, x2), sub(x0, x2)
    c, d = add(x1, x3), turn(sub(x1, x3), sign)
    return [add(a, c), add(b, d), sub(a, c), sub(b, d)]


def dft8(x, sign):
    even = dft4(x[0], x[2], x[4], x[6], sign)
    odd = dft4(x[1], x[3], x[5], x[7], sign)
    half = math.sqrt(0.5)
    o1, o3 = odd[1], odd[3]
    t1 = add(o1, turn(o1, sign))
    t3 = sub(turn(o3, sign), o3)
    odd = [
        odd[0],
        (t1[0] * half, t1[1] * half),
        turn(odd[2], sign),
        (t3[0] * half, t3[1] * half),
    ]
    return [add(e, o) for e, o in zip(even, odd)] + [sub(e, o) for e, o in zip(even, odd)]


def two_parts(value):
    high = value.astype(jnp.bfloat16)
    low = (value - high.astype(jnp.float32)).astype(jnp.bfloat16)
    return high, low


def three_products(left_high, left_low, right_high, right_low, contract):
    def product(left, right):
        return lax.dot_general(
            left, right, (contract, ((), ())), preferred_element_type=jnp.float32
        )

    return (
        product(left_high, right_high)
        + product(left_high, right_low)
        + product(left_low, right_high)
    )


def host_parts(table):
    table = np.asarray(table, np.float64)
    high = table.astype(np.float32).astype(ml_dtypes.bfloat16)
    low = (table - high.astype(np.float64)).astype(np.float32).astype(ml_dtypes.bfloat16)
    return high, low


def unit(exponent, size, sign):
    angle = sign * 2.0 * np.pi / size * (exponent % size)
    return np.cos(angle), np.sin(angle)


def real_form(cosine, sine):
    top = np.concatenate([cosine, sine], axis=-1)
    bottom = np.concatenate([-sine, cosine], axis=-1)
    return np.concatenate([top, bottom], axis=-2)


class Plan:
    def __init__(self, strips, epochs, pulses, samples):
        self.strips, self.epochs = strips, epochs
        self.pulses, self.samples = pulses, samples
        self.azimuth = pulses * strips
        self.base = samples // RADIX
        self.owned = samples // (strips * epochs)
        even = all(size & (size - 1) == 0 for size in (strips, epochs))
        self.parts = 2 if even and self.owned in (64, 128) else 1
        self.start, self.rows = 0, self.owned
        self.looks = self.rows // LOOK
        self.all_looks = self.looks
        self.blocks = self.base // self.owned
        self.lanes = self.azimuth // RADIX
        self.azimuth_looks = self.azimuth // LOOK

    def part(self, number):
        if self.parts == 1:
            return self
        own = copy.copy(self)
        size = self.owned // 4
        own.start, own.rows = (0, 3 * size) if number == 0 else (3 * size, size)
        own.looks = own.rows // LOOK
        return own

    def tile_shift(self, block, tile):
        return block * self.owned + self.start + tile * ROWS


def lag_tables(plan):
    base, samples = plan.base, plan.samples
    index = np.arange(base)
    table = host_parts(
        np.concatenate(unit(index[:, None] * index[None, :], samples, -1.0), axis=1) / samples
    )
    block = np.arange(RADIX)[:, None]
    turns = np.stack(
        unit(block * index[None, :], RADIX, -1.0)
        + tuple(np.broadcast_to(part, (RADIX, base)) for part in unit(block, RADIX, 1.0))
    )
    return table + (turns.astype(np.float32),)


def lag_vectors(plan, filter_ref, table_high, table_low, turn_ref):
    base = plan.base
    lane = lax.broadcasted_iota(jnp.int32, (RADIX, base), 1)
    chosen = lane % RADIX == lax.broadcasted_iota(jnp.int32, (RADIX, base), 0)
    rows = []
    for c in range(2):
        for e in range(RADIX):
            block = jnp.broadcast_to(filter_ref[c : c + 1, e * base : (e + 1) * base], (RADIX, base))
            rows.append(jnp.where(chosen, block, 0.0))
    high, low = two_parts(jnp.concatenate(rows, axis=0))
    sums = three_products(high, low, table_high[...], table_low[...], ((1,), (0,)))
    real, imag = 0.0, 0.0
    for e in range(RADIX):
        by_real = sums[e * RADIX : (e + 1) * RADIX]
        by_imag = sums[(RADIX + e) * RADIX : (RADIX + e + 1) * RADIX]
        part_real = by_real[:, :base] - by_imag[:, base:]
        part_imag = by_real[:, base:] + by_imag[:, :base]
        cosine, sine = turn_ref[0, e : e + 1, :], turn_ref[1, e : e + 1, :]
        real = real + part_real * cosine - part_imag * sine
        imag = imag + part_real * sine + part_imag * cosine
    cosine, sine = turn_ref[2], turn_ref[3]
    return (
        jnp.concatenate([real, real * cosine - imag * sine], axis=1),
        jnp.concatenate([imag, real * sine + imag * cosine], axis=1),
    )


def fetch(copies):
    for move in copies:
        move.start()
    return copies


def compress_kernel(
    plan, relative, filter_ref, high_any, low_any, turn_any, raw_ref, *refs
):
    outs = refs[: plan.epochs if relative else 1]
    (
        table_high, table_low, turn_ref, raw, t_high, t_low, y_high, y_low, z_ref, sems, table_sems,
    ) = refs[len(outs) :][:11]
    out_ref = refs[-2] if relative else outs[0]
    base, blocks = plan.base, plan.blocks
    tiles = plan.rows // ROWS
    chunk = blocks * plan.rows
    pieces = sems.shape[0]
    piece = plan.pulses // pieces

    def raw_copy(at):
        rows = pl.ds(at * piece, piece)
        return pltpu.make_async_copy(raw_ref.at[:, rows, :], raw.at[:, rows, :], sems.at[at])

    tables = fetch(
        [
            pltpu.make_async_copy(source, target, table_sems.at[at])
            for at, (source, target) in enumerate(
                ((high_any, table_high), (low_any, table_low), (turn_any, turn_ref))
            )
        ]
    )
    fetch([raw_copy(at) for at in range(pieces)])
    def spread_pulses(at, carry):
        rows = pl.ds(pl.multiple_of(at * 2 * ROWS, 2 * ROWS), 2 * ROWS)
        x = [
            tuple(raw[c, rows, a * base : (a + 1) * base] for c in range(2))
            for a in range(RADIX)
        ]
        for d, value in enumerate(dft8(x, -1.0)):
            for c in range(2):
                high, low = two_parts(value[c])
                y_high[d, rows, c * base : (c + 1) * base] = high
                y_low[d, rows, c * base : (c + 1) * base] = low
        return carry

    steps = piece // (2 * ROWS)
    for at in range(pieces):
        raw_copy(at).wait()
        lax.fori_loop(at * steps, (at + 1) * steps, spread_pulses, 0)

    for move in tables:
        move.wait()
    lags = lag_vectors(plan, filter_ref, table_high, table_low, turn_ref)

    for d in range(RADIX):
        spread = [
            pltpu.roll(
                jnp.broadcast_to(lag[d : d + 1, :], (ROWS, 2 * base)),
                0,
                1,
                stride=1,
                stride_axis=0,
            )
            for lag in lags
        ]
        for pair in range(blocks * tiles // 2):
            real, imag = [], []
            for at in (2 * pair, 2 * pair + 1):
                shift = plan.tile_shift(at // tiles, at % tiles)
                real.append(pltpu.roll(spread[0], shift, 1)[:, :base])
                imag.append(pltpu.roll(spread[1], shift, 1)[:, :base])
            real_high, real_low = two_parts(jnp.concatenate(real, axis=0))
            imag_high, imag_low = two_parts(jnp.concatenate(imag, axis=0))
            top = pl.ds(pair * 2 * ROWS, 2 * ROWS)
            bottom = pl.ds(chunk + pair * 2 * ROWS, 2 * ROWS)
            t_high[d, top, :base] = real_high
            t_high[d, top, base:] = -imag_high
            t_high[d, bottom, :base] = imag_high
            t_high[d, bottom, base:] = real_high
            t_low[d, top, :base] = real_low
            t_low[d, top, base:] = -imag_low
            t_low[d, bottom, :base] = imag_low
            t_low[d, bottom, base:] = real_low
        z_ref[d] = three_products(t_high[d], t_low[d], y_high[d], y_low[d], ((1,), (1,)))

    for block in range(blocks):
        for tile in range(tiles):
            top = (block * tiles + tile) * ROWS
            z = [
                (z_ref[d, top : top + ROWS, :], z_ref[d, chunk + top : chunk + top + ROWS, :])
                for d in range(RADIX)
            ]
            for a, value in enumerate(dft8(z, 1.0)):
                for c in range(2):
                    strip, owner = divmod(a * blocks + block, plan.epochs)
                    rows = slice(tile * ROWS, (tile + 1) * ROWS)
                    if relative:
                        place = owner ^ lax.axis_index("acq"), strip ^ lax.axis_index("strip")
                    else:
                        place = strip, owner
                    out_ref[place[0], place[1], c, rows, :] = value[c]
    if relative:
        copies = fetch(
            [
                pltpu.make_async_copy(out_ref.at[m], out, refs[-1].at[m])
                for m, out in enumerate(outs)
            ]
        )
        for move in copies:
            move.wait()


def compress(plan, relative, range_filter, raw):
    chunk = plan.blocks * plan.rows
    whole = pl.BlockSpec(memory_space=pltpu.VMEM)
    bytes_moved = 8 * raw.size
    tables = lag_tables(plan)
    slab = (2, plan.rows, plan.pulses)
    shape = (plan.strips,) + (slab if relative else (plan.epochs,) + slab)
    scratch, out_specs = [], whole
    if relative:
        out_specs = [pl.BlockSpec(memory_space=pltpu.HBM)] * plan.epochs
        scratch = [
            pltpu.VMEM((plan.epochs,) + shape, jnp.float32),
            pltpu.SemaphoreType.DMA((plan.epochs,)),
        ]
    shape = jax.ShapeDtypeStruct(shape, jnp.float32)
    return pl.pallas_call(
        functools.partial(compress_kernel, plan, relative),
        out_shape=[shape] * plan.epochs if relative else shape,
        in_specs=[whole] + [pl.BlockSpec(memory_space=pltpu.HBM)] * 4,
        out_specs=out_specs,
        scratch_shapes=[
            *[pltpu.VMEM(table.shape, table.dtype) for table in tables],
            pltpu.VMEM(raw.shape, jnp.float32),
            pltpu.VMEM((RADIX, 2 * chunk, 2 * plan.base), jnp.bfloat16),
            pltpu.VMEM((RADIX, 2 * chunk, 2 * plan.base), jnp.bfloat16),
            pltpu.VMEM((RADIX, plan.pulses, 2 * plan.base), jnp.bfloat16),
            pltpu.VMEM((RADIX, plan.pulses, 2 * plan.base), jnp.bfloat16),
            pltpu.VMEM((RADIX, 2 * chunk, plan.pulses), jnp.float32),
            pltpu.SemaphoreType.DMA((4,)),
            pltpu.SemaphoreType.DMA((3,)),
            *scratch,
        ],
        compiler_params=pltpu.CompilerParams(vmem_limit_bytes=RANGE_VMEM),
        cost_estimate=pl.CostEstimate(
            flops=6 * RADIX * 4 * chunk * plan.base * plan.pulses,
            bytes_accessed=bytes_moved,
            transcendentals=0,
        ),
        name="range_compress",
    )(range_filter, *tables, raw)


def focus_kernel(plan, final, field_at, own, *refs):
    filter_any, high_any, low_any, twiddle_any, sum_any = refs[:5]
    if final:
        weight_ref, before_any, halo_any, out_ref = refs[5:9]
    else:
        (out_ref,) = refs[5:6]
    scratch = refs[9 if final else 6 :]
    (
        field_ref, filter_ref, table_high, table_low, twiddle_ref, sum_ref,
        y_high, y_low, z_ref, scene_ref, product_ref, field_sems, table_sems,
    ) = scratch[:13]
    rows, lanes, epochs, looks = plan.rows, plan.lanes, plan.epochs, plan.looks
    step = 2 * ROWS
    group = max(1, step // rows)
    per_block = field_ref.shape[-1] // lanes

    half = epochs // 2
    fields = [
        [
            pltpu.make_async_copy(
                field_at(at).at[pl.ds(side * half, half)],
                field_ref.at[at, pl.ds(side * half, half)],
                field_sems.at[at, side],
            )
            for at in range(field_ref.shape[0])
        ]
        for side in range(2)
    ]
    tables = [
        pltpu.make_async_copy(source, target, table_sems.at[at])
        for at, (source, target) in enumerate(
            (
                (twiddle_any, twiddle_ref),
                (high_any, table_high),
                (low_any, table_low),
                (filter_any, filter_ref),
                (sum_any, sum_ref),
            )
        )
    ]
    fetch(tables[:1])
    for copies in fields:
        fetch(copies)
    fetch(tables[1:])
    if final:
        looked_ref, slope_ref, halo_ref, late_sems = scratch[13:]
        late = fetch(
            [
                pltpu.make_async_copy(before_any, looked_ref, late_sems.at[0]),
                pltpu.make_async_copy(halo_any, halo_ref, late_sems.at[1]),
            ]
        )
    tables[0].wait()

    def rows_of(strip, slot, c, top, start):
        some = [
            field_ref[strip, slot + g, c, top : top + min(rows, step), start : start + lanes]
            for g in range(group)
        ]
        return some[0] if group == 1 else jnp.concatenate(some, axis=0)

    def forward(at, carry):
        slot = at * group
        j = slot ^ own[0]
        for top in range(0, rows, step):
            x = []
            for a in range(RADIX):
                strip, start = a // per_block, a % per_block * lanes
                x.append(tuple(rows_of(strip ^ own[1], slot, c, top, start) for c in range(2)))
            at = pl.ds(pl.multiple_of(j * rows + top, step), step)
            for d, value in enumerate(dft8(x, -1.0)):
                if d > 0:
                    value = times(value, twiddle_ref[0, d : d + 1, :], twiddle_ref[1, d : d + 1, :])
                for c in range(2):
                    high, low = two_parts(value[c])
                    y_high[d, at, c * lanes : (c + 1) * lanes] = high
                    y_low[d, at, c * lanes : (c + 1) * lanes] = low
        return carry

    for side, copies in enumerate(fields):
        for move in copies:
            move.wait()
        lax.fori_loop(side * half // group, (side + 1) * half // group, forward, 0)
    for move in tables[1:]:
        move.wait()

    each = epochs * rows
    per = max(1, 1024 // each)
    while RADIX % per:
        per -= 1
    for d in range(0, RADIX, per):
        some = slice(d, d + per)
        spectrum = three_products(
            y_high[some].reshape(per * each, 2 * lanes),
            y_low[some].reshape(per * each, 2 * lanes),
            table_high[...],
            table_low[...],
            ((1,), (0,)),
        ).reshape(per, epochs, rows, 2 * lanes)
        real, imag = spectrum[..., :lanes], spectrum[..., lanes:]
        by_real, by_imag = filter_ref[0, some][:, None], filter_ref[1, some][:, None]
        spectrum = jnp.concatenate(
            [real * by_real - imag * by_imag, real * by_imag + imag * by_real], axis=3
        )
        high, low = two_parts(spectrum.reshape(per * each, 2 * lanes))
        z_ref[some] = three_products(
            high, low, table_high[...], table_low[...], ((1,), (1,))
        ).reshape(per, each, 2 * lanes)

    scene_ref[0] = jnp.zeros_like(scene_ref[0])
    scene_ref[1] = jnp.zeros_like(scene_ref[1])

    def backward(j, carry):
        for top in range(0, rows, ROWS):
            at = pl.ds(pl.multiple_of(j * rows + top, ROWS), ROWS)
            z = [
                times(
                    tuple(z_ref[d, at, c * lanes : (c + 1) * lanes] for c in range(2)),
                    twiddle_ref[2, d : d + 1, :],
                    twiddle_ref[3, d : d + 1, :],
                )
                for d in range(RADIX)
            ]
            for a, value in enumerate(dft8(z, 1.0)):
                for c in range(2):
                    scene_ref[j + 2, c, a, top : top + ROWS, :] = value[c]
        return carry

    lax.fori_loop(0, epochs, backward, 0)

    def interfere(j, carry):
        for a in range(RADIX):
            columns = pl.ds(a * lanes, lanes)
            sums = [0.0] * 4
            for q in range(LOOK):
                rows_at = pl.ds(q, looks, stride=LOOK)
                later, *earlier = [
                    tuple(scene_ref[j + 2 - lag, c, a, rows_at, :] for c in range(2))
                    for lag in range(3)
                ]
                for at, value in enumerate(earlier):
                    sums[2 * at] += value[0] * later[0] + value[1] * later[1]
                    sums[2 * at + 1] += value[1] * later[0] - value[0] * later[1]
            place = pl.ds(pl.multiple_of(j * 4 * looks, ROWS), 4 * looks)
            product_ref[place, columns] = jnp.concatenate(sums, axis=0)
        return carry

    lax.fori_loop(0, epochs, interfere, 0)

    products = product_ref[...]
    high, low = two_parts(products)
    weights = sum_ref[...]
    looked = []
    for start in range(0, plan.azimuth, weights.shape[0]):
        columns = slice(start, start + weights.shape[0])
        looked.append(
            jnp.dot(high[:, columns], weights, preferred_element_type=jnp.float32)
            + jnp.dot(low[:, columns], weights, preferred_element_type=jnp.float32)
        )
    looked = jnp.concatenate(looked, axis=1)
    looked = looked.reshape(epochs, 2, 2, looks, plan.azimuth_looks)
    if final:
        for move in late:
            move.wait()
        looked_ref[:, :, :, plan.all_looks - looks :, :] = looked
        slopes_and_sums(plan, weight_ref, looked_ref, halo_ref, out_ref, slope_ref)
    else:
        out_ref[:, :, :, :looks, :] = looked
        if looks < plan.all_looks:
            rest = (epochs, 2, 2, plan.all_looks - looks, plan.azimuth_looks)
            out_ref[:, :, :, looks:, :] = jnp.zeros(rest, jnp.float32)


def slopes_and_sums(plan, weight_ref, looked_ref, halo_ref, out_ref, slope_ref):
    epochs = plan.epochs
    columns = plan.azimuth_looks
    inner = lax.broadcasted_iota(jnp.int32, (plan.all_looks, columns), 1) < columns - 1

    def slopes(at, carry):
        j, lag = at // 2, at % 2
        real, imag = looked_ref[j, lag, 0], looked_ref[j, lag, 1]
        next_real = pltpu.roll(real, columns - 1, 1)
        next_imag = pltpu.roll(imag, columns - 1, 1)
        slope_ref[at, 0] = jnp.where(inner, next_imag * real - next_real * imag, 0.0)
        next_real = jnp.concatenate([real[1:], halo_ref[j, lag, 0]], axis=0)
        next_imag = jnp.concatenate([imag[1:], halo_ref[j, lag, 1]], axis=0)
        slope_ref[at, 1] = next_imag * real - next_real * imag
        return carry

    lax.fori_loop(0, 2 * epochs, slopes, 0)

    def epoch(e, carry):
        total = weight_ref[e, 0] * slope_ref[0]
        for at in range(1, 2 * epochs):
            total = total + weight_ref[e, at] * slope_ref[at]
        out_ref[e] = total
        return carry

    lax.fori_loop(0, epochs, epoch, 0)


def focus_tables(plan):
    lanes = plan.lanes
    index = np.arange(lanes)
    table = host_parts(real_form(*unit(index[:, None] * index[None, :], lanes, -1.0)))
    cosine, sine = unit(np.arange(RADIX)[:, None] * index[None, :], plan.azimuth, -1.0)
    twiddles = np.stack([cosine, sine, cosine / plan.azimuth, -sine / plan.azimuth])
    sums = np.arange(plan.azimuth // 2)[:, None] // LOOK == np.arange(plan.azimuth_looks // 2)[None, :]
    return table + (twiddles.astype(np.float32), (sums / LOOK).astype(ml_dtypes.bfloat16))


def focus(plan, fields, spectrum, finish=None):
    lanes = plan.lanes
    total = plan.epochs * plan.rows
    tables = focus_tables(plan)
    whole = pl.BlockSpec(memory_space=pltpu.VMEM)
    looked = (plan.epochs, 2, 2, plan.all_looks, plan.azimuth_looks)
    gradients = (plan.epochs, 2, plan.all_looks, plan.azimuth_looks)
    operands = [*fields, spectrum, *tables]
    in_specs = [pl.BlockSpec(memory_space=pltpu.HBM)] * len(operands)
    blocks = plan.azimuth // fields[0].shape[-1]
    scratch = [
        pltpu.VMEM((blocks, plan.epochs) + fields[0].shape[-3:], jnp.float32),
        pltpu.VMEM(spectrum.shape, jnp.float32),
        *[pltpu.VMEM(table.shape, table.dtype) for table in tables],
        pltpu.VMEM((RADIX, total, 2 * lanes), jnp.bfloat16),
        pltpu.VMEM((RADIX, total, 2 * lanes), jnp.bfloat16),
        pltpu.VMEM((RADIX, total, 2 * lanes), jnp.float32),
        pltpu.VMEM((plan.epochs + 2, 2, RADIX, plan.rows, lanes), jnp.float32),
        pltpu.VMEM((plan.epochs * 4 * plan.looks, plan.azimuth), jnp.float32),
        pltpu.SemaphoreType.DMA((blocks, 2)),
        pltpu.SemaphoreType.DMA((5,)),
    ]
    shape = looked
    if finish is not None:
        weights, before, halo = finish
        shape = gradients
        operands += [weights, before, halo]
        in_specs += [pl.BlockSpec(memory_space=pltpu.SMEM)]
        in_specs += [pl.BlockSpec(memory_space=pltpu.HBM)] * 2
        scratch += [
            pltpu.VMEM(looked, jnp.float32),
            pltpu.VMEM((2 * plan.epochs,) + gradients[1:], jnp.float32),
            pltpu.VMEM(halo.shape, jnp.float32),
            pltpu.SemaphoreType.DMA((2,)),
        ]

    def kernel(*refs):
        some, refs = refs[: len(fields)], refs[len(fields) :]

        relative = len(some) > 1
        own = (lax.axis_index("acq"), lax.axis_index("strip")) if relative else (0, 0)

        def field_at(at):
            return some[at] if relative else some[0].at[at]

        focus_kernel(plan, finish is not None, field_at, own, *refs)

    return pl.pallas_call(
        kernel,
        out_shape=jax.ShapeDtypeStruct(shape, jnp.float32),
        in_specs=in_specs,
        out_specs=whole,
        scratch_shapes=scratch,
        compiler_params=pltpu.CompilerParams(vmem_limit_bytes=FOCUS_VMEM),
        cost_estimate=pl.CostEstimate(
            flops=2 * 6 * RADIX * total * 4 * lanes * lanes,
            bytes_accessed=4 * total * 2 * plan.azimuth + 4 * 1024 * 1024,
            transcendentals=0,
        ),
        name="azimuth_focus",
    )(*operands)


def slope_kernel(plan, weight_ref, looked_ref, halo_ref, out_ref, slope_ref):
    slopes_and_sums(plan, weight_ref, looked_ref, halo_ref, out_ref, slope_ref)


def slopes_to_epochs(plan, weights, looked, halo):
    whole = pl.BlockSpec(memory_space=pltpu.VMEM)
    looks = plan.all_looks
    return pl.pallas_call(
        functools.partial(slope_kernel, plan),
        out_shape=jax.ShapeDtypeStruct(
            (plan.epochs, 2, looks, plan.azimuth_looks), jnp.float32
        ),
        in_specs=[pl.BlockSpec(memory_space=pltpu.SMEM), whole, whole],
        out_specs=whole,
        scratch_shapes=[
            pltpu.VMEM((2 * plan.epochs, 2, looks, plan.azimuth_looks), jnp.float32)
        ],
        compiler_params=pltpu.CompilerParams(vmem_limit_bytes=FOCUS_VMEM),
        cost_estimate=pl.CostEstimate(
            flops=8 * looked.size * plan.epochs, bytes_accessed=5 * looked.size, transcendentals=0
        ),
        name="slopes_to_epochs",
    )(weights, looked, halo)


def own_filter(plan, azimuth_filter):
    start = lax.axis_index("acq") * plan.owned
    own = lax.dynamic_slice_in_dim(azimuth_filter, start, plan.owned, axis=2)
    return own.reshape(2, plan.lanes, RADIX, plan.owned).transpose(0, 2, 3, 1)


def own_filter_kernel(plan, filter_any, *refs):
    *outs, block_ref, turned_ref, sem = refs
    width = block_ref.shape[-1]
    acq = lax.axis_index("acq")
    start = acq * plan.owned // width * width
    inside = acq * plan.owned % width
    move = pltpu.make_async_copy(
        filter_any.at[:, :, pl.ds(pl.multiple_of(start, width), width)], block_ref, sem
    )
    move.start()
    move.wait()
    for c in range(2):
        for d in range(RADIX):
            turned_ref[...] = block_ref[c, pl.ds(d, plan.lanes, stride=RADIX), :].T
            for number, out_ref in enumerate(outs):
                part = plan.part(number)
                start = pl.multiple_of(inside + part.start, ROWS)
                out_ref[c, d] = turned_ref[pl.ds(start, part.rows), :]


def own_filter_by_kernel(plan, azimuth_filter):
    width = 128
    return pl.pallas_call(
        functools.partial(own_filter_kernel, plan),
        out_shape=[
            jax.ShapeDtypeStruct((2, RADIX, plan.part(number).rows, plan.lanes), jnp.float32)
            for number in range(plan.parts)
        ],
        in_specs=[pl.BlockSpec(memory_space=pltpu.HBM)],
        out_specs=[pl.BlockSpec(memory_space=pltpu.VMEM)] * plan.parts,
        scratch_shapes=[
            pltpu.VMEM((2, plan.azimuth, width), jnp.float32),
            pltpu.VMEM((width, plan.lanes), jnp.float32),
            pltpu.SemaphoreType.DMA,
        ],
        compiler_params=pltpu.CompilerParams(vmem_limit_bytes=LAYOUT_VMEM),
        cost_estimate=pl.CostEstimate(flops=0, bytes_accessed=1024, transcendentals=0),
        name="own_filter",
    )(azimuth_filter)


def exchange_all(plan, block):
    shape = block.shape
    block = block.reshape((plan.strips * plan.epochs,) + shape[2:])
    received = lax.all_to_all(block, OWNERS, split_axis=0, concat_axis=0, tiled=True)
    join = max(1, plan.lanes // plan.pulses)
    received = received.reshape((plan.strips // join, join) + shape[1:])
    if join > 1:
        received = received.transpose(0, 2, 3, 4, 1, 5)
    return received.reshape(plan.strips // join, plan.epochs, 2, plan.rows, join * plan.pulses)


def partners(slots, axis):
    size = lax.axis_size(axis)
    moved = []
    for k, slot in enumerate(slots):
        moved.append(slot if k == 0 else lax.ppermute(slot, axis, [(i, i ^ k) for i in range(size)]))
    return moved


def regroup(blocks):
    count, inner = len(blocks), blocks[0].shape[0]

    def kernel(*refs):
        ins, outs = refs[:count], refs[count : count + inner]
        stage, in_sems, out_sems = refs[count + inner :]
        inward = [
            fetch(
                [
                    pltpu.make_async_copy(ins[m].at[k], stage.at[k, m], in_sems.at[k, m])
                    for m in range(count)
                ]
            )
            for k in range(inner)
        ]
        outward = []
        for k in range(inner):
            for move in inward[k]:
                move.wait()
            outward += fetch([pltpu.make_async_copy(stage.at[k], outs[k], out_sems.at[k])])
        for move in outward:
            move.wait()

    slab = (count,) + blocks[0].shape[1:]
    place = pl.BlockSpec(memory_space=pltpu.HBM)
    return pl.pallas_call(
        kernel,
        out_shape=[jax.ShapeDtypeStruct(slab, jnp.float32)] * inner,
        in_specs=[place] * count,
        out_specs=[place] * inner,
        scratch_shapes=[
            pltpu.VMEM((inner,) + slab, jnp.float32),
            pltpu.SemaphoreType.DMA((inner, count)),
            pltpu.SemaphoreType.DMA((inner,)),
        ],
        compiler_params=pltpu.CompilerParams(vmem_limit_bytes=LAYOUT_VMEM),
        cost_estimate=pl.CostEstimate(flops=0, bytes_accessed=1024, transcendentals=0),
        name="regroup",
    )(*blocks)


def all_weights(pair_mask, inversion):
    lags = jnp.array([1, 2], dtype=jnp.int32)
    usable = pair_mask[0].astype(jnp.float32) * (lax.axis_index("acq") >= lags).astype(jnp.float32)
    weights = lax.all_gather(inversion[:, 0, :] * usable[None, :], "acq", axis=1, tiled=False)
    return weights.reshape(weights.shape[0], -1)


def per_device(raw_echoes, range_filter, azimuth_filter, pair_mask, inversion):
    strips, epochs = lax.axis_size("strip"), lax.axis_size("acq")
    plan = Plan(strips, epochs, raw_echoes.shape[2], raw_echoes.shape[3])

    raw = raw_echoes[0]
    big, small = plan.part(0), plan.part(1)
    block = compress(big, False, range_filter, raw)
    if plan.parts > 1:
        range_filter, block = lax.optimization_barrier((range_filter, block))
        other = compress(small, True, range_filter, raw)
        *other, azimuth_filter, pair_mask, inversion = lax.optimization_barrier(
            (*other, azimuth_filter, pair_mask, inversion)
        )
        weights = all_weights(pair_mask, inversion)
        spectrum, other_spectrum = own_filter_by_kernel(plan, azimuth_filter)
        field = exchange_all(big, block)
        other = partners(other, "acq")
        *other, spectrum, weights = lax.optimization_barrier((*other, spectrum, weights))
        other = partners(regroup(other), "strip")
    else:
        weights = all_weights(pair_mask, inversion)
        spectrum = own_filter(plan, azimuth_filter)
        field = exchange_all(plan, block)
    before = focus(big, [field], spectrum)

    owners = strips * epochs
    device = [i % epochs * strips + i // epochs for i in range(owners)]
    halo = lax.ppermute(
        before[:, :, :, :1, :],
        ("acq", "strip"),
        [(device[i], device[i - 1]) for i in range(1, owners)],
    )
    if plan.parts > 1:
        gradients = focus(small, other, other_spectrum, (weights, before, halo))
    else:
        gradients = slopes_to_epochs(plan, weights, before, halo)
    gathered = lax.all_to_all(gradients, "acq", split_axis=0, concat_axis=0, tiled=True)
    gathered = gathered.reshape(epochs, 2, plan.all_looks, plan.azimuth_looks)
    return gathered.swapaxes(0, 1).reshape(1, 2, -1, plan.azimuth_looks)


def solution(mesh):
    return jax.shard_map(
        per_device,
        mesh=mesh,
        in_specs=(
            P("acq", None, "strip", None),
            P(),
            P(None, None, "strip"),
            P("acq", None),
            P(None, "acq", None),
        ),
        out_specs=P("acq", None, "strip", None),
        check_vma=False,
    )
```

```python
import copy
import functools
import math

import jax
import jax.numpy as jnp
import ml_dtypes
import numpy as np
from jax import lax
from jax.experimental import pallas as pl
from jax.experimental.pallas import tpu as pltpu
from jax.sharding import PartitionSpec as P

LOOK = 4
RADIX = 8
ROWS = 8
RANGE_VMEM = 63 * 1024 * 1024
LAYOUT_VMEM = 8 * 1024 * 1024
FOCUS_VMEM = 32 * 1024 * 1024
OWNERS = ("strip", "acq")


def add(left, right):
    return (left[0] + right[0], left[1] + right[1])


def sub(left, right):
    return (left[0] - right[0], left[1] - right[1])


def times(value, cosine, sine):
    return (value[0] * cosine - value[1] * sine, value[0] * sine + value[1] * cosine)


def turn(value, sign):
    if sign > 0:
        return (-value[1], value[0])
    return (value[1], -value[0])


def dft4(x0, x1, x2, x3, sign):
    a, b = add(x0, x2), sub(x0, x2)
    c, d = add(x1, x3), turn(sub(x1, x3), sign)
    return [add(a, c), add(b, d), sub(a, c), sub(b, d)]


def dft8(x, sign):
    even = dft4(x[0], x[2], x[4], x[6], sign)
    odd = dft4(x[1], x[3], x[5], x[7], sign)
    half = math.sqrt(0.5)
    o1, o3 = odd[1], odd[3]
    t1 = add(o1, turn(o1, sign))
    t3 = sub(turn(o3, sign), o3)
    odd = [
        odd[0],
        (t1[0] * half, t1[1] * half),
        turn(odd[2], sign),
        (t3[0] * half, t3[1] * half),
    ]
    return [add(e, o) for e, o in zip(even, odd)] + [sub(e, o) for e, o in zip(even, odd)]


def two_parts(value):
    high = value.astype(jnp.bfloat16)
    low = (value - high.astype(jnp.float32)).astype(jnp.bfloat16)
    return high, low


def three_products(left_high, left_low, right_high, right_low, contract):
    def product(left, right):
        return lax.dot_general(
            left, right, (contract, ((), ())), preferred_element_type=jnp.float32
        )

    return (
        product(left_high, right_high)
        + product(left_high, right_low)
        + product(left_low, right_high)
    )


def host_parts(table):
    table = np.asarray(table, np.float64)
    high = table.astype(np.float32).astype(ml_dtypes.bfloat16)
    low = (table - high.astype(np.float64)).astype(np.float32).astype(ml_dtypes.bfloat16)
    return high, low


def unit(exponent, size, sign):
    angle = sign * 2.0 * np.pi / size * (exponent % size)
    return np.cos(angle), np.sin(angle)


def real_form(cosine, sine):
    top = np.concatenate([cosine, sine], axis=-1)
    bottom = np.concatenate([-sine, cosine], axis=-1)
    return np.concatenate([top, bottom], axis=-2)


class Plan:
    def __init__(self, strips, epochs, pulses, samples):
        self.strips, self.epochs = strips, epochs
        self.pulses, self.samples = pulses, samples
        self.azimuth = pulses * strips
        self.base = samples // RADIX
        self.owned = samples // (strips * epochs)
        even = all(size & (size - 1) == 0 for size in (strips, epochs))
        self.parts = 2 if even and self.owned in (64, 128) else 1
        self.start, self.rows = 0, self.owned
        self.looks = self.rows // LOOK
        self.all_looks = self.looks
        self.blocks = self.base // self.owned
        self.lanes = self.azimuth // RADIX
        self.azimuth_looks = self.azimuth // LOOK

    def part(self, number):
        if self.parts == 1:
            return self
        own = copy.copy(self)
        size = self.owned // 4
        own.start, own.rows = (0, 3 * size) if number == 0 else (3 * size, size)
        own.looks = own.rows // LOOK
        return own

    def tile_shift(self, block, tile):
        return block * self.owned + self.start + tile * ROWS


def lag_tables(plan):
    base, samples = plan.base, plan.samples
    index = np.arange(base)
    table = host_parts(
        np.concatenate(unit(index[:, None] * index[None, :], samples, -1.0), axis=1) / samples
    )
    block = np.arange(RADIX)[:, None]
    turns = np.stack(
        unit(block * index[None, :], RADIX, -1.0)
        + tuple(np.broadcast_to(part, (RADIX, base)) for part in unit(block, RADIX, 1.0))
    )
    return table + (turns.astype(np.float32),)


def lag_vectors(plan, filter_ref, table_high, table_low, turn_ref):
    base = plan.base
    lane = lax.broadcasted_iota(jnp.int32, (RADIX, base), 1)
    chosen = lane % RADIX == lax.broadcasted_iota(jnp.int32, (RADIX, base), 0)
    rows = []
    for c in range(2):
        for e in range(RADIX):
            block = jnp.broadcast_to(filter_ref[c : c + 1, e * base : (e + 1) * base], (RADIX, base))
            rows.append(jnp.where(chosen, block, 0.0))
    high, low = two_parts(jnp.concatenate(rows, axis=0))
    sums = three_products(high, low, table_high[...], table_low[...], ((1,), (0,)))
    real, imag = 0.0, 0.0
    for e in range(RADIX):
        by_real = sums[e * RADIX : (e + 1) * RADIX]
        by_imag = sums[(RADIX + e) * RADIX : (RADIX + e + 1) * RADIX]
        part_real = by_real[:, :base] - by_imag[:, base:]
        part_imag = by_real[:, base:] + by_imag[:, :base]
        cosine, sine = turn_ref[0, e : e + 1, :], turn_ref[1, e : e + 1, :]
        real = real + part_real * cosine - part_imag * sine
        imag = imag + part_real * sine + part_imag * cosine
    cosine, sine = turn_ref[2], turn_ref[3]
    return (
        jnp.concatenate([real, real * cosine - imag * sine], axis=1),
        jnp.concatenate([imag, real * sine + imag * cosine], axis=1),
    )


def fetch(copies):
    for move in copies:
        move.start()
    return copies


def compress_kernel(
    plan, relative, filter_ref, high_any, low_any, turn_any, raw_ref, *refs
):
    outs = refs[: plan.epochs if relative else 1]
    (
        table_high, table_low, turn_ref, raw, t_high, t_low, y_high, y_low, z_ref, sems, table_sems,
    ) = refs[len(outs) :][:11]
    out_ref = refs[-2] if relative else outs[0]
    base, blocks = plan.base, plan.blocks
    tiles = plan.rows // ROWS
    chunk = blocks * plan.rows
    pieces = sems.shape[0]
    piece = plan.pulses // pieces

    def raw_copy(at):
        rows = pl.ds(at * piece, piece)
        return pltpu.make_async_copy(raw_ref.at[:, rows, :], raw.at[:, rows, :], sems.at[at])

    tables = fetch(
        [
            pltpu.make_async_copy(source, target, table_sems.at[at])
            for at, (source, target) in enumerate(
                ((high_any, table_high), (low_any, table_low), (turn_any, turn_ref))
            )
        ]
    )
    fetch([raw_copy(at) for at in range(pieces)])
    def spread_pulses(at, carry):
        rows = pl.ds(pl.multiple_of(at * 2 * ROWS, 2 * ROWS), 2 * ROWS)
        x = [
            tuple(raw[c, rows, a * base : (a + 1) * base] for c in range(2))
            for a in range(RADIX)
        ]
        for d, value in enumerate(dft8(x, -1.0)):
            for c in range(2):
                high, low = two_parts(value[c])
                y_high[d, rows, c * base : (c + 1) * base] = high
                y_low[d, rows, c * base : (c + 1) * base] = low
        return carry

    steps = piece // (2 * ROWS)
    for at in range(pieces):
        raw_copy(at).wait()
        lax.fori_loop(at * steps, (at + 1) * steps, spread_pulses, 0)

    for move in tables:
        move.wait()
    lags = lag_vectors(plan, filter_ref, table_high, table_low, turn_ref)

    for d in range(RADIX):
        spread = [
            pltpu.roll(
                jnp.broadcast_to(lag[d : d + 1, :], (ROWS, 2 * base)),
                0,
                1,
                stride=1,
                stride_axis=0,
            )
            for lag in lags
        ]
        for pair in range(blocks * tiles // 2):
            real, imag = [], []
            for at in (2 * pair, 2 * pair + 1):
                shift = plan.tile_shift(at // tiles, at % tiles)
                real.append(pltpu.roll(spread[0], shift, 1)[:, :base])
                imag.append(pltpu.roll(spread[1], shift, 1)[:, :base])
            real_high, real_low = two_parts(jnp.concatenate(real, axis=0))
            imag_high, imag_low = two_parts(jnp.concatenate(imag, axis=0))
            top = pl.ds(pair * 2 * ROWS, 2 * ROWS)
            bottom = pl.ds(chunk + pair * 2 * ROWS, 2 * ROWS)
            t_high[d, top, :base] = real_high
            t_high[d, top, base:] = -imag_high
            t_high[d, bottom, :base] = imag_high
            t_high[d, bottom, base:] = real_high
            t_low[d, top, :base] = real_low
            t_low[d, top, base:] = -imag_low
            t_low[d, bottom, :base] = imag_low
            t_low[d, bottom, base:] = real_low
        z_ref[d] = three_products(t_high[d], t_low[d], y_high[d], y_low[d], ((1,), (1,)))

    for block in range(blocks):
        for tile in range(tiles):
            top = (block * tiles + tile) * ROWS
            z = [
                (z_ref[d, top : top + ROWS, :], z_ref[d, chunk + top : chunk + top + ROWS, :])
                for d in range(RADIX)
            ]
            for a, value in enumerate(dft8(z, 1.0)):
                for c in range(2):
                    strip, owner = divmod(a * blocks + block, plan.epochs)
                    rows = slice(tile * ROWS, (tile + 1) * ROWS)
                    if relative:
                        place = owner ^ lax.axis_index("acq"), strip ^ lax.axis_index("strip")
                    else:
                        place = strip, owner
                    out_ref[place[0], place[1], c, rows, :] = value[c]
    if relative:
        copies = fetch(
            [
                pltpu.make_async_copy(out_ref.at[m], out, refs[-1].at[m])
                for m, out in enumerate(outs)
            ]
        )
        for move in copies:
            move.wait()


def compress(plan, relative, range_filter, raw):
    chunk = plan.blocks * plan.rows
    whole = pl.BlockSpec(memory_space=pltpu.VMEM)
    bytes_moved = 8 * raw.size
    tables = lag_tables(plan)
    slab = (2, plan.rows, plan.pulses)
    shape = (plan.strips,) + (slab if relative else (plan.epochs,) + slab)
    scratch, out_specs = [], whole
    if relative:
        out_specs = [pl.BlockSpec(memory_space=pltpu.HBM)] * plan.epochs
        scratch = [
            pltpu.VMEM((plan.epochs,) + shape, jnp.float32),
            pltpu.SemaphoreType.DMA((plan.epochs,)),
        ]
    shape = jax.ShapeDtypeStruct(shape, jnp.float32)
    return pl.pallas_call(
        functools.partial(compress_kernel, plan, relative),
        out_shape=[shape] * plan.epochs if relative else shape,
        in_specs=[whole] + [pl.BlockSpec(memory_space=pltpu.HBM)] * 4,
        out_specs=out_specs,
        scratch_shapes=[
            *[pltpu.VMEM(table.shape, table.dtype) for table in tables],
            pltpu.VMEM(raw.shape, jnp.float32),
            pltpu.VMEM((RADIX, 2 * chunk, 2 * plan.base), jnp.bfloat16),
            pltpu.VMEM((RADIX, 2 * chunk, 2 * plan.base), jnp.bfloat16),
            pltpu.VMEM((RADIX, plan.pulses, 2 * plan.base), jnp.bfloat16),
            pltpu.VMEM((RADIX, plan.pulses, 2 * plan.base), jnp.bfloat16),
            pltpu.VMEM((RADIX, 2 * chunk, plan.pulses), jnp.float32),
            pltpu.SemaphoreType.DMA((4,)),
            pltpu.SemaphoreType.DMA((3,)),
            *scratch,
        ],
        compiler_params=pltpu.CompilerParams(vmem_limit_bytes=RANGE_VMEM),
        cost_estimate=pl.CostEstimate(
            flops=6 * RADIX * 4 * chunk * plan.base * plan.pulses,
            bytes_accessed=bytes_moved,
            transcendentals=0,
        ),
        name="range_compress",
    )(range_filter, *tables, raw)


def focus_kernel(plan, final, field_at, own, *refs):
    filter_any, high_any, low_any, twiddle_any, sum_any = refs[:5]
    if final:
        weight_ref, before_any, halo_any, out_ref = refs[5:9]
    else:
        (out_ref,) = refs[5:6]
    scratch = refs[9 if final else 6 :]
    (
        field_ref, filter_ref, table_high, table_low, twiddle_ref, sum_ref,
        y_high, y_low, z_ref, scene_ref, product_ref, field_sems, table_sems,
    ) = scratch[:13]
    rows, lanes, epochs, looks = plan.rows, plan.lanes, plan.epochs, plan.looks
    step = 2 * ROWS
    group = max(1, step // rows)
    per_block = field_ref.shape[-1] // lanes

    half = epochs // 2
    fields = [
        [
            pltpu.make_async_copy(
                field_at(at).at[pl.ds(side * half, half)],
                field_ref.at[at, pl.ds(side * half, half)],
                field_sems.at[at, side],
            )
            for at in range(field_ref.shape[0])
        ]
        for side in range(2)
    ]
    tables = [
        pltpu.make_async_copy(source, target, table_sems.at[at])
        for at, (source, target) in enumerate(
            (
                (twiddle_any, twiddle_ref),
                (high_any, table_high),
                (low_any, table_low),
                (filter_any, filter_ref),
                (sum_any, sum_ref),
            )
        )
    ]
    fetch(tables[:1])
    for copies in fields:
        fetch(copies)
    fetch(tables[1:])
    if final:
        looked_ref, slope_ref, halo_ref, late_sems = scratch[13:]
        late = fetch(
            [
                pltpu.make_async_copy(before_any, looked_ref, late_sems.at[0]),
                pltpu.make_async_copy(halo_any, halo_ref, late_sems.at[1]),
            ]
        )
    tables[0].wait()

    def rows_of(strip, slot, c, top, start):
        some = [
            field_ref[strip, slot + g, c, top : top + min(rows, step), start : start + lanes]
            for g in range(group)
        ]
        return some[0] if group == 1 else jnp.concatenate(some, axis=0)

    def forward(at, carry):
        slot = at * group
        j = slot ^ own[0]
        for top in range(0, rows, step):
            x = []
            for a in range(RADIX):
                strip, start = a // per_block, a % per_block * lanes
                x.append(tuple(rows_of(strip ^ own[1], slot, c, top, start) for c in range(2)))
            at = pl.ds(pl.multiple_of(j * rows + top, step), step)
            for d, value in enumerate(dft8(x, -1.0)):
                if d > 0:
                    value = times(value, twiddle_ref[0, d : d + 1, :], twiddle_ref[1, d : d + 1, :])
                for c in range(2):
                    high, low = two_parts(value[c])
                    y_high[d, at, c * lanes : (c + 1) * lanes] = high
                    y_low[d, at, c * lanes : (c + 1) * lanes] = low
        return carry

    for side, copies in enumerate(fields):
        for move in copies:
            move.wait()
        lax.fori_loop(side * half // group, (side + 1) * half // group, forward, 0)
    for move in tables[1:]:
        move.wait()

    for d in range(RADIX):
        spectrum = three_products(
            y_high[d], y_low[d], table_high[...], table_low[...], ((1,), (0,))
        )
        spectrum = spectrum.reshape(epochs, rows, 2 * lanes)
        real, imag = spectrum[:, :, :lanes], spectrum[:, :, lanes:]
        by_real, by_imag = filter_ref[0, d][None], filter_ref[1, d][None]
        spectrum = jnp.concatenate(
            [real * by_real - imag * by_imag, real * by_imag + imag * by_real], axis=2
        )
        high, low = two_parts(spectrum.reshape(epochs * rows, 2 * lanes))
        z_ref[d] = three_products(high, low, table_high[...], table_low[...], ((1,), (1,)))

    scene_ref[0] = jnp.zeros_like(scene_ref[0])
    scene_ref[1] = jnp.zeros_like(scene_ref[1])

    def backward(j, carry):
        for top in range(0, rows, ROWS):
            at = pl.ds(pl.multiple_of(j * rows + top, ROWS), ROWS)
            z = [
                times(
                    tuple(z_ref[d, at, c * lanes : (c + 1) * lanes] for c in range(2)),
                    twiddle_ref[2, d : d + 1, :],
                    twiddle_ref[3, d : d + 1, :],
                )
                for d in range(RADIX)
            ]
            for a, value in enumerate(dft8(z, 1.0)):
                for c in range(2):
                    scene_ref[j + 2, c, a, top : top + ROWS, :] = value[c]
        return carry

    lax.fori_loop(0, epochs, backward, 0)

    def interfere(j, carry):
        for a in range(RADIX):
            columns = pl.ds(a * lanes, lanes)
            sums = [0.0] * 4
            for q in range(LOOK):
                rows_at = pl.ds(q, looks, stride=LOOK)
                later, *earlier = [
                    tuple(scene_ref[j + 2 - lag, c, a, rows_at, :] for c in range(2))
                    for lag in range(3)
                ]
                for at, value in enumerate(earlier):
                    sums[2 * at] += value[0] * later[0] + value[1] * later[1]
                    sums[2 * at + 1] += value[1] * later[0] - value[0] * later[1]
            place = pl.ds(pl.multiple_of(j * 4 * looks, ROWS), 4 * looks)
            product_ref[place, columns] = jnp.concatenate(sums, axis=0)
        return carry

    lax.fori_loop(0, epochs, interfere, 0)

    products = product_ref[...]
    high, low = two_parts(products)
    weights = sum_ref[...]
    looked = []
    for start in range(0, plan.azimuth, weights.shape[0]):
        columns = slice(start, start + weights.shape[0])
        looked.append(
            jnp.dot(high[:, columns], weights, preferred_element_type=jnp.float32)
            + jnp.dot(low[:, columns], weights, preferred_element_type=jnp.float32)
        )
    looked = jnp.concatenate(looked, axis=1)
    looked = looked.reshape(epochs, 2, 2, looks, plan.azimuth_looks)
    if final:
        for move in late:
            move.wait()
        looked_ref[:, :, :, plan.all_looks - looks :, :] = looked
        slopes_and_sums(plan, weight_ref, looked_ref, halo_ref, out_ref, slope_ref)
    else:
        out_ref[:, :, :, :looks, :] = looked
        if looks < plan.all_looks:
            rest = (epochs, 2, 2, plan.all_looks - looks, plan.azimuth_looks)
            out_ref[:, :, :, looks:, :] = jnp.zeros(rest, jnp.float32)


def slopes_and_sums(plan, weight_ref, looked_ref, halo_ref, out_ref, slope_ref):
    epochs = plan.epochs
    columns = plan.azimuth_looks
    inner = lax.broadcasted_iota(jnp.int32, (plan.all_looks, columns), 1) < columns - 1

    def slopes(at, carry):
        j, lag = at // 2, at % 2
        real, imag = looked_ref[j, lag, 0], looked_ref[j, lag, 1]
        next_real = pltpu.roll(real, columns - 1, 1)
        next_imag = pltpu.roll(imag, columns - 1, 1)
        slope_ref[at, 0] = jnp.where(inner, next_imag * real - next_real * imag, 0.0)
        next_real = jnp.concatenate([real[1:], halo_ref[j, lag, 0]], axis=0)
        next_imag = jnp.concatenate([imag[1:], halo_ref[j, lag, 1]], axis=0)
        slope_ref[at, 1] = next_imag * real - next_real * imag
        return carry

    lax.fori_loop(0, 2 * epochs, slopes, 0)

    def epoch(e, carry):
        total = weight_ref[e, 0] * slope_ref[0]
        for at in range(1, 2 * epochs):
            total = total + weight_ref[e, at] * slope_ref[at]
        out_ref[e] = total
        return carry

    lax.fori_loop(0, epochs, epoch, 0)


def focus_tables(plan):
    lanes = plan.lanes
    index = np.arange(lanes)
    table = host_parts(real_form(*unit(index[:, None] * index[None, :], lanes, -1.0)))
    cosine, sine = unit(np.arange(RADIX)[:, None] * index[None, :], plan.azimuth, -1.0)
    twiddles = np.stack([cosine, sine, cosine / plan.azimuth, -sine / plan.azimuth])
    sums = np.arange(plan.azimuth // 2)[:, None] // LOOK == np.arange(plan.azimuth_looks // 2)[None, :]
    return table + (twiddles.astype(np.float32), (sums / LOOK).astype(ml_dtypes.bfloat16))


def focus(plan, fields, spectrum, finish=None):
    lanes = plan.lanes
    total = plan.epochs * plan.rows
    tables = focus_tables(plan)
    whole = pl.BlockSpec(memory_space=pltpu.VMEM)
    looked = (plan.epochs, 2, 2, plan.all_looks, plan.azimuth_looks)
    gradients = (plan.epochs, 2, plan.all_looks, plan.azimuth_looks)
    operands = [*fields, spectrum, *tables]
    in_specs = [pl.BlockSpec(memory_space=pltpu.HBM)] * len(operands)
    blocks = plan.azimuth // fields[0].shape[-1]
    scratch = [
        pltpu.VMEM((blocks, plan.epochs) + fields[0].shape[-3:], jnp.float32),
        pltpu.VMEM(spectrum.shape, jnp.float32),
        *[pltpu.VMEM(table.shape, table.dtype) for table in tables],
        pltpu.VMEM((RADIX, total, 2 * lanes), jnp.bfloat16),
        pltpu.VMEM((RADIX, total, 2 * lanes), jnp.bfloat16),
        pltpu.VMEM((RADIX, total, 2 * lanes), jnp.float32),
        pltpu.VMEM((plan.epochs + 2, 2, RADIX, plan.rows, lanes), jnp.float32),
        pltpu.VMEM((plan.epochs * 4 * plan.looks, plan.azimuth), jnp.float32),
        pltpu.SemaphoreType.DMA((blocks, 2)),
        pltpu.SemaphoreType.DMA((5,)),
    ]
    shape = looked
    if finish is not None:
        weights, before, halo = finish
        shape = gradients
        operands += [weights, before, halo]
        in_specs += [pl.BlockSpec(memory_space=pltpu.SMEM)]
        in_specs += [pl.BlockSpec(memory_space=pltpu.HBM)] * 2
        scratch += [
            pltpu.VMEM(looked, jnp.float32),
            pltpu.VMEM((2 * plan.epochs,) + gradients[1:], jnp.float32),
            pltpu.VMEM(halo.shape, jnp.float32),
            pltpu.SemaphoreType.DMA((2,)),
        ]

    def kernel(*refs):
        some, refs = refs[: len(fields)], refs[len(fields) :]

        relative = len(some) > 1
        own = (lax.axis_index("acq"), lax.axis_index("strip")) if relative else (0, 0)

        def field_at(at):
            return some[at] if relative else some[0].at[at]

        focus_kernel(plan, finish is not None, field_at, own, *refs)

    return pl.pallas_call(
        kernel,
        out_shape=jax.ShapeDtypeStruct(shape, jnp.float32),
        in_specs=in_specs,
        out_specs=whole,
        scratch_shapes=scratch,
        compiler_params=pltpu.CompilerParams(vmem_limit_bytes=FOCUS_VMEM),
        cost_estimate=pl.CostEstimate(
            flops=2 * 6 * RADIX * total * 4 * lanes * lanes,
            bytes_accessed=4 * total * 2 * plan.azimuth + 4 * 1024 * 1024,
            transcendentals=0,
        ),
        name="azimuth_focus",
    )(*operands)


def slope_kernel(plan, weight_ref, looked_ref, halo_ref, out_ref, slope_ref):
    slopes_and_sums(plan, weight_ref, looked_ref, halo_ref, out_ref, slope_ref)


def slopes_to_epochs(plan, weights, looked, halo):
    whole = pl.BlockSpec(memory_space=pltpu.VMEM)
    looks = plan.all_looks
    return pl.pallas_call(
        functools.partial(slope_kernel, plan),
        out_shape=jax.ShapeDtypeStruct(
            (plan.epochs, 2, looks, plan.azimuth_looks), jnp.float32
        ),
        in_specs=[pl.BlockSpec(memory_space=pltpu.SMEM), whole, whole],
        out_specs=whole,
        scratch_shapes=[
            pltpu.VMEM((2 * plan.epochs, 2, looks, plan.azimuth_looks), jnp.float32)
        ],
        compiler_params=pltpu.CompilerParams(vmem_limit_bytes=FOCUS_VMEM),
        cost_estimate=pl.CostEstimate(
            flops=8 * looked.size * plan.epochs, bytes_accessed=5 * looked.size, transcendentals=0
        ),
        name="slopes_to_epochs",
    )(weights, looked, halo)


def own_filter(plan, azimuth_filter):
    start = lax.axis_index("acq") * plan.owned
    own = lax.dynamic_slice_in_dim(azimuth_filter, start, plan.owned, axis=2)
    return own.reshape(2, plan.lanes, RADIX, plan.owned).transpose(0, 2, 3, 1)


def own_filter_kernel(plan, filter_any, *refs):
    *outs, block_ref, turned_ref, sem = refs
    width = block_ref.shape[-1]
    acq = lax.axis_index("acq")
    start = acq * plan.owned // width * width
    inside = acq * plan.owned % width
    move = pltpu.make_async_copy(
        filter_any.at[:, :, pl.ds(pl.multiple_of(start, width), width)], block_ref, sem
    )
    move.start()
    move.wait()
    for c in range(2):
        for d in range(RADIX):
            turned_ref[...] = block_ref[c, pl.ds(d, plan.lanes, stride=RADIX), :].T
            for number, out_ref in enumerate(outs):
                part = plan.part(number)
                start = pl.multiple_of(inside + part.start, ROWS)
                out_ref[c, d] = turned_ref[pl.ds(start, part.rows), :]


def own_filter_by_kernel(plan, azimuth_filter):
    width = 128
    return pl.pallas_call(
        functools.partial(own_filter_kernel, plan),
        out_shape=[
            jax.ShapeDtypeStruct((2, RADIX, plan.part(number).rows, plan.lanes), jnp.float32)
            for number in range(plan.parts)
        ],
        in_specs=[pl.BlockSpec(memory_space=pltpu.HBM)],
        out_specs=[pl.BlockSpec(memory_space=pltpu.VMEM)] * plan.parts,
        scratch_shapes=[
            pltpu.VMEM((2, plan.azimuth, width), jnp.float32),
            pltpu.VMEM((width, plan.lanes), jnp.float32),
            pltpu.SemaphoreType.DMA,
        ],
        compiler_params=pltpu.CompilerParams(vmem_limit_bytes=LAYOUT_VMEM),
        cost_estimate=pl.CostEstimate(flops=0, bytes_accessed=1024, transcendentals=0),
        name="own_filter",
    )(azimuth_filter)


def exchange_all(plan, block):
    shape = block.shape
    block = block.reshape((plan.strips * plan.epochs,) + shape[2:])
    received = lax.all_to_all(block, OWNERS, split_axis=0, concat_axis=0, tiled=True)
    join = max(1, plan.lanes // plan.pulses)
    received = received.reshape((plan.strips // join, join) + shape[1:])
    if join > 1:
        received = received.transpose(0, 2, 3, 4, 1, 5)
    return received.reshape(plan.strips // join, plan.epochs, 2, plan.rows, join * plan.pulses)


def partners(slots, axis, first=0):
    size = lax.axis_size(axis)
    moved = []
    for k, slot in enumerate(slots, first):
        moved.append(slot if k == 0 else lax.ppermute(slot, axis, [(i, i ^ k) for i in range(size)]))
    return moved


def regroup(blocks):
    count, inner = len(blocks), blocks[0].shape[0]

    def kernel(*refs):
        ins, outs = refs[:count], refs[count : count + inner]
        stage, in_sems, out_sems = refs[count + inner :]
        inward = [
            fetch(
                [
                    pltpu.make_async_copy(ins[m].at[k], stage.at[k, m], in_sems.at[k, m])
                    for m in range(count)
                ]
            )
            for k in range(inner)
        ]
        outward = []
        for k in range(inner):
            for move in inward[k]:
                move.wait()
            outward += fetch([pltpu.make_async_copy(stage.at[k], outs[k], out_sems.at[k])])
        for move in outward:
            move.wait()

    slab = (count,) + blocks[0].shape[1:]
    place = pl.BlockSpec(memory_space=pltpu.HBM)
    return pl.pallas_call(
        kernel,
        out_shape=[jax.ShapeDtypeStruct(slab, jnp.float32)] * inner,
        in_specs=[place] * count,
        out_specs=[place] * inner,
        scratch_shapes=[
            pltpu.VMEM((inner,) + slab, jnp.float32),
            pltpu.SemaphoreType.DMA((inner, count)),
            pltpu.SemaphoreType.DMA((inner,)),
        ],
        compiler_params=pltpu.CompilerParams(vmem_limit_bytes=LAYOUT_VMEM),
        cost_estimate=pl.CostEstimate(flops=0, bytes_accessed=1024, transcendentals=0),
        name="regroup",
    )(*blocks)


def all_weights(pair_mask, inversion):
    lags = jnp.array([1, 2], dtype=jnp.int32)
    usable = pair_mask[0].astype(jnp.float32) * (lax.axis_index("acq") >= lags).astype(jnp.float32)
    weights = lax.all_gather(inversion[:, 0, :] * usable[None, :], "acq", axis=1, tiled=False)
    return weights.reshape(weights.shape[0], -1)


def per_device(raw_echoes, range_filter, azimuth_filter, pair_mask, inversion):
    strips, epochs = lax.axis_size("strip"), lax.axis_size("acq")
    plan = Plan(strips, epochs, raw_echoes.shape[2], raw_echoes.shape[3])

    raw = raw_echoes[0]
    big, small = plan.part(0), plan.part(1)
    block = compress(big, False, range_filter, raw)
    if plan.parts > 1:
        range_filter, block = lax.optimization_barrier((range_filter, block))
        other = compress(small, True, range_filter, raw)
        *other, azimuth_filter, pair_mask, inversion = lax.optimization_barrier(
            (*other, azimuth_filter, pair_mask, inversion)
        )
        weights = all_weights(pair_mask, inversion)
        spectrum, other_spectrum = own_filter_by_kernel(plan, azimuth_filter)
        field = exchange_all(big, block)
        other = partners(other, "acq")
        *other, spectrum, weights = lax.optimization_barrier((*other, spectrum, weights))
        other = list(regroup(other))
        near = partners(other[:2], "strip")
        near[1], *far = lax.optimization_barrier((near[1], *other[2:]))
        other = near + partners(far, "strip", 2)
    else:
        weights = all_weights(pair_mask, inversion)
        spectrum = own_filter(plan, azimuth_filter)
        field = exchange_all(plan, block)
    before = focus(big, [field], spectrum)

    owners = strips * epochs
    device = [i % epochs * strips + i // epochs for i in range(owners)]
    halo = lax.ppermute(
        before[:, :, :, :1, :],
        ("acq", "strip"),
        [(device[i], device[i - 1]) for i in range(1, owners)],
    )
    if plan.parts > 1:
        gradients = focus(small, other, other_spectrum, (weights, before, halo))
    else:
        gradients = slopes_to_epochs(plan, weights, before, halo)
    gathered = lax.all_to_all(gradients, "acq", split_axis=0, concat_axis=0, tiled=True)
    gathered = gathered.reshape(epochs, 2, plan.all_looks, plan.azimuth_looks)
    return gathered.swapaxes(0, 1).reshape(1, 2, -1, plan.azimuth_looks)


def solution(mesh):
    return jax.shard_map(
        per_device,
        mesh=mesh,
        in_specs=(
            P("acq", None, "strip", None),
            P(),
            P(None, None, "strip"),
            P("acq", None),
            P(None, "acq", None),
        ),
        out_specs=P("acq", None, "strip", None),
        check_vma=False,
    )
```
